128 devices in a mesh: row: 8 (over y, core), col: 16 (over x, z).
Axes of the slice: x: 4, y: 4, z: 4, core: 2. Of those that a mesh axis runs over, the one named last changes fastest.
Arguments:
- fine_input: bfloat16 [4, 128, 128, 512], P(None, 'row', 'col'), may hold values from -6 to 6
- gain_fine: float32 [512], replicated, may hold values from 0.25 to 1.75
- fine_qkv: bfloat16 [512, 1536], replicated, may hold values from -0.25 to 0.25
- fine_out: bfloat16 [512, 512], replicated, may hold values from -0.75 to 0.75
- fine_scale: float32 [8], replicated, may hold values from 4 to 12
- merge_weight: bfloat16 [2048, 1024], replicated, may hold values from -0.125 to 0.125
- gain_coarse: float32 [1024], replicated, may hold values from 0.25 to 1.75
- coarse_qkv: bfloat16 [3, 1024, 1024], P(None, None, 'col'), may hold values from -0.1875 to 0.1875
- coarse_out: bfloat16 [1024, 1024], P('col'), may hold values from -0.75 to 0.75
- coarse_scale: float32 [16], P('col'), may hold values from 4 to 12
- cotangent: bfloat16 [4, 64, 64, 1024], P(None, 'row', 'col'), may hold values from -6 to 6
Outputs:
- coarse_output: bfloat16 [4, 64, 64, 1024], P(None, 'row', 'col')
- input_grad: float32 [4, 64, 64, 1024], P(None, 'row', 'col')
- qkv_grad: float32 [3, 1024, 1024], P(None, 'row', 'col')
- out_grad: float32 [1024, 1024], P('col', 'row')
The draws below stay inside these ranges and needn't reach their ends.
All inputs are finite; a program needn't handle non-finite values.
Results may differ from the reference program's by a relative error of at most 0.034.
Values may be sent and summed in bfloat16 or wider, within the bound.
A program may use at most 128 MiB of HBM per device.

```python
import math
import jax
import jax.numpy as jnp
from jax import lax

C1 = 512
C2 = 1024
DH = 64
G1 = 128
IMAGES = 4
HEADS1 = 8
HEADS2 = 16
G2 = 64


def shard_levels(stream_key, dims, pieces, smallest, high):
    gain, own = 1.0, jax.random.fold_in(stream_key, 6)
    for position, shards_of in pieces:
        steps = jnp.exp(jax.random.uniform(jax.random.fold_in(own, position), (shards_of,), jnp.float32, smallest / len(pieces), high / len(pieces)))
        gain = gain * jnp.repeat(steps, dims[position] // shards_of).reshape([-1 if axis == position else 1 for axis in range(len(dims))])
    return gain


def scatter_about(rng, dims, width, reach, split=(), kind=jnp.bfloat16):
    drawn = jax.random.normal(rng, dims, jnp.float32) * width
    if len(split) > 0:
        drawn = shard_levels(rng, dims, split, -0.22, 0.18) * drawn
    return jnp.clip(drawn, min=-reach, max=reach).astype(kind)


def setup_inputs(seed: int = 0) -> dict:
    seeds = jax.random.split(jax.random.key(seed), 12)
    return {
        "fine_input": scatter_about(seeds[0], (IMAGES, G1, G1, C1), 1.0, 6.0, ((1, 8), (2, 16))),
        "gain_fine": jnp.clip(1.0 + 0.15 * jax.random.normal(seeds[1], (C1,), jnp.float32), 0.25, 1.75),
        "fine_qkv": scatter_about(seeds[2], (C1, 3 * C1), C1 ** -0.5, 0.25),
        "fine_out": scatter_about(seeds[3], (C1, C1), DH ** -0.5, 0.75),
        "fine_scale": jnp.clip(jnp.exp(jax.random.uniform(seeds[4], (HEADS1,), jnp.float32, math.log(4.0), math.log(12.0))), 4.0, 12.0),
        "merge_weight": scatter_about(seeds[5], (4 * C1, C2), (4 * C1) ** -0.5, 0.125),
        "gain_coarse": jnp.clip(1.0 + 0.15 * jax.random.normal(seeds[6], (C2,), jnp.float32), 0.25, 1.75),
        "coarse_qkv": scatter_about(seeds[7], (3, C2, C2), C2 ** -0.5, 0.1875, ((2, 16),)),
        "coarse_out": scatter_about(seeds[8], (C2, C2), DH ** -0.5, 0.75, ((0, 16),)),
        "coarse_scale": jnp.clip(jnp.exp(math.log(12.0) - 1.0986123 * jax.random.uniform(seeds[9], (HEADS2,), jnp.float32) ** shard_levels(seeds[9], (HEADS2,), ((0, 16),), -0.2, 0.2)), 4.0, 12.0),
        "cotangent": scatter_about(seeds[10], (IMAGES, G2, G2, C2), 1.0, 6.0, ((1, 8), (2, 16))),
    }


def normalize(values):
    return values * lax.rsqrt(lax.optimization_barrier(jnp.mean(values * values, axis=-1, keepdims=True)) + 1e-06)

def norm_back(values, upstream):
    factor = lax.rsqrt(lax.optimization_barrier(jnp.mean(values * values, axis=-1, keepdims=True)) + 1e-06)
    unit = values * factor
    return factor * (upstream - unit * lax.optimization_barrier(jnp.mean(upstream * unit, axis=-1, keepdims=True)))

def neighbour_attention(queries, keys_wide, values_wide, row_inside, col_inside, scales):
    rows = queries.shape[1]
    cols = queries.shape[2]
    head_scale = scales / queries.shape[-1]
    totals = jnp.zeros(queries.shape[:4], jnp.float32)
    weighted = jnp.zeros(queries.shape, jnp.float32)
    for row_off in range(7):
        for col_off in range(7):
            keys_here = keys_wide[:, row_off:row_off + rows, col_off:col_off + cols]
            values_here = values_wide[:, row_off:row_off + rows, col_off:col_off + cols].astype(jnp.float32)
            scores = lax.optimization_barrier(jnp.sum(queries * keys_here, axis=-1)) * head_scale
            inside = row_inside[row_off:row_off + rows][:, None] * col_inside[col_off:col_off + cols][None, :]
            powered = jnp.exp(scores) * inside[None, :, :, None]
            totals = totals + powered
            weighted = weighted + powered[..., None] * values_here
    return weighted / totals[..., None]

def attend(queries, keys, values, grads, scales):
    head_size = queries.shape[-1]
    factor = (scales / head_size)[:, None, None]
    head_factor = (scales / head_size)[None, :, None]
    query_f = queries.astype(jnp.float32)
    key_f = keys.astype(jnp.float32)
    value_f = values.astype(jnp.float32)
    grad_f = grads.astype(jnp.float32)
    scores = jnp.einsum('qhd,khd->hqk', query_f, key_f) * factor
    powered = jnp.exp(scores)
    denoms = lax.optimization_barrier(jnp.sum(powered, axis=-1))
    rounded = lax.optimization_barrier(powered.astype(jnp.bfloat16)).astype(jnp.float32)
    numerator = jnp.einsum('hqk,khd->qhd', rounded, value_f)
    outputs = numerator / denoms.T[:, :, None]
    chance = powered / denoms[:, :, None]
    deltas = lax.optimization_barrier(jnp.sum(grad_f * outputs, axis=-1))
    grad_prob = jnp.einsum('qhd,khd->hqk', grad_f, value_f)
    grad_score = chance * (grad_prob - deltas.T[:, :, None])
    chance_b = lax.optimization_barrier(chance.astype(jnp.bfloat16)).astype(jnp.float32)
    grad_value = jnp.einsum('hqk,qhd->khd', chance_b, grad_f)
    score_b = lax.optimization_barrier(grad_score.astype(jnp.bfloat16)).astype(jnp.float32)
    grad_query = jnp.einsum('hqk,khd->qhd', score_b, key_f) * head_factor
    grad_key = jnp.einsum('hqk,qhd->khd', score_b, query_f) * head_factor
    return (outputs, grad_query, grad_key, grad_value)

def reference(fine_input, gain_fine, fine_qkv, fine_out, fine_scale, merge_weight, gain_coarse, coarse_qkv, coarse_out, coarse_scale, cotangent):
    inputs = fine_input.astype(jnp.float32)
    normed = (normalize(inputs) * gain_fine).astype(jnp.bfloat16)
    projected = jnp.dot(normed.reshape(-1, C1), fine_qkv, preferred_element_type=jnp.float32).astype(jnp.bfloat16)
    projected = projected.reshape(IMAGES, G1, G1, 3, HEADS1, DH)
    queries = normalize(projected[:, :, :, 0].astype(jnp.float32))
    keys = normalize(projected[:, :, :, 1].astype(jnp.float32))
    padding = ((0, 0), (3, 3), (3, 3), (0, 0), (0, 0))
    keys_wide = jnp.pad(keys, padding)
    values_wide = jnp.pad(projected[:, :, :, 2], padding)
    places = jnp.arange(G1 + 6, dtype=jnp.int32) - 3
    inside = ((places >= 0) & (places < G1)).astype(jnp.float32)
    mixed = neighbour_attention(queries, keys_wide, values_wide, inside, inside, fine_scale).astype(jnp.bfloat16)
    fine_result = (inputs + jnp.dot(mixed.reshape(-1, C1), fine_out, preferred_element_type=jnp.float32).reshape(inputs.shape)).astype(jnp.bfloat16)
    merged = fine_result.reshape(IMAGES, G2, 2, G2, 2, C1).transpose(0, 1, 3, 2, 4, 5).reshape(-1, 4 * C1)
    coarse_in = jnp.dot(merged, merge_weight, preferred_element_type=jnp.float32).astype(jnp.bfloat16)
    coarse_float = coarse_in.astype(jnp.float32).reshape(IMAGES, G2 * G2, C2)
    coarse_normed = (normalize(coarse_float) * gain_coarse).astype(jnp.bfloat16)
    flat_normed = coarse_normed.reshape(-1, C2)
    raw = [jnp.dot(flat_normed, coarse_qkv[index], preferred_element_type=jnp.float32).astype(jnp.bfloat16).reshape(IMAGES, G2 * G2, HEADS2, DH) for index in range(3)]
    query_n = normalize(raw[0].astype(jnp.float32))
    key_n = normalize(raw[1].astype(jnp.float32))
    grad_flat = cotangent.reshape(-1, C2)
    grad_attn = jnp.dot(grad_flat, coarse_out.T, preferred_element_type=jnp.float32).astype(jnp.bfloat16).reshape(IMAGES, G2 * G2, HEADS2, DH)

    def split_heads(array):
        return array.transpose(0, 2, 1, 3).reshape(IMAGES * HEADS2, G2 * G2, 1, DH)

    def join_heads(array):
        return array.reshape(IMAGES, HEADS2, G2 * G2, DH).transpose(0, 2, 1, 3)
    scale_rep = jnp.tile(coarse_scale, IMAGES).reshape(IMAGES * HEADS2, 1)
    results = lax.map(lambda member: attend(*member), (split_heads(query_n.astype(jnp.bfloat16)), split_heads(key_n.astype(jnp.bfloat16)), split_heads(raw[2]), split_heads(grad_attn), scale_rep))
    attn_f, grad_qn, grad_kn, grad_v = [join_heads(part) for part in results]
    attn = attn_f.astype(jnp.bfloat16).reshape(-1, C2)
    coarse_output = (coarse_float.reshape(-1, C2) + jnp.dot(attn, coarse_out, preferred_element_type=jnp.float32)).astype(jnp.bfloat16)
    out_grad = jnp.dot(attn.T, grad_flat, preferred_element_type=jnp.float32)
    grad_q2 = norm_back(raw[0].astype(jnp.float32), grad_qn).astype(jnp.bfloat16).reshape(-1, C2)
    grad_k2 = norm_back(raw[1].astype(jnp.float32), grad_kn).astype(jnp.bfloat16).reshape(-1, C2)
    grad_v2 = grad_v.astype(jnp.bfloat16).reshape(-1, C2)
    grads = [grad_q2, grad_k2, grad_v2]
    qkv_grad = jnp.stack([jnp.dot(flat_normed.T, grads[index], preferred_element_type=jnp.float32) for index in range(3)])
    grad_normed = jnp.dot(grad_q2, coarse_qkv[0].T, preferred_element_type=jnp.float32)
    grad_normed = grad_normed + jnp.dot(grad_k2, coarse_qkv[1].T, preferred_element_type=jnp.float32)
    grad_normed = grad_normed + jnp.dot(grad_v2, coarse_qkv[2].T, preferred_element_type=jnp.float32)
    input_grad = grad_flat.astype(jnp.float32) + norm_back(coarse_float.reshape(-1, C2), grad_normed * gain_coarse)
    shape = (IMAGES, G2, G2, C2)
    return (coarse_output.reshape(shape), input_grad.reshape(shape), qkv_grad, out_grad)
```

```python
import functools

import jax
import jax.numpy as jnp
import numpy as np
from jax import lax
from jax.experimental import pallas as pl
from jax.experimental.pallas import tpu as pltpu
from jax.sharding import PartitionSpec as P

MESH = pl.DeviceIdType.MESH
F32 = jnp.float32
BF16 = jnp.bfloat16
SEG = ((128, 48), (176, 48), (224, 32), (256, 32), (288, 16), (304, 16), (320, 16), (336, 16))
WAY = ((0, 1), (0, -1), (1, 0), (-1, 0), (1, 1), (1, -1), (-1, 1), (-1, -1))
KEYS = 384


def dot(a, b):
    return jnp.dot(a, b, preferred_element_type=F32)


def dot_nt(a, b):
    return lax.dot_general(a, b, (((1,), (1,)), ((), ())), preferred_element_type=F32)


def fine_tables():
    sel = np.zeros((KEYS, 128), np.float32)
    place = np.full((8, KEYS), 10000, np.int32)
    query = np.zeros((256, 128), np.int32)
    for p in range(4):
        for u in range(8):
            for w in range(4):
                n = p * 32 + u * 4 + w
                i, j = 2 * u + p // 2, 2 * w + p % 2
                sel[n, i * 8 + j] = 1
                place[0, n], place[1, n] = i, j
                query[n, 0] = query[n + 128, 0] = i
                query[n, 1] = query[n + 128, 1] = j
    for (start, _), (down, right) in zip(SEG, WAY):
        rows = {0: range(16), 1: range(13, 16), -1: range(3)}[down]
        cols = {0: range(8), 1: range(5, 8), -1: range(3)}[right]
        n = start
        for i in rows:
            for j in cols:
                sel[n, i * 8 + j] = 1
                place[0, n], place[1, n] = i - 16 * down, j - 8 * right
                n += 1
    return sel, place, query


def fine_kernel(
    x_ref, sel_ref, place_ref, query_ref, gain_ref, wqkv_ref, wout_ref, scale_ref, wmerge_ref, gain2_ref,
    in_ref, normed_ref,
    keys_in, send, kn, vv, qn, fr, bias, send_sem, recv_sem,
):
    row, col = lax.axis_index("row"), lax.axis_index("col")
    barrier = pltpu.get_barrier_semaphore()
    peers = [(lax.rem(row + a + 8, 8), lax.rem(col + b + 16, 16)) for a, b in WAY]
    for peer in peers:
        pl.semaphore_signal(barrier, inc=1, device_id=peer, device_id_type=MESH)

    @pl.loop(0, 4)
    def _(img):
        packed = dot(sel_ref[...], x_ref[img]).astype(BF16)
        keys_in[img, 0:128, :] = packed[0:128]
        send[img] = packed[128:352]
        keys_in[img, 352:384, :] = packed[352:384]

    pl.semaphore_wait(barrier, 8)
    copies = []
    for k, ((start, size), peer) in enumerate(zip(SEG, peers)):
        copy = pltpu.make_async_remote_copy(
            src_ref=send.at[:, start - 128 : start - 128 + size, :],
            dst_ref=keys_in.at[:, start : start + size, :],
            send_sem=send_sem.at[k],
            recv_sem=recv_sem.at[k],
            device_id=peer,
            device_id_type=MESH,
        )
        copy.start()
        copies.append(copy)

    seen = (
        (jnp.abs(place_ref[0:1, :] - query_ref[:, 0:1]) <= 3)
        & (jnp.abs(place_ref[1:2, :] - query_ref[:, 1:2]) <= 3)
    )
    gi = place_ref[0:1, :] + row * 16
    gj = place_ref[1:2, :] + col * 8
    inside = (gi >= 0) & (gi < 128) & (gj >= 0) & (gj < 128)
    bias[...] = jnp.where(seen & inside, 0.0, -1e30).astype(F32)

    lane = lax.broadcasted_iota(jnp.int32, (128, 128), 1)
    sub = lax.broadcasted_iota(jnp.int32, (128, 128), 0)
    same = jnp.where((lane < 64) == (sub < 64), 1.0 / 64, 0.0).astype(BF16)

    def token_norm(tokens):
        xf = tokens.astype(F32)
        factor = lax.rsqrt(jnp.mean(xf * xf, axis=-1, keepdims=True) + 1e-06)
        return (xf * factor * gain_ref[...]).astype(BF16)

    def head_norm(values):
        vf = values.astype(BF16).astype(F32)
        sq = (vf * vf).astype(BF16)
        parts = [dot(sq[:, k * 128 : k * 128 + 128], same) for k in range(4)]
        return vf * lax.rsqrt(jnp.concatenate(parts, axis=1) + 1e-06)

    @pl.loop(0, 4)
    def _(img):
        nx = token_norm(keys_in[img, 0:128, :])
        qn[img] = (head_norm(dot(nx, wqkv_ref[:, 0:512])) * scale_ref[...]).astype(BF16)
        kn[img, 0:128, :] = head_norm(dot(nx, wqkv_ref[:, 512:1024])).astype(BF16)
        vv[img, 0:128, :] = dot(nx, wqkv_ref[:, 1024:1536]).astype(BF16)

    for copy in copies:
        copy.wait()

    @pl.loop(0, 4)
    def _(img):
        nx = token_norm(keys_in[img, 128:384, :])
        kn[img, 128:384, :] = head_norm(dot(nx, wqkv_ref[:, 512:1024])).astype(BF16)
        vv[img, 128:384, :] = dot(nx, wqkv_ref[:, 1024:1536]).astype(BF16)

    ones = jnp.ones((KEYS, 128), BF16)

    @pl.loop(0, 4)
    def _(img):
        mixed = []
        for pair in range(4):
            at = slice(pair * 128, pair * 128 + 128)
            q = qn[img, :, at]
            zero = jnp.zeros_like(q)
            both = jnp.concatenate([jnp.where(lane < 64, q, zero), jnp.where(lane < 64, zero, q)], axis=0)
            powered = jnp.exp(dot_nt(both, kn[img, :, at]) + bias[...]).astype(BF16)
            sums = dot(powered, jnp.concatenate([vv[img, :, at], ones], axis=1))
            ratio = sums[:, 0:128] / sums[:, 128:256]
            mixed.append(jnp.where(lane < 64, ratio[0:128], ratio[128:256]).astype(BF16))
        mix = jnp.concatenate(mixed, axis=1)
        fr[img] = (keys_in[img, 0:128, :].astype(F32) + dot(mix, wout_ref[...])).astype(BF16)

    merged = jnp.zeros((128, 1024), F32)
    for p in range(4):
        part = jnp.concatenate([fr[img, p * 32 : p * 32 + 32, :] for img in range(4)], axis=0)
        merged = merged + dot(part, wmerge_ref[p * 512 : p * 512 + 512, :])
    inner = merged.astype(BF16)
    in_ref[...] = inner
    xf = inner.astype(F32)
    factor = lax.rsqrt(jnp.mean(xf * xf, axis=-1, keepdims=True) + 1e-06)
    normed_ref[...] = (xf * factor * gain2_ref[...]).astype(BF16)


def fine_level(x, gain, wqkv, wout, scale, wmerge, gain2):
    sel, place, query = fine_tables()
    vmem = pl.BlockSpec(memory_space=pltpu.VMEM)
    return pl.pallas_call(
        fine_kernel,
        out_shape=(jax.ShapeDtypeStruct((128, 1024), BF16),) * 2,
        in_specs=[vmem] * 10,
        out_specs=(vmem,) * 2,
        scratch_shapes=[
            pltpu.VMEM((4, KEYS, 512), BF16),
            pltpu.VMEM((4, 224, 512), BF16),
            pltpu.VMEM((4, KEYS, 512), BF16),
            pltpu.VMEM((4, KEYS, 512), BF16),
            pltpu.VMEM((4, 128, 512), BF16),
            pltpu.VMEM((4, 128, 512), BF16),
            pltpu.VMEM((256, KEYS), F32),
            pltpu.SemaphoreType.DMA((8,)),
            pltpu.SemaphoreType.DMA((8,)),
        ],
        compiler_params=pltpu.CompilerParams(
            collective_id=0, has_side_effects=True, vmem_limit_bytes=48 * 1024 * 1024
        ),
        cost_estimate=pl.CostEstimate(flops=6_000_000_000, bytes_accessed=8_000_000, transcendentals=2_000_000),
        name="fine_level",
    )(
        x.reshape(4, 128, 512),
        jnp.asarray(sel, BF16),
        jnp.asarray(place),
        jnp.asarray(query),
        gain.reshape(1, 512),
        wqkv,
        wout,
        jnp.repeat(scale / 64, 64).reshape(1, 512),
        wmerge,
        gain2.reshape(1, 1024),
    )


def normalize(values):
    return values * lax.rsqrt(jnp.mean(values * values, axis=-1, keepdims=True) + 1e-06)


def norm_back(values, upstream):
    factor = lax.rsqrt(jnp.mean(values * values, axis=-1, keepdims=True) + 1e-06)
    unit = values * factor
    return factor * (upstream - unit * jnp.mean(upstream * unit, axis=-1, keepdims=True))


def attend(queries, keys, values, grads, scales):
    head_size = queries.shape[-1]
    factor = (scales / head_size)[:, None, None]
    head_factor = (scales / head_size)[None, :, None]
    scores = jnp.einsum("qhd,khd->hqk", queries, keys, preferred_element_type=jnp.float32) * factor
    powered = jnp.exp(scores)
    denoms = jnp.sum(powered, axis=-1)
    numerator = jnp.einsum(
        "hqk,khd->qhd", powered.astype(jnp.bfloat16), values, preferred_element_type=jnp.float32
    )
    outputs = numerator / denoms.T[:, :, None]
    chance = powered / denoms[:, :, None]
    deltas = jnp.sum(grads.astype(jnp.float32) * outputs, axis=-1)
    grad_prob = jnp.einsum("qhd,khd->hqk", grads, values, preferred_element_type=jnp.float32)
    grad_score = (chance * (grad_prob - deltas.T[:, :, None])).astype(jnp.bfloat16)
    grad_value = jnp.einsum(
        "hqk,qhd->khd", chance.astype(jnp.bfloat16), grads, preferred_element_type=jnp.float32
    )
    grad_query = (
        jnp.einsum("hqk,khd->qhd", grad_score, keys, preferred_element_type=jnp.float32)
        * head_factor
    )
    grad_key = (
        jnp.einsum("hqk,qhd->khd", grad_score, queries, preferred_element_type=jnp.float32)
        * head_factor
    )
    return (outputs, grad_query, grad_key, grad_value)


def per_device(
    fine_input,
    gain_fine,
    fine_qkv,
    fine_out,
    fine_scale,
    merge_weight,
    gain_coarse,
    coarse_qkv,
    coarse_out,
    coarse_scale,
    cotangent,
):
    images, tile_rows, tile_cols, width_fine = fine_input.shape
    head_size = 64
    half_rows, half_cols = tile_rows // 2, tile_cols // 2
    width_coarse = merge_weight.shape[1]
    coarse_in, coarse_normed = fine_level(
        fine_input, gain_fine, fine_qkv, fine_out, fine_scale, merge_weight, gain_coarse
    )
    coarse_float = coarse_in.astype(jnp.float32).reshape(images, half_rows, half_cols, width_coarse)
    coarse_normed = coarse_normed.reshape(images, half_rows, half_cols, width_coarse)
    band = lax.all_gather(coarse_normed, "col", axis=2, tiled=True)
    band_cols = band.shape[2]
    band_tokens = half_rows * band_cols
    band_flat = band.reshape(-1, width_coarse)
    heads_local = coarse_scale.shape[0]
    group_width = coarse_qkv.shape[2]
    raw = [
        jnp.dot(band_flat, coarse_qkv[index], preferred_element_type=jnp.float32).astype(
            jnp.bfloat16
        )
        for index in range(3)
    ]
    query_f = raw[0].astype(jnp.float32).reshape(images, band_tokens, heads_local, head_size)
    key_f = raw[1].astype(jnp.float32).reshape(images, band_tokens, heads_local, head_size)
    query_n = normalize(query_f).astype(jnp.bfloat16)
    key_n = normalize(key_f).astype(jnp.bfloat16)
    key_value_band = jnp.concatenate(
        [
            key_n.reshape(images, band_tokens, group_width),
            raw[2].reshape(images, band_tokens, group_width),
        ],
        axis=-1,
    )
    key_value_all = lax.all_gather(key_value_band, "row", axis=1, tiled=True)
    all_tokens = key_value_all.shape[1]
    keys_all = key_value_all[:, :, :group_width].reshape(images, all_tokens, heads_local, head_size)
    values_all = key_value_all[:, :, group_width:].reshape(
        images, all_tokens, heads_local, head_size
    )
    grad_band = lax.all_gather(cotangent, "col", axis=2, tiled=True).reshape(-1, width_coarse)
    grad_attn = jnp.dot(grad_band, coarse_out.T, preferred_element_type=jnp.float32).astype(
        jnp.bfloat16
    )
    grad_attn = grad_attn.reshape(images, band_tokens, heads_local, head_size)
    results = lax.map(
        lambda member: attend(member[0], member[1], member[2], member[3], coarse_scale),
        (query_n, keys_all, values_all, grad_attn),
    )
    attn_f, grad_qn, grad_kn, grad_v = results
    attn = attn_f.astype(jnp.bfloat16)
    attn_band = attn.reshape(-1, group_width)
    partial_out = jnp.dot(attn_band, coarse_out, preferred_element_type=jnp.float32).reshape(
        images, half_rows, band_cols, width_coarse
    )
    projected = lax.psum_scatter(
        partial_out.astype(jnp.bfloat16), "col", scatter_dimension=2, tiled=True
    ).astype(jnp.float32)
    coarse_output = (coarse_float + projected).astype(jnp.bfloat16)
    weight_term = jnp.dot(attn_band.T, grad_band, preferred_element_type=jnp.float32)
    out_grad = lax.psum_scatter(
        weight_term.astype(jnp.bfloat16), "row", scatter_dimension=1, tiled=True
    ).astype(jnp.float32)
    key_grads = jnp.concatenate(
        [
            grad_kn.reshape(images, all_tokens, group_width),
            grad_v.reshape(images, all_tokens, group_width),
        ],
        axis=-1,
    )
    key_grads = lax.psum_scatter(
        key_grads.astype(jnp.bfloat16), "row", scatter_dimension=1, tiled=True
    ).astype(jnp.float32)
    grad_kn_band = key_grads[:, :, :group_width].reshape(
        images, band_tokens, heads_local, head_size
    )
    grad_v2 = key_grads[:, :, group_width:].astype(jnp.bfloat16).reshape(-1, group_width)
    grad_q2 = norm_back(query_f, grad_qn).astype(jnp.bfloat16).reshape(-1, group_width)
    grad_k2 = norm_back(key_f, grad_kn_band).astype(jnp.bfloat16).reshape(-1, group_width)
    grads = [grad_q2, grad_k2, grad_v2]
    weight_grads = jnp.stack(
        [
            jnp.dot(band_flat.T, grads[index], preferred_element_type=jnp.float32)
            for index in range(3)
        ]
    )
    qkv_grad = lax.psum_scatter(
        weight_grads.astype(jnp.bfloat16), "row", scatter_dimension=1, tiled=True
    ).astype(jnp.float32)
    grad_normed = jnp.dot(grad_q2, coarse_qkv[0].T, preferred_element_type=jnp.float32)
    grad_normed = grad_normed + jnp.dot(
        grad_k2, coarse_qkv[1].T, preferred_element_type=jnp.float32
    )
    grad_normed = grad_normed + jnp.dot(
        grad_v2, coarse_qkv[2].T, preferred_element_type=jnp.float32
    )
    grad_normed = lax.psum_scatter(
        grad_normed.reshape(images, half_rows, band_cols, width_coarse).astype(jnp.bfloat16),
        "col",
        scatter_dimension=2,
        tiled=True,
    ).astype(jnp.float32)
    input_grad = cotangent.astype(jnp.float32) + norm_back(coarse_float, grad_normed * gain_coarse)
    return (coarse_output, input_grad, qkv_grad, out_grad)


def solution(mesh):
    return jax.shard_map(
        per_device,
        mesh=mesh,
        in_specs=(
            P(None, "row", "col", None),
            P(),
            P(),
            P(),
            P(),
            P(),
            P(),
            P(None, None, "col"),
            P("col", None),
            P("col"),
            P(None, "row", "col", None),
        ),
        out_specs=(
            P(None, "row", "col", None),
            P(None, "row", "col", None),
            P(None, "row", "col"),
            P("col", "row"),
        ),
        check_vma=False,
    )
```

```python
import jax
import jax.numpy as jnp
import numpy as np
from jax import lax
from jax.experimental import pallas as pl
from jax.experimental.pallas import tpu as pltpu
from jax.sharding import PartitionSpec as P

MESH = pl.DeviceIdType.MESH
F32 = jnp.float32
BF16 = jnp.bfloat16
SEG = ((128, 48), (176, 48), (224, 32), (256, 32), (288, 16), (304, 16), (320, 16), (336, 16))
WAY = ((0, 1), (0, -1), (1, 0), (-1, 0), (1, 1), (1, -1), (-1, 1), (-1, -1))
KEYS = 384
RING = (1, 3, 2)
BLOCK = 512
CHUNK = 1024
LOG2E = 1.4426950408889634
LN2 = 0.6931471805599453


def dot(a, b):
    return jnp.dot(a, b, preferred_element_type=F32)


def dot_nt(a, b):
    return lax.dot_general(a, b, (((1,), (1,)), ((), ())), preferred_element_type=F32)


def start_copy(source, target, send_sem, recv_sem, device):
    copy = pltpu.make_async_remote_copy(
        src_ref=source, dst_ref=target, send_sem=send_sem, recv_sem=recv_sem, device_id=device, device_id_type=MESH
    )
    copy.start()
    return copy


def swap_peers(x, y, z, core):
    peers = []
    for d in range(1, 16):
        px, py = lax.rem(x + d // 4, 4), lax.rem(y + d % 4, 4)
        peers.append((px, py, (py * 2 + core, px * 4 + z)))
    return peers


def fine_tables():
    sel = np.zeros((KEYS, 128), np.float32)
    place = np.full((8, KEYS), 10000, np.int32)
    query = np.zeros((256, 128), np.int32)
    for p in range(4):
        for u in range(8):
            for w in range(4):
                n = p * 32 + u * 4 + w
                i, j = 2 * u + p // 2, 2 * w + p % 2
                sel[n, i * 8 + j] = 1
                place[0, n], place[1, n] = i, j
                query[n, 0] = query[n + 128, 0] = i
                query[n, 1] = query[n + 128, 1] = j
    for (start, _), (down, right) in zip(SEG, WAY):
        rows = {0: range(16), 1: range(13, 16), -1: range(3)}[down]
        cols = {0: range(8), 1: range(5, 8), -1: range(3)}[right]
        n = start
        for i in rows:
            for j in cols:
                sel[n, i * 8 + j] = 1
                place[0, n], place[1, n] = i - 16 * down, j - 8 * right
                n += 1
    return sel, place, query


def fine_kernel(
    x_ref, sel_ref, place_ref, query_ref, gain_ref, wqkv_ref, wout_ref, scale_ref, wmerge_ref, gain2_ref,
    cot_ref, wpack_ref, scale2_ref,
    in_ref, ng, cg, wg, tr, qg, kv,
    keys_in, send, kn, vv, qn, fr, bias, ts,
    send_sem, recv_sem, w_s, w_r, f_s, f_r, c_s, c_r, n_s, n_r, a_s, a_r, k_s, k_r,
):
    row, col = lax.axis_index("row"), lax.axis_index("col")
    y, core, x, z = lax.div(row, 2), lax.rem(row, 2), lax.div(col, 4), lax.rem(col, 4)
    barrier = pltpu.get_barrier_semaphore()
    peers = [(lax.rem(row + a + 8, 8), lax.rem(col + b + 16, 16)) for a, b in WAY]
    z_peers = [(row, x * 4 + lax.rem(z + off, 4)) for off in RING]
    x_peers = [(row, lax.rem(x + off, 4) * 4 + z) for off in RING]
    twin = (y * 2 + 1 - core, col)
    swap = swap_peers(x, y, z, core)
    for peer in peers + z_peers + x_peers + [twin] + [p for _, _, p in swap]:
        pl.semaphore_signal(barrier, inc=1, device_id=peer, device_id_type=MESH)

    wg[x] = wpack_ref[...]
    cg[z] = cot_ref[...]

    @pl.loop(0, 4)
    def _(img):
        packed = dot(sel_ref[...], x_ref[img]).astype(BF16)
        keys_in[img, 0:128, :] = packed[0:128]
        send[img] = packed[128:352]
        keys_in[img, 352:384, :] = packed[352:384]

    pl.semaphore_wait(barrier, 30)
    copies = []
    for k, ((start, size), peer) in enumerate(zip(SEG, peers)):
        copy = pltpu.make_async_remote_copy(
            src_ref=send.at[:, start - 128 : start - 128 + size, :],
            dst_ref=keys_in.at[:, start : start + size, :],
            send_sem=send_sem.at[k],
            recv_sem=recv_sem.at[k],
            device_id=peer,
            device_id_type=MESH,
        )
        copy.start()
        copies.append(copy)

    half = pl.ds(pl.multiple_of(core * 512, 512), 512)
    w_copies = [
        start_copy(wpack_ref.at[half, :], wg.at[x, half, :], w_s.at[k], w_r.at[k], x_peers[k]) for k in range(3)
    ]

    seen = (
        (jnp.abs(place_ref[0:1, :] - query_ref[:, 0:1]) <= 3)
        & (jnp.abs(place_ref[1:2, :] - query_ref[:, 1:2]) <= 3)
    )
    gi = place_ref[0:1, :] + row * 16
    gj = place_ref[1:2, :] + col * 8
    inside = (gi >= 0) & (gi < 128) & (gj >= 0) & (gj < 128)
    bias[...] = jnp.where(seen & inside, 0.0, -1e30).astype(F32)

    lane = lax.broadcasted_iota(jnp.int32, (128, 128), 1)
    sub = lax.broadcasted_iota(jnp.int32, (128, 128), 0)
    same = jnp.where((lane < 64) == (sub < 64), 1.0 / 64, 0.0).astype(BF16)

    def token_norm(tokens):
        xf = tokens.astype(F32)
        factor = lax.rsqrt(jnp.mean(xf * xf, axis=-1, keepdims=True) + 1e-06)
        return (xf * factor * gain_ref[...]).astype(BF16)

    def head_norm(values):
        vf = values.astype(BF16).astype(F32)
        sq = (vf * vf).astype(BF16)
        parts = [dot(sq[:, k * 128 : k * 128 + 128], same) for k in range(4)]
        return vf * lax.rsqrt(jnp.concatenate(parts, axis=1) + 1e-06)

    @pl.loop(0, 4)
    def _(img):
        nx = token_norm(keys_in[img, 0:128, :])
        qn[img] = (head_norm(dot(nx, wqkv_ref[:, 0:512])) * scale_ref[...]).astype(BF16)
        kn[img, 0:128, :] = head_norm(dot(nx, wqkv_ref[:, 512:1024])).astype(BF16)
        vv[img, 0:128, :] = dot(nx, wqkv_ref[:, 1024:1536]).astype(BF16)

    for copy in copies:
        copy.wait()
    c_copies = [start_copy(cot_ref, cg.at[z], c_s.at[k], c_r.at[k], z_peers[k]) for k in range(3)]

    @pl.loop(0, 4)
    def _(img):
        nx = token_norm(keys_in[img, 128:384, :])
        kn[img, 128:384, :] = head_norm(dot(nx, wqkv_ref[:, 512:1024])).astype(BF16)
        vv[img, 128:384, :] = dot(nx, wqkv_ref[:, 1024:1536]).astype(BF16)

    ones = jnp.ones((KEYS, 128), BF16)

    @pl.loop(0, 4)
    def _(img):
        mixed = []
        for pair in range(4):
            at = slice(pair * 128, pair * 128 + 128)
            q = qn[img, :, at]
            zero = jnp.zeros_like(q)
            both = jnp.concatenate([jnp.where(lane < 64, q, zero), jnp.where(lane < 64, zero, q)], axis=0)
            powered = jnp.exp(dot_nt(both, kn[img, :, at]) + bias[...]).astype(BF16)
            sums = dot(powered, jnp.concatenate([vv[img, :, at], ones], axis=1))
            ratio = sums[:, 0:128] / sums[:, 128:256]
            mixed.append(jnp.where(lane < 64, ratio[0:128], ratio[128:256]).astype(BF16))
        mix = jnp.concatenate(mixed, axis=1)
        fr[img] = (keys_in[img, 0:128, :].astype(F32) + dot(mix, wout_ref[...])).astype(BF16)

    f_copies = []
    for k, off in enumerate(RING):
        w_copies[k].wait()
        block = wg.at[lax.rem(x - off + 4, 4), half, :]
        f_copies.append(start_copy(block, block, f_s.at[k], f_r.at[k], twin))

    merged = jnp.zeros((128, 1024), F32)
    for p in range(4):
        part = jnp.concatenate([fr[img, p * 32 : p * 32 + 32, :] for img in range(4)], axis=0)
        merged = merged + dot(part, wmerge_ref[p * 512 : p * 512 + 512, :])
    inner = merged.astype(BF16)
    in_ref[...] = inner
    xf = inner.astype(F32)
    factor = lax.rsqrt(jnp.mean(xf * xf, axis=-1, keepdims=True) + 1e-06)
    ng[z] = (xf * factor * gain2_ref[...]).astype(BF16)
    n_copies = [start_copy(ng.at[z], ng.at[z], n_s.at[k], n_r.at[k], z_peers[k]) for k in range(3)]
    for copy in f_copies:
        copy.wait()

    a_copies = []
    for step in range(4):
        if step == 0:
            zi = z
        else:
            zi = lax.rem(z - RING[step - 1] + 4, 4)
            c_copies[step - 1].wait()
            n_copies[step - 1].wait()
        normed, grads = ng[zi], cg[zi]
        for h in range(4):
            first = dot(normed, wg[h])
            second = dot(grads, wg[h, :, 128:256])
            ts[h, zi, :, 0:128] = first[:, 0:128].astype(BF16)
            ts[h, zi, :, 128:256] = jnp.where(lane < 64, first[:, 128:256], second).astype(BF16)
        for d, (px, py, peer) in enumerate(swap):
            rows = pl.ds(pl.multiple_of(py * 32, 32), 32)
            a_copies.append(
                start_copy(ts.at[px, zi, rows, :], tr.at[x * 4 + y, zi], a_s.at[d, step], a_r.at[d, step], peer)
            )
        tr[x * 4 + y, zi] = ts[x, zi, pl.ds(pl.multiple_of(y * 32, 32), 32), :]

    low = jnp.where(sub < 64, 1.0 / 64, 0.0).astype(BF16)
    for d in range(16):
        if d > 0:
            for step in range(4):
                a_copies[step * 15 + d - 1].wait()
        dx, dy = d // 4, d % 4
        slot = lax.rem(x - dx + 4, 4) * 4 + lax.rem(y - dy + 4, 4)
        raw = tr[slot].reshape(128, 256).astype(F32)
        k_f, q_f = raw[:, 0:128], raw[:, 128:256]
        k_n = k_f * lax.rsqrt(dot((k_f * k_f).astype(BF16), low) + 1e-06)
        q_n = q_f * lax.rsqrt(dot((q_f * q_f).astype(BF16), low) + 1e-06) * scale2_ref[...]
        at = pl.ds(pl.multiple_of(slot * 128, 128), 128)
        kv[0, at, :] = jnp.where(lane < 64, k_n, k_f).astype(BF16)
        qg[at, :] = jnp.where(lane < 64, q_n, q_f).astype(BF16)
    start_copy(kv.at[0], kv.at[1], k_s, k_r, twin).wait()


def front(x, gain, wqkv, wout, scale, wmerge, gain2, cot, wpack, scale2):
    sel, place, query = fine_tables()
    vmem = pl.BlockSpec(memory_space=pltpu.VMEM)
    dma = pltpu.SemaphoreType.DMA
    return pl.pallas_call(
        fine_kernel,
        out_shape=(
            jax.ShapeDtypeStruct((128, 1024), BF16),
            jax.ShapeDtypeStruct((4, 128, 1024), BF16),
            jax.ShapeDtypeStruct((4, 128, 1024), BF16),
            jax.ShapeDtypeStruct((4, 1024, 256), BF16),
            jax.ShapeDtypeStruct((16, 4, 32, 256), BF16),
            jax.ShapeDtypeStruct((2048, 128), BF16),
            jax.ShapeDtypeStruct((2, 2048, 128), BF16),
        ),
        in_specs=[vmem] * 13,
        out_specs=(vmem,) * 7,
        scratch_shapes=[
            pltpu.VMEM((4, KEYS, 512), BF16),
            pltpu.VMEM((4, 224, 512), BF16),
            pltpu.VMEM((4, KEYS, 512), BF16),
            pltpu.VMEM((4, KEYS, 512), BF16),
            pltpu.VMEM((4, 128, 512), BF16),
            pltpu.VMEM((4, 128, 512), BF16),
            pltpu.VMEM((256, KEYS), F32),
            pltpu.VMEM((4, 4, 128, 256), BF16),
            dma((8,)), dma((8,)),
            dma((3,)), dma((3,)), dma((3,)), dma((3,)), dma((3,)), dma((3,)), dma((3,)), dma((3,)),
            dma((15, 4)), dma((15, 4)), dma(()), dma(()),
        ],
        compiler_params=pltpu.CompilerParams(
            collective_id=0, has_side_effects=True, vmem_limit_bytes=50 * 1024 * 1024
        ),
        cost_estimate=pl.CostEstimate(flops=8_000_000_000, bytes_accessed=16_000_000, transcendentals=2_000_000),
        name="front",
    )(
        x.reshape(4, 128, 512),
        jnp.asarray(sel, BF16),
        jnp.asarray(place),
        jnp.asarray(query),
        gain.reshape(1, 512),
        wqkv,
        wout,
        jnp.repeat(scale / 64, 64).reshape(1, 512),
        wmerge,
        gain2.reshape(1, 1024),
        cot,
        wpack,
        scale2,
    )


def attention_kernel(qg_ref, kv_ref, back_ref, gqa_ref, gkv_ref, powers, ones_v, sums):
    step = pl.program_id(0)
    lane = lax.broadcasted_iota(jnp.int32, (BLOCK, 128), 1)

    @pl.when(step == 0)
    def _():
        kv = kv_ref[...]
        lanes = lax.broadcasted_iota(jnp.int32, kv.shape, 1)
        ones_v[...] = jnp.where(lanes < 64, jnp.ones_like(kv), kv)
        sums[...] = jnp.zeros_like(sums)

    tile = qg_ref[...]
    zero = jnp.zeros_like(tile)
    q = jnp.where(lane < 64, tile, zero)
    total = jnp.zeros((BLOCK, 128), F32)
    for c in range(4096 // CHUNK):
        at = slice(c * CHUNK, c * CHUNK + CHUNK)
        powered = jnp.exp2(dot_nt(q, kv_ref[at, :])).astype(BF16)
        powers[:, at] = powered
        total = total + dot(powered, ones_v[at, :])
    turned = pltpu.roll(total, 64, 1)
    upper = lane >= 64
    inverse = 1.0 / jnp.where(upper, turned, total)
    outputs = total * inverse
    g = tile.astype(F32)
    delta = jnp.sum(jnp.where(upper, g * outputs, 0.0), axis=1, keepdims=True) * inverse
    high = delta.astype(BF16).astype(F32)
    rest = jnp.where(lane == 0, -high, jnp.where(lane == 1, high - delta, 0.0))
    scaled = jnp.where(upper, g * inverse, rest)
    g_aug = scaled.astype(BF16)
    g_turn = scaled.T[64:128].astype(BF16)
    q_turn = g.T[0:64].astype(BF16)
    grad_q = jnp.zeros((BLOCK, 128), F32)
    for c in range(4096 // CHUNK):
        at = slice(c * CHUNK, c * CHUNK + CHUNK)
        powered = powers[:, at]
        grad_s = (powered.astype(F32) * dot_nt(g_aug, ones_v[at, :])).astype(BF16)
        grad_q = grad_q + dot(grad_s, kv_ref[at, :])
        sums[64:128, at] += dot(g_turn, powered)
        sums[0:64, at] += dot(q_turn, grad_s)
    gqa_ref[...] = jnp.where(upper, outputs, grad_q * back_ref[...])

    @pl.when(step == 2048 // BLOCK - 1)
    def _():
        for c in range(8):
            part = sums[:, c * 512 : c * 512 + 512].T
            lanes = lax.broadcasted_iota(jnp.int32, part.shape, 1)
            gkv_ref[c * 512 : c * 512 + 512, :] = jnp.where(lanes < 64, part * LN2, part)


def attention(qg, kv, back):
    whole = pl.BlockSpec((4096, 128), lambda i: (0, 0))
    part = pl.BlockSpec((BLOCK, 128), lambda i: (i, 0))
    return pl.pallas_call(
        attention_kernel,
        grid=(2048 // BLOCK,),
        out_shape=(jax.ShapeDtypeStruct((2048, 128), F32), jax.ShapeDtypeStruct((4096, 128), F32)),
        in_specs=[part, whole, pl.BlockSpec((1, 128), lambda i: (0, 0))],
        out_specs=(part, whole),
        scratch_shapes=[
            pltpu.VMEM((BLOCK, 4096), BF16),
            pltpu.VMEM((4096, 128), BF16),
            pltpu.VMEM((128, 4096), F32),
        ],
        compiler_params=pltpu.CompilerParams(vmem_limit_bytes=50 * 1024 * 1024),
        cost_estimate=pl.CostEstimate(flops=20_000_000_000, bytes_accessed=8_000_000, transcendentals=8_000_000),
        name="attention",
    )(qg, kv, back)


def back_kernel(
    gkv_ref, gqa_ref, raw_ref, wg_ref, ng_ref, cg_ref, in_ref, cot_ref, gain_ref,
    out_ref, grad_ref, dw_ref, do_ref,
    other, r, rr, ps, pr, ws, wr,
    k_s, k_r, a_s, a_r, p_s, p_r, d_s, d_r,
):
    row, col = lax.axis_index("row"), lax.axis_index("col")
    y, core, x, z = lax.div(row, 2), lax.rem(row, 2), lax.div(col, 4), lax.rem(col, 4)
    barrier = pltpu.get_barrier_semaphore()
    z_peers = [(row, x * 4 + lax.rem(z + off, 4)) for off in RING]
    twin = (y * 2 + 1 - core, col)
    swap = swap_peers(x, y, z, core)
    plane = [
        (dx, dr, lax.rem(x + dx, 4), lax.rem(row + dr, 8))
        for dx in (2, 1, 3, 0)
        for dr in range(8)
    ]
    others = [(pr_, px * 4 + z) for dx, dr, px, pr_ in plane if dx + dr > 0]
    for peer in z_peers + [twin] + [p for _, _, p in swap] + others:
        pl.semaphore_signal(barrier, inc=1, device_id=peer, device_id_type=MESH)
    pl.semaphore_wait(barrier, 50)
    start_copy(gkv_ref.at[1], other, k_s, k_r, twin).wait()

    lane = lax.broadcasted_iota(jnp.int32, (128, 128), 1)
    sub = lax.broadcasted_iota(jnp.int32, (128, 128), 0)
    low = jnp.where(sub < 64, 1.0 / 64, 0.0).astype(BF16)

    def head_back(values, upstream):
        factor = lax.rsqrt(dot((values * values).astype(BF16), low) + 1e-06)
        unit = values * factor
        grad = factor * (upstream - unit * dot((upstream * unit).astype(BF16), low))
        return jnp.where(lane < 64, grad, upstream).astype(BF16)

    def prepare(slot):
        at = pl.ds(pl.multiple_of(slot * 128, 128), 128)
        raw = raw_ref[slot].reshape(128, 256).astype(F32)
        r[slot, :, :, 0:128] = head_back(raw[:, 0:128], gkv_ref[0, at, :] + other[at, :]).reshape(4, 32, 128)
        r[slot, :, :, 128:256] = head_back(raw[:, 128:256], gqa_ref[at, :]).reshape(4, 32, 128)

    mine = pl.ds(pl.multiple_of(y * 32, 32), 32)
    a_copies = []
    for d, (px, py, peer) in enumerate(swap):
        prepare(px * 4 + py)
        a_copies.append(
            start_copy(r.at[px * 4 + py], rr.at[x, :, mine, :], a_s.at[d], a_r.at[d], peer)
        )
    prepare(x * 4 + y)
    rr[x, :, mine, :] = r[x * 4 + y]
    for copy in a_copies:
        copy.wait()

    wide = lax.broadcasted_iota(jnp.int32, (128, 256), 1)

    def partial(zi):
        grad = jnp.zeros((128, 1024), F32)
        term = jnp.zeros((128, 1024), F32)
        for h in range(4):
            part = rr[h, zi]
            zero = jnp.zeros_like(part)
            grad = grad + dot_nt(jnp.where(wide < 192, part, zero), wg_ref[h])
            last = part[:, 128:256]
            term = term + dot_nt(jnp.where(lane >= 64, last, jnp.zeros_like(last)), wg_ref[h, :, 128:256])
        return grad, term

    p_copies = []
    for k in (2, 0, 1):
        zi = lax.rem(z + RING[k], 4)
        grad, term = partial(zi)
        ps[k, 0] = grad.astype(BF16)
        ps[k, 1] = term.astype(BF16)
        p_copies.append(start_copy(ps.at[k], pr.at[k], p_s.at[k], p_r.at[k], z_peers[k]))

    normed = ng_ref[...].reshape(512, 1024)
    cots = cg_ref[...].reshape(512, 1024)
    d_copies = []
    for k in range(4):
        h = plane[k * 8][2]
        turned = rr[h].reshape(512, 256).astype(F32).T.astype(BF16)
        ws[h, 0:192, :] = dot(turned[0:192], normed).astype(BF16)
        ws[h, 192:256, :] = dot(turned[192:256], cots).astype(BF16)
        for dx, dr, px, prow in plane[k * 8 : k * 8 + 8]:
            piece = ws.at[px, :, pl.ds(pl.multiple_of(prow * 128, 128), 128)]
            if dx + dr > 0:
                n = dx * 8 + dr
                d_copies.append(
                    start_copy(piece, wr.at[x * 8 + row], d_s.at[n], d_r.at[n], (prow, px * 4 + z))
                )
    wr[x * 8 + row] = ws[x, :, pl.ds(pl.multiple_of(row * 128, 128), 128)]

    grad, term = partial(z)
    for copy in p_copies:
        copy.wait()
    for k in range(3):
        grad = grad + pr[k, 0].astype(F32)
        term = term + pr[k, 1].astype(F32)
    values = in_ref[...].astype(F32)
    out_ref[...] = (values + term).astype(BF16)
    factor = lax.rsqrt(jnp.mean(values * values, axis=-1, keepdims=True) + 1e-06)
    unit = values * factor
    upstream = grad * gain_ref[...]
    grad_ref[...] = cot_ref[...].astype(F32) + factor * (
        upstream - unit * jnp.mean(upstream * unit, axis=-1, keepdims=True)
    )

    for copy in d_copies:
        copy.wait()
    total = jnp.zeros((256, 128), F32)
    for n in range(32):
        total = total + wr[n].astype(F32)
    do_ref[...] = total[192:256]
    turned = total.T
    dw_ref[0] = turned[:, 128:192]
    dw_ref[1] = turned[:, 0:64]
    dw_ref[2] = turned[:, 64:128]


def back(gkv, gqa, raw, wg, ng, cg, inner, cot, gain):
    vmem = pl.BlockSpec(memory_space=pltpu.VMEM)
    dma = pltpu.SemaphoreType.DMA
    return pl.pallas_call(
        back_kernel,
        out_shape=(
            jax.ShapeDtypeStruct((128, 1024), BF16),
            jax.ShapeDtypeStruct((128, 1024), F32),
            jax.ShapeDtypeStruct((3, 128, 64), F32),
            jax.ShapeDtypeStruct((64, 128), F32),
        ),
        in_specs=[vmem] * 9,
        out_specs=(vmem,) * 4,
        scratch_shapes=[
            pltpu.VMEM((2048, 128), F32),
            pltpu.VMEM((16, 4, 32, 256), BF16),
            pltpu.VMEM((4, 4, 128, 256), BF16),
            pltpu.VMEM((3, 2, 128, 1024), BF16),
            pltpu.VMEM((3, 2, 128, 1024), BF16),
            pltpu.VMEM((4, 256, 1024), BF16),
            pltpu.VMEM((32, 256, 128), BF16),
            dma(()), dma(()), dma((15,)), dma((15,)), dma((3,)), dma((3,)), dma((32,)), dma((32,)),
        ],
        compiler_params=pltpu.CompilerParams(
            collective_id=1, has_side_effects=True, vmem_limit_bytes=50 * 1024 * 1024
        ),
        cost_estimate=pl.CostEstimate(flops=8_000_000_000, bytes_accessed=16_000_000, transcendentals=1_000_000),
        name="back",
    )(gkv, gqa, raw, wg, ng, cg, inner, cot, gain)


def per_device(
    fine_input,
    gain_fine,
    fine_qkv,
    fine_out,
    fine_scale,
    merge_weight,
    gain_coarse,
    coarse_qkv,
    coarse_out,
    coarse_scale,
    cotangent,
):
    cot = cotangent.reshape(128, 1024)
    wpack = jnp.concatenate([coarse_qkv[1], coarse_qkv[2], coarse_qkv[0], coarse_out.T], axis=1)
    back_scale = jnp.broadcast_to(coarse_scale.reshape(1, 1) / 64, (1, 128))
    inner, ng, cg, wg, raw, qg, kv = front(
        fine_input, gain_fine, fine_qkv, fine_out, fine_scale, merge_weight, gain_coarse,
        cot, wpack, back_scale * LOG2E,
    )
    gqa, gkv = attention(qg, kv.reshape(4096, 128), back_scale)
    output, grad, qkv_grad, out_grad = back(
        gkv.reshape(2, 2048, 128), gqa, raw, wg, ng, cg, inner, cot, gain_coarse.reshape(1, 1024)
    )
    return (output.reshape(4, 8, 4, 1024), grad.reshape(4, 8, 4, 1024), qkv_grad, out_grad)


def solution(mesh):
    return jax.shard_map(
        per_device,
        mesh=mesh,
        in_specs=(
            P(None, "row", "col", None),
            P(),
            P(),
            P(),
            P(),
            P(),
            P(),
            P(None, None, "col"),
            P("col", None),
            P("col"),
            P(None, "row", "col", None),
        ),
        out_specs=(
            P(None, "row", "col", None),
            P(None, "row", "col", None),
            P(None, "row", "col"),
            P("col", "row"),
        ),
        check_vma=False,
    )
```

```python
import jax
import jax.numpy as jnp
import numpy as np
from jax import lax
from jax.experimental import pallas as pl
from jax.experimental.pallas import tpu as pltpu
from jax.sharding import PartitionSpec as P

MESH = pl.DeviceIdType.MESH
F32 = jnp.float32
BF16 = jnp.bfloat16
SEG = ((128, 48), (176, 48), (224, 32), (256, 32), (288, 16), (304, 16), (320, 16), (336, 16))
WAY = ((0, 1), (0, -1), (1, 0), (-1, 0), (1, 1), (1, -1), (-1, 1), (-1, -1))
KEYS = 384
RING = (1, 3, 2)
BLOCK = 512
CHUNK = 1024
LOG2E = 1.4426950408889634
LN2 = 0.6931471805599453


def dot(a, b):
    return jnp.dot(a, b, preferred_element_type=F32)


def dot_nt(a, b):
    return lax.dot_general(a, b, (((1,), (1,)), ((), ())), preferred_element_type=F32)


def start_copy(source, target, send_sem, recv_sem, device):
    copy = pltpu.make_async_remote_copy(
        src_ref=source, dst_ref=target, send_sem=send_sem, recv_sem=recv_sem, device_id=device, device_id_type=MESH
    )
    copy.start()
    return copy


def swap_peers(x, y, z, core):
    peers = []
    for d in range(1, 16):
        px, py = lax.rem(x + d // 4, 4), lax.rem(y + d % 4, 4)
        peers.append((px, py, (py * 2 + core, px * 4 + z)))
    return peers


def fine_tables():
    sel = np.zeros((KEYS, 128), np.float32)
    place = np.full((8, KEYS), 10000, np.int32)
    query = np.zeros((256, 128), np.int32)
    for p in range(4):
        for u in range(8):
            for w in range(4):
                n = p * 32 + u * 4 + w
                i, j = 2 * u + p // 2, 2 * w + p % 2
                sel[n, i * 8 + j] = 1
                place[0, n], place[1, n] = i, j
                query[n, 0] = query[n + 128, 0] = i
                query[n, 1] = query[n + 128, 1] = j
    for (start, _), (down, right) in zip(SEG, WAY):
        rows = {0: range(16), 1: range(13, 16), -1: range(3)}[down]
        cols = {0: range(8), 1: range(5, 8), -1: range(3)}[right]
        n = start
        for i in rows:
            for j in cols:
                sel[n, i * 8 + j] = 1
                place[0, n], place[1, n] = i - 16 * down, j - 8 * right
                n += 1
    return sel, place, query


def kernel(
    x_ref, sel_ref, place_ref, query_ref, gain_ref, wqkv_ref, wout_ref, scale_ref, wmerge_ref, gain2_ref,
    cot_ref, wpack_ref, scale2_ref,
    back_ref,
    out_ref, grad_ref, dw_ref, do_ref,
    inner_ref, ng, cg, wg, tr, qg, kv,
    keys_in, send, kn, vv, qn, fr, bias, ts,
    powers, ones_v, sums, r0, r1, rr0, rr1, gsend, grecv, ps, pr, ws, wt, wsum, wr,
    send_sem, recv_sem, w_s, w_r, f_s, f_r, c_s, c_r, n_s, n_r, a_s, a_r, k_s, k_r,
    g_s, g_r, q_s, q_r, b_s, b_r, p_s, p_r, t_s, t_r, d_s, d_r,
):
    row, col = lax.axis_index("row"), lax.axis_index("col")
    y, core, x, z = lax.div(row, 2), lax.rem(row, 2), lax.div(col, 4), lax.rem(col, 4)
    barrier = pltpu.get_barrier_semaphore()
    peers = [(lax.rem(row + a + 8, 8), lax.rem(col + b + 16, 16)) for a, b in WAY]
    z_peers = [(row, x * 4 + lax.rem(z + off, 4)) for off in RING]
    x_peers = [(row, lax.rem(x + off, 4) * 4 + z) for off in RING]
    twin = (y * 2 + 1 - core, col)
    swap = swap_peers(x, y, z, core)
    for peer in peers + z_peers + x_peers + [twin] + [p for _, _, p in swap]:
        pl.semaphore_signal(barrier, inc=1, device_id=peer, device_id_type=MESH)

    wg[x] = wpack_ref[...]
    cg[z] = cot_ref[...]

    @pl.loop(0, 4)
    def _(img):
        packed = dot(sel_ref[...], x_ref[img]).astype(BF16)
        keys_in[img, 0:128, :] = packed[0:128]
        send[img] = packed[128:352]
        keys_in[img, 352:384, :] = packed[352:384]

    pl.semaphore_wait(barrier, 30)
    copies = []
    for k, ((start, size), peer) in enumerate(zip(SEG, peers)):
        copy = pltpu.make_async_remote_copy(
            src_ref=send.at[:, start - 128 : start - 128 + size, :],
            dst_ref=keys_in.at[:, start : start + size, :],
            send_sem=send_sem.at[k],
            recv_sem=recv_sem.at[k],
            device_id=peer,
            device_id_type=MESH,
        )
        copy.start()
        copies.append(copy)

    half = pl.ds(pl.multiple_of(core * 512, 512), 512)
    w_copies = [
        start_copy(wpack_ref.at[half, :], wg.at[x, half, :], w_s.at[k], w_r.at[k], x_peers[k]) for k in range(3)
    ]

    seen = (
        (jnp.abs(place_ref[0:1, :] - query_ref[:, 0:1]) <= 3)
        & (jnp.abs(place_ref[1:2, :] - query_ref[:, 1:2]) <= 3)
    )
    gi = place_ref[0:1, :] + row * 16
    gj = place_ref[1:2, :] + col * 8
    inside = (gi >= 0) & (gi < 128) & (gj >= 0) & (gj < 128)
    bias[...] = jnp.where(seen & inside, 0.0, -1e30).astype(F32)

    lane = lax.broadcasted_iota(jnp.int32, (128, 128), 1)
    sub = lax.broadcasted_iota(jnp.int32, (128, 128), 0)
    same = jnp.where((lane < 64) == (sub < 64), 1.0 / 64, 0.0).astype(BF16)

    def token_norm(tokens):
        xf = tokens.astype(F32)
        factor = lax.rsqrt(jnp.mean(xf * xf, axis=-1, keepdims=True) + 1e-06)
        return (xf * factor * gain_ref[...]).astype(BF16)

    def head_norm(values):
        vf = values.astype(BF16).astype(F32)
        sq = (vf * vf).astype(BF16)
        parts = [dot(sq[:, k * 128 : k * 128 + 128], same) for k in range(4)]
        return vf * lax.rsqrt(jnp.concatenate(parts, axis=1) + 1e-06)

    @pl.loop(0, 4)
    def _(img):
        nx = token_norm(keys_in[img, 0:128, :])
        qn[img] = (head_norm(dot(nx, wqkv_ref[:, 0:512])) * scale_ref[...]).astype(BF16)
        kn[img, 0:128, :] = head_norm(dot(nx, wqkv_ref[:, 512:1024])).astype(BF16)
        vv[img, 0:128, :] = dot(nx, wqkv_ref[:, 1024:1536]).astype(BF16)

    for copy in copies:
        copy.wait()
    c_copies = [start_copy(cot_ref, cg.at[z], c_s.at[k], c_r.at[k], z_peers[k]) for k in range(3)]

    @pl.loop(0, 4)
    def _(img):
        nx = token_norm(keys_in[img, 128:384, :])
        kn[img, 128:384, :] = head_norm(dot(nx, wqkv_ref[:, 512:1024])).astype(BF16)
        vv[img, 128:384, :] = dot(nx, wqkv_ref[:, 1024:1536]).astype(BF16)

    ones = jnp.ones((KEYS, 128), BF16)

    @pl.loop(0, 4)
    def _(img):
        mixed = []
        for pair in range(4):
            at = slice(pair * 128, pair * 128 + 128)
            q = qn[img, :, at]
            zero = jnp.zeros_like(q)
            both = jnp.concatenate([jnp.where(lane < 64, q, zero), jnp.where(lane < 64, zero, q)], axis=0)
            powered = jnp.exp(dot_nt(both, kn[img, :, at]) + bias[...]).astype(BF16)
            sums = dot(powered, jnp.concatenate([vv[img, :, at], ones], axis=1))
            ratio = sums[:, 0:128] / sums[:, 128:256]
            mixed.append(jnp.where(lane < 64, ratio[0:128], ratio[128:256]).astype(BF16))
        mix = jnp.concatenate(mixed, axis=1)
        fr[img] = (keys_in[img, 0:128, :].astype(F32) + dot(mix, wout_ref[...])).astype(BF16)

    f_copies = []
    for k, off in enumerate(RING):
        w_copies[k].wait()
        block = wg.at[lax.rem(x - off + 4, 4), half, :]
        f_copies.append(start_copy(block, block, f_s.at[k], f_r.at[k], twin))

    merged = jnp.zeros((128, 1024), F32)
    for p in range(4):
        part = jnp.concatenate([fr[img, p * 32 : p * 32 + 32, :] for img in range(4)], axis=0)
        merged = merged + dot(part, wmerge_ref[p * 512 : p * 512 + 512, :])
    inner = merged.astype(BF16)
    inner_ref[...] = inner
    xf = inner.astype(F32)
    factor = lax.rsqrt(jnp.mean(xf * xf, axis=-1, keepdims=True) + 1e-06)
    ng[z] = (xf * factor * gain2_ref[...]).astype(BF16)
    up, down = z_peers[0], z_peers[1]
    above, below, far = lax.rem(z + 1, 4), lax.rem(z + 3, 4), lax.rem(z + 2, 4)
    from_below = start_copy(ng.at[z], ng.at[z], n_s.at[0], n_r.at[0], up)
    from_above = start_copy(ng.at[z], ng.at[z], n_s.at[1], n_r.at[1], down)
    for copy in f_copies + c_copies:
        copy.wait()

    a_copies = []
    far_copies = []
    for step, zi in enumerate((z, below, above, far)):
        if step == 1:
            from_below.wait()
            half_block = ng.at[below, 0:64, :]
            far_copies.append(start_copy(half_block, half_block, n_s.at[2], n_r.at[2], up))
            from_above.wait()
            half_block = ng.at[above, 64:128, :]
            far_copies.append(start_copy(half_block, half_block, n_s.at[3], n_r.at[3], down))
        if step == 3:
            for copy in far_copies:
                copy.wait()
        normed, grads = ng[zi], cg[zi]
        for h in range(4):
            first = dot(normed, wg[h])
            second = dot(grads, wg[h, :, 128:256])
            ts[h, zi, :, 0:128] = first[:, 0:128].astype(BF16)
            ts[h, zi, :, 128:256] = jnp.where(lane < 64, first[:, 128:256], second).astype(BF16)
        for d, (px, py, peer) in enumerate(swap):
            rows = pl.ds(pl.multiple_of(py * 32, 32), 32)
            a_copies.append(
                start_copy(ts.at[px, zi, rows, :], tr.at[x * 4 + y, zi], a_s.at[d, step], a_r.at[d, step], peer)
            )
        tr[x * 4 + y, zi] = ts[x, zi, pl.ds(pl.multiple_of(y * 32, 32), 32), :]

    low = jnp.where(sub < 64, 1.0 / 64, 0.0).astype(BF16)
    for d in range(16):
        if d > 0:
            for step in range(4):
                a_copies[step * 15 + d - 1].wait()
        dx, dy = d // 4, d % 4
        slot = lax.rem(x - dx + 4, 4) * 4 + lax.rem(y - dy + 4, 4)
        raw = tr[slot].reshape(128, 256).astype(F32)
        k_f, q_f = raw[:, 0:128], raw[:, 128:256]
        k_n = k_f * lax.rsqrt(dot((k_f * k_f).astype(BF16), low) + 1e-06)
        q_n = q_f * lax.rsqrt(dot((q_f * q_f).astype(BF16), low) + 1e-06) * scale2_ref[...]
        at = pl.ds(pl.multiple_of(slot * 128, 128), 128)
        kv[0, at, :] = jnp.where(lane < 64, k_n, k_f).astype(BF16)
        qg[at, :] = jnp.where(lane < 64, q_n, q_f).astype(BF16)
    start_copy(kv.at[0], kv.at[1], k_s, k_r, twin).wait()

    for part in range(2):
        ones_v[part] = jnp.where(
            lax.broadcasted_iota(jnp.int32, (2048, 128), 1) < 64, jnp.ones((2048, 128), BF16), kv[part]
        )
    sums[...] = jnp.zeros_like(sums)

    def head_back(values, upstream):
        factor = lax.rsqrt(dot((values * values).astype(BF16), low) + 1e-06)
        unit = values * factor
        grad = factor * (upstream - unit * dot((upstream * unit).astype(BF16), low))
        return jnp.where(lane < 64, grad, upstream).astype(BF16)

    tall = lax.broadcasted_iota(jnp.int32, (BLOCK, 128), 1)
    upper = tall >= 64
    mine = pl.ds(pl.multiple_of(y * 32, 32), 32)
    chunks = [(c // 2, slice(c % 2 * CHUNK, c % 2 * CHUNK + CHUNK), slice(c * CHUNK, c * CHUNK + CHUNK)) for c in range(4)]

    def q_copy(i, dy):
        px, py = lax.rem(x + i + 1, 4), lax.rem(y + dy, 4)
        n = lax.rem(i + 1, 4) * 4 + dy
        return pltpu.make_async_remote_copy(
            src_ref=r1.at[px * 4 + py], dst_ref=rr1.at[x, :, mine, :],
            send_sem=q_s.at[n], recv_sem=q_r.at[n],
            device_id=(py * 2 + core, px * 4 + z), device_id_type=MESH,
        )

    @pl.loop(0, 4)
    def _(i):
        block = lax.rem(x + i + 1, 4)
        tile = qg[pl.ds(pl.multiple_of(block * BLOCK, BLOCK), BLOCK), :]
        q = jnp.where(upper, jnp.zeros_like(tile), tile)
        total = jnp.zeros((BLOCK, 128), F32)
        for part, at, wide_at in chunks:
            powered = jnp.exp2(dot_nt(q, kv[part, at, :])).astype(BF16)
            powers[:, wide_at] = powered
            total = total + dot(powered, ones_v[part, at, :])
        turned = pltpu.roll(total, 64, 1)
        inverse = 1.0 / jnp.where(upper, turned, total)
        outputs = total * inverse
        g = tile.astype(F32)
        delta = jnp.sum(jnp.where(upper, g * outputs, 0.0), axis=1, keepdims=True) * inverse
        high = delta.astype(BF16).astype(F32)
        rest = jnp.where(tall == 0, -high, jnp.where(tall == 1, high - delta, 0.0))
        scaled = jnp.where(upper, g * inverse, rest)
        g_aug = scaled.astype(BF16)
        g_turn = scaled.T[64:128].astype(BF16)
        q_turn = g.T[0:64].astype(BF16)
        grad_q = jnp.zeros((BLOCK, 128), F32)
        for part, at, wide_at in chunks:
            powered = powers[:, wide_at]
            grad_s = (powered.astype(F32) * dot_nt(g_aug, ones_v[part, at, :])).astype(BF16)
            grad_q = grad_q + dot(grad_s, kv[part, at, :])
            sums[64:128, wide_at] += dot(g_turn, powered)
            sums[0:64, wide_at] += dot(q_turn, grad_s)
        both = jnp.where(upper, outputs, grad_q * back_ref[...])
        for py in range(4):
            raw = tr[block * 4 + py, :, :, 128:256].reshape(128, 128).astype(F32)
            r1[block * 4 + py] = head_back(raw, both[py * 128 : py * 128 + 128]).reshape(4, 32, 128)
        for dy in range(1, 4):
            q_copy(i, dy).start()

        @pl.when(i < 3)
        def _():
            q_copy(i, 0).start()

    gsend[...] = sums[:, 2048:4096].astype(BF16)
    g_copy = start_copy(gsend, grecv, g_s, g_r, twin)

    rr1[x, :, mine, :] = r1[x * 4 + y]
    for i in range(4):
        for dy in range(4):
            if i < 3 or dy > 0:
                q_copy(i, dy).wait()

    def out_part(zi):
        term = jnp.zeros((128, 1024), F32)
        for h in range(4):
            last = rr1[h, zi]
            term = term + dot_nt(jnp.where(lane >= 64, last, jnp.zeros_like(last)), wg[h, :, 128:256])
        return term

    def grad_part(zi):
        grad = jnp.zeros((128, 1024), F32)
        for h in range(4):
            last = rr1[h, zi]
            both = jnp.concatenate([rr0[h, zi], jnp.where(lane < 64, last, jnp.zeros_like(last))], axis=1)
            grad = grad + dot_nt(both, wg[h])
        return grad

    p_copies = []

    def send_part(kind, k, value):
        ps[kind, k] = value.astype(BF16)
        n = kind * 3 + k
        p_copies.append(start_copy(ps.at[kind, k], pr.at[kind, k], p_s.at[n], p_r.at[n], z_peers[k]))

    def weight_part(part):
        normed = ng[...].reshape(512, 1024)
        cots = cg[...].reshape(512, 1024)
        for h in range(4):
            if part == 0:
                turned = rr0[h].reshape(512, 128).astype(F32).T.astype(BF16)
                value = dot(turned, normed)
            else:
                turned = rr1[h].reshape(512, 128).astype(F32).T.astype(BF16)
                value = jnp.concatenate([dot(turned[0:64], normed), dot(turned[64:128], cots)], axis=0)
            for band in range(8):
                ws[part, band % 2, h, band // 2] = value[:, band * 128 : band * 128 + 128].astype(BF16)
        return start_copy(ws.at[part, 1 - core], wt.at[part], t_s.at[part], t_r.at[part], twin)

    def weight_send(part, copy):
        copy.wait()
        for h in range(4):
            for py in range(4):
                wsum[part, h, py] = (ws[part, core, h, py].astype(F32) + wt[part, h, py].astype(F32)).astype(BF16)
        copies = []
        for d, (px, py, peer) in enumerate(swap):
            n = part * 15 + d
            copies.append(
                start_copy(wsum.at[part, px, py], wr.at[part, x * 4 + y], d_s.at[n], d_r.at[n], peer)
            )
        wr[part, x * 4 + y] = wsum[part, x, y]
        return copies

    for k in (2, 0, 1):
        send_part(0, k, out_part(lax.rem(z + RING[k], 4)))

    g_copy.wait()

    def prepare(slot):
        at = pl.ds(pl.multiple_of(slot * 128, 128), 128)
        upstream = (sums[:, at] + grecv[:, at].astype(F32)).T
        upstream = jnp.where(lane < 64, upstream * LN2, upstream)
        raw = tr[slot, :, :, 0:128].reshape(128, 128).astype(F32)
        r0[slot] = head_back(raw, upstream).reshape(4, 32, 128)

    b_copies = []
    for d, (px, py, peer) in enumerate(swap):
        prepare(px * 4 + py)
        b_copies.append(start_copy(r0.at[px * 4 + py], rr0.at[x, :, mine, :], b_s.at[d], b_r.at[d], peer))
    prepare(x * 4 + y)
    rr0[x, :, mine, :] = r0[x * 4 + y]

    term = out_part(z)
    w_copy = weight_part(1)
    for copy in b_copies:
        copy.wait()
    d_copies = weight_send(1, w_copy)
    for k in (2, 0, 1):
        send_part(1, k, grad_part(lax.rem(z + RING[k], 4)))
    w_copy = weight_part(0)
    grad = grad_part(z)
    d_copies += weight_send(0, w_copy)

    for copy in p_copies:
        copy.wait()
    for k in range(3):
        term = term + pr[0, k].astype(F32)
        grad = grad + pr[1, k].astype(F32)
    values = inner_ref[...].astype(F32)
    out_ref[...] = (values + term).astype(BF16)
    factor = lax.rsqrt(jnp.mean(values * values, axis=-1, keepdims=True) + 1e-06)
    unit = values * factor
    upstream = grad * gain2_ref[...]
    grad_ref[...] = cot_ref[...].astype(F32) + factor * (
        upstream - unit * jnp.mean(upstream * unit, axis=-1, keepdims=True)
    )

    for copy in d_copies:
        copy.wait()
    total = jnp.zeros((128, 128), F32)
    for n in range(16):
        total = total + wr[1, n].astype(F32)
    do_ref[...] = total[64:128]
    dw_ref[0] = total.T[:, 0:64]
    total = jnp.zeros((128, 128), F32)
    for n in range(16):
        total = total + wr[0, n].astype(F32)
    turned = total.T
    dw_ref[1] = turned[:, 0:64]
    dw_ref[2] = turned[:, 64:128]


def per_device(
    fine_input,
    gain_fine,
    fine_qkv,
    fine_out,
    fine_scale,
    merge_weight,
    gain_coarse,
    coarse_qkv,
    coarse_out,
    coarse_scale,
    cotangent,
):
    cot = cotangent.reshape(128, 1024)
    wpack = jnp.concatenate([coarse_qkv[1], coarse_qkv[2], coarse_qkv[0], coarse_out.T], axis=1)
    back_scale = jnp.broadcast_to(coarse_scale.reshape(1, 1) / 64, (1, 128))
    sel, place, query = fine_tables()
    vmem = pl.BlockSpec(memory_space=pltpu.VMEM)
    dma = pltpu.SemaphoreType.DMA
    output, grad, qkv_grad, out_grad = pl.pallas_call(
        kernel,
        out_shape=(
            jax.ShapeDtypeStruct((128, 1024), BF16),
            jax.ShapeDtypeStruct((128, 1024), F32),
            jax.ShapeDtypeStruct((3, 128, 64), F32),
            jax.ShapeDtypeStruct((64, 128), F32),
        ),
        in_specs=[vmem] * 14,
        out_specs=(vmem,) * 4,
        scratch_shapes=[
            pltpu.VMEM((128, 1024), BF16),
            pltpu.VMEM((4, 128, 1024), BF16),
            pltpu.VMEM((4, 128, 1024), BF16),
            pltpu.VMEM((4, 1024, 256), BF16),
            pltpu.VMEM((16, 4, 32, 256), BF16),
            pltpu.VMEM((2048, 128), BF16),
            pltpu.VMEM((2, 2048, 128), BF16),
            pltpu.VMEM((4, KEYS, 512), BF16),
            pltpu.VMEM((4, 224, 512), BF16),
            pltpu.VMEM((4, KEYS, 512), BF16),
            pltpu.VMEM((4, KEYS, 512), BF16),
            pltpu.VMEM((4, 128, 512), BF16),
            pltpu.VMEM((4, 128, 512), BF16),
            pltpu.VMEM((256, KEYS), F32),
            pltpu.VMEM((4, 4, 128, 256), BF16),
            pltpu.VMEM((BLOCK, 4096), BF16),
            pltpu.VMEM((2, 2048, 128), BF16),
            pltpu.VMEM((128, 4096), F32),
            pltpu.VMEM((16, 4, 32, 128), BF16),
            pltpu.VMEM((16, 4, 32, 128), BF16),
            pltpu.VMEM((4, 4, 128, 128), BF16),
            pltpu.VMEM((4, 4, 128, 128), BF16),
            pltpu.VMEM((128, 2048), BF16),
            pltpu.VMEM((128, 2048), BF16),
            pltpu.VMEM((2, 3, 128, 1024), BF16),
            pltpu.VMEM((2, 3, 128, 1024), BF16),
            pltpu.VMEM((2, 2, 4, 4, 128, 128), BF16),
            pltpu.VMEM((2, 4, 4, 128, 128), BF16),
            pltpu.VMEM((2, 4, 4, 128, 128), BF16),
            pltpu.VMEM((2, 16, 128, 128), BF16),
            dma((8,)), dma((8,)),
            dma((3,)), dma((3,)), dma((3,)), dma((3,)), dma((3,)), dma((3,)), dma((4,)), dma((4,)),
            dma((15, 4)), dma((15, 4)), dma(()), dma(()),
            dma(()), dma(()), dma((16,)), dma((16,)), dma((15,)), dma((15,)), dma((6,)), dma((6,)),
            dma((2,)), dma((2,)), dma((30,)), dma((30,)),
        ],
        compiler_params=pltpu.CompilerParams(
            collective_id=0, has_side_effects=True, vmem_limit_bytes=58 * 1024 * 1024
        ),
        cost_estimate=pl.CostEstimate(flops=36_000_000_000, bytes_accessed=16_000_000, transcendentals=12_000_000),
        name="step",
    )(
        fine_input.reshape(4, 128, 512),
        jnp.asarray(sel, BF16),
        jnp.asarray(place),
        jnp.asarray(query),
        gain_fine.reshape(1, 512),
        fine_qkv,
        fine_out,
        jnp.repeat(fine_scale / 64, 64).reshape(1, 512),
        merge_weight,
        gain_coarse.reshape(1, 1024),
        cot,
        wpack,
        back_scale * LOG2E,
        back_scale,
    )
    return (output.reshape(4, 8, 4, 1024), grad.reshape(4, 8, 4, 1024), qkv_grad, out_grad)


def solution(mesh):
    return jax.shard_map(
        per_device,
        mesh=mesh,
        in_specs=(
            P(None, "row", "col", None),
            P(),
            P(),
            P(),
            P(),
            P(),
            P(),
            P(None, None, "col"),
            P("col", None),
            P("col"),
            P(None, "row", "col", None),
        ),
        out_specs=(
            P(None, "row", "col", None),
            P(None, "row", "col", None),
            P(None, "row", "col"),
            P("col", "row"),
        ),
        check_vma=False,
    )
```

```python
import jax
import jax.numpy as jnp
import numpy as np
from jax import lax
from jax.experimental import pallas as pl
from jax.experimental.pallas import tpu as pltpu
from jax.sharding import PartitionSpec as P

MESH = pl.DeviceIdType.MESH
F32 = jnp.float32
BF16 = jnp.bfloat16
SEG = ((128, 48), (176, 48), (224, 32), (256, 32), (288, 16), (304, 16), (320, 16), (336, 16))
WAY = ((0, 1), (0, -1), (1, 0), (-1, 0), (1, 1), (1, -1), (-1, 1), (-1, -1))
KEYS = 384
RING = (1, 3, 2)
BLOCK = 512
LOG2E = 1.4426950408889634
LN2 = 0.6931471805599453


def dot(a, b):
    return jnp.dot(a, b, preferred_element_type=F32)


def dot_nt(a, b):
    return lax.dot_general(a, b, (((1,), (1,)), ((), ())), preferred_element_type=F32)


def start_copy(source, target, send_sem, recv_sem, device):
    copy = pltpu.make_async_remote_copy(
        src_ref=source, dst_ref=target, send_sem=send_sem, recv_sem=recv_sem, device_id=device, device_id_type=MESH
    )
    copy.start()
    return copy


def swap_peers(x, y, z, core):
    peers = []
    for d in range(1, 16):
        px, py = lax.rem(x + d // 4, 4), lax.rem(y + d % 4, 4)
        peers.append((px, py, (py * 2 + core, px * 4 + z)))
    return peers


def fine_tables():
    sel = np.zeros((KEYS, 128), np.float32)
    place = np.full((8, KEYS), 10000, np.int32)
    query = np.zeros((256, 128), np.int32)
    for p in range(4):
        for u in range(8):
            for w in range(4):
                n = p * 32 + u * 4 + w
                i, j = 2 * u + p // 2, 2 * w + p % 2
                sel[n, i * 8 + j] = 1
                place[0, n], place[1, n] = i, j
                query[n, 0] = query[n + 128, 0] = i
                query[n, 1] = query[n + 128, 1] = j
    for (start, _), (down, right) in zip(SEG, WAY):
        rows = {0: range(16), 1: range(13, 16), -1: range(3)}[down]
        cols = {0: range(8), 1: range(5, 8), -1: range(3)}[right]
        n = start
        for i in rows:
            for j in cols:
                sel[n, i * 8 + j] = 1
                place[0, n], place[1, n] = i - 16 * down, j - 8 * right
                n += 1
    return sel, place, query


def kernel(
    x_ref, sel_ref, place_ref, query_ref, gain_ref, wqkv_hbm, wout_hbm, scale_ref, wmerge_hbm, gain2_ref,
    cot_ref, heads_ref, proj_ref, scale2_ref,
    out_ref, grad_ref, dw_ref, do_ref,
    inner_ref, ng, cg, wg, tr, qg, kv,
    keys_in, send, kn, vv, qn, fr, bias, ts,
    powers, ones_v, kvt, vt, g_aug, g_turn, q_turn, gq_turn,
    r0, r1, rq, rr0, rr1, rrq, gsend, grecv, ps, pr, ws, wt, wsum, wr,
    send_sem, recv_sem, w_s, w_r, f_s, f_r, c_s, c_r, n_s, n_r, a_s, a_r, k_s, k_r,
    g_s, g_r, q_s, q_r, b_s, b_r, e_s, e_r, p_s, p_r, t_s, t_r, d_s, d_r, l_s,
):
    row, col = lax.axis_index("row"), lax.axis_index("col")
    y, core, x, z = lax.div(row, 2), lax.rem(row, 2), lax.div(col, 4), lax.rem(col, 4)
    barrier = pltpu.get_barrier_semaphore()
    peers = [(lax.rem(row + a + 8, 8), lax.rem(col + b + 16, 16)) for a, b in WAY]
    z_peers = [(row, x * 4 + lax.rem(z + off, 4)) for off in RING]
    x_peers = [(row, lax.rem(x + off, 4) * 4 + z) for off in RING]
    twin = (y * 2 + 1 - core, col)
    swap = swap_peers(x, y, z, core)
    for peer in peers + z_peers + x_peers + [twin] + [p for _, _, p in swap]:
        pl.semaphore_signal(barrier, inc=1, device_id=peer, device_id_type=MESH)

    wqkv_ref = powers.at[0:512, 1024:2560]
    wout_ref = powers.at[512:1024, 1024:1536]
    wmerge_ref = powers.at[:, 0:1024]
    loads = [
        pltpu.make_async_copy(wqkv_hbm, wqkv_ref, l_s.at[0]),
        pltpu.make_async_copy(wout_hbm, wout_ref, l_s.at[1]),
        pltpu.make_async_copy(wmerge_hbm, wmerge_ref, l_s.at[2]),
    ]
    for load in loads:
        load.start()
    wg[x] = jnp.concatenate(
        [heads_ref[1], heads_ref[2], heads_ref[0], proj_ref[...].astype(F32).T.astype(BF16)], axis=1
    )
    cg[z] = cot_ref[...].reshape(128, 1024)
    back = scale2_ref[...] * (1.0 / 64)
    head_of = lax.shift_right_logical(lax.broadcasted_iota(jnp.int32, (1, 512), 1), 6)
    fine_scale = jnp.zeros((1, 512), F32)
    for h in range(8):
        fine_scale = jnp.where(head_of == h, scale_ref[0:1, h : h + 1] * (1.0 / 64), fine_scale)

    @pl.loop(0, 4)
    def _(img):
        packed = dot(sel_ref[...], x_ref[img]).astype(BF16)
        keys_in[img, 0:128, :] = packed[0:128]
        send[img] = packed[128:352]
        keys_in[img, 352:384, :] = packed[352:384]

    pl.semaphore_wait(barrier, 30)
    copies = []
    for k, ((start, size), peer) in enumerate(zip(SEG, peers)):
        copy = pltpu.make_async_remote_copy(
            src_ref=send.at[:, start - 128 : start - 128 + size, :],
            dst_ref=keys_in.at[:, start : start + size, :],
            send_sem=send_sem.at[k],
            recv_sem=recv_sem.at[k],
            device_id=peer,
            device_id_type=MESH,
        )
        copy.start()
        copies.append(copy)

    half = pl.ds(pl.multiple_of(core * 512, 512), 512)
    w_copies = [
        start_copy(wg.at[x, half, :], wg.at[x, half, :], w_s.at[k], w_r.at[k], x_peers[k]) for k in range(3)
    ]

    seen = (
        (jnp.abs(place_ref[0:1, :] - query_ref[:, 0:1]) <= 3)
        & (jnp.abs(place_ref[1:2, :] - query_ref[:, 1:2]) <= 3)
    )
    gi = place_ref[0:1, :] + row * 16
    gj = place_ref[1:2, :] + col * 8
    inside = (gi >= 0) & (gi < 128) & (gj >= 0) & (gj < 128)
    bias[...] = jnp.where(seen & inside, 0.0, -1e30).astype(F32)

    lane = lax.broadcasted_iota(jnp.int32, (128, 128), 1)
    sub = lax.broadcasted_iota(jnp.int32, (128, 128), 0)
    same = jnp.where((lane < 64) == (sub < 64), 1.0 / 64, 0.0).astype(BF16)

    def token_norm(tokens):
        xf = tokens.astype(F32)
        factor = lax.rsqrt(jnp.mean(xf * xf, axis=-1, keepdims=True) + 1e-06)
        return (xf * factor * gain_ref[...]).astype(BF16)

    def head_norm(values):
        vf = values.astype(BF16).astype(F32)
        sq = (vf * vf).astype(BF16)
        parts = [dot(sq[:, k * 128 : k * 128 + 128], same) for k in range(4)]
        return vf * lax.rsqrt(jnp.concatenate(parts, axis=1) + 1e-06)

    loads[0].wait()

    @pl.loop(0, 4)
    def _(img):
        nx = token_norm(keys_in[img, 0:128, :])
        qn[img] = (head_norm(dot(nx, wqkv_ref[:, 0:512])) * fine_scale).astype(BF16)
        kn[img, 0:128, :] = head_norm(dot(nx, wqkv_ref[:, 512:1024])).astype(BF16)
        vv[img, 0:128, :] = dot(nx, wqkv_ref[:, 1024:1536]).astype(BF16)

    for copy in copies:
        copy.wait()
    c_copies = [start_copy(cg.at[z], cg.at[z], c_s.at[k], c_r.at[k], z_peers[k]) for k in range(3)]

    @pl.loop(0, 4)
    def _(img):
        nx = token_norm(keys_in[img, 128:384, :])
        kn[img, 128:384, :] = head_norm(dot(nx, wqkv_ref[:, 512:1024])).astype(BF16)
        vv[img, 128:384, :] = dot(nx, wqkv_ref[:, 1024:1536]).astype(BF16)

    ones = jnp.ones((KEYS, 128), BF16)
    loads[1].wait()
    loads[2].wait()

    @pl.loop(0, 4)
    def _(img):
        mixed = []
        for pair in range(4):
            at = slice(pair * 128, pair * 128 + 128)
            q = qn[img, :, at]
            zero = jnp.zeros_like(q)
            both = jnp.concatenate([jnp.where(lane < 64, q, zero), jnp.where(lane < 64, zero, q)], axis=0)
            powered = jnp.exp(dot_nt(both, kn[img, :, at]) + bias[...]).astype(BF16)
            sums = dot(powered, jnp.concatenate([vv[img, :, at], ones], axis=1))
            ratio = sums[:, 0:128] / sums[:, 128:256]
            mixed.append(jnp.where(lane < 64, ratio[0:128], ratio[128:256]).astype(BF16))
        mix = jnp.concatenate(mixed, axis=1)
        fr[img] = (keys_in[img, 0:128, :].astype(F32) + dot(mix, wout_ref[...])).astype(BF16)

    f_copies = []
    for k, off in enumerate(RING):
        w_copies[k].wait()
        block = wg.at[lax.rem(x - off + 4, 4), half, :]
        f_copies.append(start_copy(block, block, f_s.at[k], f_r.at[k], twin))

    merged = jnp.zeros((128, 1024), F32)
    for p in range(4):
        part = jnp.concatenate([fr[img, p * 32 : p * 32 + 32, :] for img in range(4)], axis=0)
        merged = merged + dot(part, wmerge_ref[p * 512 : p * 512 + 512, :])
    inner = merged.astype(BF16)
    inner_ref[...] = inner
    xf = inner.astype(F32)
    factor = lax.rsqrt(jnp.mean(xf * xf, axis=-1, keepdims=True) + 1e-06)
    ng[z] = (xf * factor * gain2_ref[...]).astype(BF16)
    up, down = z_peers[0], z_peers[1]
    above, below, far = lax.rem(z + 1, 4), lax.rem(z + 3, 4), lax.rem(z + 2, 4)
    from_below = start_copy(ng.at[z], ng.at[z], n_s.at[0], n_r.at[0], up)
    from_above = start_copy(ng.at[z], ng.at[z], n_s.at[1], n_r.at[1], down)
    for copy in f_copies + c_copies:
        copy.wait()

    a_copies = []
    far_copies = []
    for step, zi in enumerate((z, below, above, far)):
        if step == 1:
            from_below.wait()
            half_block = ng.at[below, 0:64, :]
            far_copies.append(start_copy(half_block, half_block, n_s.at[2], n_r.at[2], up))
            from_above.wait()
            half_block = ng.at[above, 64:128, :]
            far_copies.append(start_copy(half_block, half_block, n_s.at[3], n_r.at[3], down))
        if step == 3:
            for copy in far_copies:
                copy.wait()
        normed, grads = ng[zi], cg[zi]
        for h in range(4):
            first = dot(normed, wg[h])
            second = dot(grads, wg[h, :, 128:256])
            ts[h, zi, :, 0:128] = first[:, 0:128].astype(BF16)
            ts[h, zi, :, 128:256] = jnp.where(lane < 64, first[:, 128:256], second).astype(BF16)
        for d, (px, py, peer) in enumerate(swap):
            rows = pl.ds(pl.multiple_of(py * 32, 32), 32)
            a_copies.append(
                start_copy(ts.at[px, zi, rows, :], tr.at[x * 4 + y, zi], a_s.at[d, step], a_r.at[d, step], peer)
            )
        tr[x * 4 + y, zi] = ts[x, zi, pl.ds(pl.multiple_of(y * 32, 32), 32), :]

    low = jnp.where(sub < 64, 1.0 / 64, 0.0).astype(BF16)
    for d in range(16):
        if d > 0:
            for step in range(4):
                a_copies[step * 15 + d - 1].wait()
        dx, dy = d // 4, d % 4
        slot = lax.rem(x - dx + 4, 4) * 4 + lax.rem(y - dy + 4, 4)
        raw = tr[slot].reshape(128, 256).astype(F32)
        k_f, q_f = raw[:, 0:128], raw[:, 128:256]
        k_n = k_f * lax.rsqrt(dot((k_f * k_f).astype(BF16), low) + 1e-06)
        q_n = q_f * lax.rsqrt(dot((q_f * q_f).astype(BF16), low) + 1e-06) * (back * LOG2E)
        at = pl.ds(pl.multiple_of(slot * 128, 128), 128)
        kv[at, :] = jnp.where(lane < 64, k_n, k_f).astype(BF16)
        qg[at, :] = jnp.where(lane < 64, q_n, q_f).astype(BF16)
    k_copy = start_copy(kv.at[0:2048, :], kv.at[2048:4096, :], k_s, k_r, twin)

    def key_side(c):
        at = slice(c * 512, c * 512 + 512)
        tile = kv[at, :]
        ones_v[at, :] = jnp.where(lax.broadcasted_iota(jnp.int32, (512, 128), 1) < 64, jnp.ones_like(tile), tile)
        turned = tile.astype(F32).T.astype(BF16)
        kvt[:, at] = turned[0:64]
        vt[0:64, at] = turned[64:128]

    vt[64:80, :] = jnp.ones((16, 4096), BF16)
    for c in range(4):
        key_side(c)
    k_copy.wait()
    for c in range(4, 8):
        key_side(c)

    def head_back(values, upstream, means):
        factor = lax.rsqrt(dot((values * values).astype(BF16), means) + 1e-06)
        unit = values * factor
        return factor * (upstream - unit * dot((upstream * unit).astype(BF16), means))

    tall = lax.broadcasted_iota(jnp.int32, (BLOCK, 128), 1)
    sub64 = lax.broadcasted_iota(jnp.int32, (64, BLOCK), 0)
    mine = pl.ds(pl.multiple_of(y * 32, 32), 32)

    def block_copy(source, target, send, recv, i, dy):
        px, py = lax.rem(x + i + 1, 4), lax.rem(y + dy, 4)
        n = lax.rem(i + 1, 4) * 4 + dy
        return pltpu.make_async_remote_copy(
            src_ref=source.at[px * 4 + py], dst_ref=target.at[x, :, mine, :],
            send_sem=send.at[n], recv_sem=recv.at[n],
            device_id=(py * 2 + core, px * 4 + z), device_id_type=MESH,
        )

    def block_start(source, target, send, recv, i):
        for dy in range(1, 4):
            block_copy(source, target, send, recv, i, dy).start()

        @pl.when(i < 3)
        def _():
            block_copy(source, target, send, recv, i, 0).start()

    def block_finish(source, target, send, recv):
        target[x, :, mine, :] = source[x * 4 + y]
        for i in range(4):
            for dy in range(4):
                if i < 3 or dy > 0:
                    block_copy(source, target, send, recv, i, dy).wait()

    @pl.loop(0, 4)
    def _(i):
        block = lax.rem(x + i + 1, 4)
        rows = pl.ds(pl.multiple_of(block * BLOCK, BLOCK), BLOCK)
        tile = qg[rows, :]
        q = jnp.where(tall < 64, tile, jnp.zeros_like(tile))
        for c in range(8):
            at = slice(c * 512, c * 512 + 512)
            powers[rows, at] = jnp.exp2(dot_nt(q, kv[at, :])).astype(BF16)
        total = dot_nt(vt[...], powers[rows, :])
        turned = tile.astype(F32).T
        inverse = 1.0 / total[64:65]
        outputs = total[0:64] * inverse
        g = turned[64:128]
        delta = jnp.sum(g * outputs, axis=0, keepdims=True) * inverse
        high = delta.astype(BF16).astype(F32)
        rest = jnp.where(sub64 == 0, -high, jnp.where(sub64 == 1, high - delta, 0.0))
        scaled = g * inverse
        g_turn[:, rows] = scaled.astype(BF16)
        q_turn[:, rows] = turned[0:64].astype(BF16)
        g_aug[rows, :] = jnp.concatenate([rest, scaled], axis=0).T.astype(BF16)
        attn = jnp.concatenate([jnp.zeros_like(outputs), outputs], axis=0).T.astype(BF16)
        for py in range(4):
            r1[block * 4 + py] = attn[py * 128 : py * 128 + 128].reshape(4, 32, 128)
        block_start(r1, rr1, q_s, q_r, i)

    gq_turn[...] = jnp.zeros_like(gq_turn)

    def key_block(at):
        powered = powers[:, at]
        value_part = dot(g_turn[...], powered)
        powers[:, at] = (powered.astype(F32) * dot_nt(g_aug[...], ones_v[at, :])).astype(BF16)
        grad_s = powers[:, at]
        key_part = dot(q_turn[...], grad_s)
        gq_turn[...] += dot_nt(kvt[:, at], grad_s)
        return jnp.concatenate([key_part * LN2, value_part], axis=0)

    @pl.loop(0, 4)
    def _(i):
        at = pl.ds(pl.multiple_of(i * 512, 512), 512)
        gsend[:, at] = key_block(pl.ds(pl.multiple_of(2048 + i * 512, 512), 512)).astype(BF16)

    g_copy = start_copy(gsend, grecv, g_s, g_r, twin)
    block_finish(r1, rr1, q_s, q_r)

    def out_part(zi):
        term = jnp.zeros((128, 1024), F32)
        for h in range(4):
            term = term + dot_nt(rr1[h, zi], wg[h, :, 128:256])
        return term

    def grad_part(zi):
        grad = jnp.zeros((128, 1024), F32)
        for h in range(4):
            packed = rrq[h, lax.rem(zi, 2)].astype(F32)
            last = jnp.where(lane < 64, jnp.where(zi < 2, packed, pltpu.roll(packed, 64, 1)), 0.0).astype(BF16)
            grad = grad + dot_nt(jnp.concatenate([rr0[h, zi], last], axis=1), wg[h])
        return grad

    p_copies = []

    def send_part(kind, k, value):
        ps[kind, k] = value.astype(BF16)
        n = kind * 3 + k
        p_copies.append(start_copy(ps.at[kind, k], pr.at[kind, k], p_s.at[n], p_r.at[n], z_peers[k]))

    def weight_part(part):
        normed = ng[...].reshape(512, 1024)
        cots = cg[...].reshape(512, 1024)
        for h in range(4):
            if part == 0:
                turned = rr0[h].reshape(512, 128).astype(F32).T.astype(BF16)
                value = dot(turned, normed)
            else:
                turned = rr1[h].reshape(512, 128).astype(F32).T.astype(BF16)[64:128]
                even, odd = rrq[h, 0].astype(F32).T, rrq[h, 1].astype(F32).T
                grad_q = jnp.concatenate([even[0:64], odd[0:64], even[64:128], odd[64:128]], axis=1).astype(BF16)
                value = jnp.concatenate([dot(grad_q, normed), dot(turned, cots)], axis=0)
            for band in range(8):
                ws[part, band % 2, h, band // 2] = value[:, band * 128 : band * 128 + 128].astype(BF16)
        return start_copy(ws.at[part, 1 - core], wt.at[part], t_s.at[part], t_r.at[part], twin)

    def weight_send(part, copy):
        copy.wait()
        for h in range(4):
            for py in range(4):
                wsum[part, h, py] = (ws[part, core, h, py].astype(F32) + wt[part, h, py].astype(F32)).astype(BF16)
        copies = []
        for d, (px, py, peer) in enumerate(swap):
            n = part * 15 + d
            copies.append(
                start_copy(wsum.at[part, px, py], wr.at[part, x * 4 + y], d_s.at[n], d_r.at[n], peer)
            )
        wr[part, x * 4 + y] = wsum[part, x, y]
        return copies

    for k in (2, 0, 1):
        send_part(0, k, out_part(lax.rem(z + RING[k], 4)))

    @pl.loop(0, 4)
    def _(i):
        block = lax.rem(x + i + 1, 4)
        at = pl.ds(pl.multiple_of(block * 512, 512), 512)
        own = key_block(at)

        @pl.when(i == 0)
        def _():
            pltpu.make_async_remote_copy(
                src_ref=gsend, dst_ref=grecv, send_sem=g_s, recv_sem=g_r, device_id=twin, device_id_type=MESH
            ).wait()

        upstream = (own + grecv[:, at].astype(F32)).T
        for py in range(4):
            raw = tr[block * 4 + py, :, :, 0:128].reshape(128, 128).astype(F32)
            part = upstream[py * 128 : py * 128 + 128]
            r0[block * 4 + py] = (
                jnp.where(lane < 64, head_back(raw, part, low), part).astype(BF16).reshape(4, 32, 128)
            )
        block_start(r0, rr0, b_s, b_r, i)

    @pl.loop(0, 4)
    def _(i):
        block = lax.rem(x + i + 1, 4)
        for py in range(4):
            slot = block * 4 + py
            part = gq_turn[:, pl.ds(pl.multiple_of(slot * 128, 128), 128)] * back
            packed = jnp.concatenate([part[:, 0:64], part[:, 64:128]], axis=0).T
            raw = tr[slot, :, :, 128:256].reshape(128, 128).astype(F32)
            raw = jnp.where(lane[0:64] < 64, raw[0:64], pltpu.roll(raw[64:128], 64, 1))
            rq[slot] = head_back(raw, packed, same).astype(BF16).reshape(2, 32, 128)
        block_start(rq, rrq, e_s, e_r, i)

    block_finish(r0, rr0, b_s, b_r)
    w_copy = weight_part(0)
    term = out_part(z)
    block_finish(rq, rrq, e_s, e_r)
    for k in (2, 0, 1):
        send_part(1, k, grad_part(lax.rem(z + RING[k], 4)))
    d_copies = weight_send(0, w_copy)
    w_copy = weight_part(1)
    grad = grad_part(z)
    d_copies += weight_send(1, w_copy)

    for copy in p_copies:
        copy.wait()
    for k in range(3):
        term = term + pr[0, k].astype(F32)
        grad = grad + pr[1, k].astype(F32)
    values = inner_ref[...].astype(F32)
    out_ref[...] = (values + term).astype(BF16).reshape(32, 4, 1024)
    factor = lax.rsqrt(jnp.mean(values * values, axis=-1, keepdims=True) + 1e-06)
    unit = values * factor
    upstream = grad * gain2_ref[...]
    grad = cg[z].astype(F32) + factor * (
        upstream - unit * jnp.mean(upstream * unit, axis=-1, keepdims=True)
    )
    grad_ref[...] = grad.reshape(32, 4, 1024)

    for copy in d_copies:
        copy.wait()
    total = jnp.zeros((128, 128), F32)
    for n in range(16):
        total = total + wr[1, n].astype(F32)
    do_ref[...] = total[64:128]
    dw_ref[0] = total.T[:, 0:64]
    total = jnp.zeros((128, 128), F32)
    for n in range(16):
        total = total + wr[0, n].astype(F32)
    turned = total.T
    dw_ref[1] = turned[:, 0:64]
    dw_ref[2] = turned[:, 64:128]


def per_device(
    fine_input,
    gain_fine,
    fine_qkv,
    fine_out,
    fine_scale,
    merge_weight,
    gain_coarse,
    coarse_qkv,
    coarse_out,
    coarse_scale,
    cotangent,
):
    sel, place, query = fine_tables()
    vmem = pl.BlockSpec(memory_space=pltpu.VMEM)
    hbm = pl.BlockSpec(memory_space=pl.ANY)
    dma = pltpu.SemaphoreType.DMA
    output, grad, qkv_grad, out_grad = pl.pallas_call(
        kernel,
        out_shape=(
            jax.ShapeDtypeStruct((32, 4, 1024), BF16),
            jax.ShapeDtypeStruct((32, 4, 1024), F32),
            jax.ShapeDtypeStruct((3, 128, 64), F32),
            jax.ShapeDtypeStruct((64, 128), F32),
        ),
        in_specs=[vmem] * 5 + [hbm, hbm, vmem, hbm] + [vmem] * 5,
        out_specs=(vmem,) * 4,
        scratch_shapes=[
            pltpu.VMEM((128, 1024), BF16),
            pltpu.VMEM((4, 128, 1024), BF16),
            pltpu.VMEM((4, 128, 1024), BF16),
            pltpu.VMEM((4, 1024, 256), BF16),
            pltpu.VMEM((16, 4, 32, 256), BF16),
            pltpu.VMEM((2048, 128), BF16),
            pltpu.VMEM((4096, 128), BF16),
            pltpu.VMEM((4, KEYS, 512), BF16),
            pltpu.VMEM((4, 224, 512), BF16),
            pltpu.VMEM((4, KEYS, 512), BF16),
            pltpu.VMEM((4, KEYS, 512), BF16),
            pltpu.VMEM((4, 128, 512), BF16),
            pltpu.VMEM((4, 128, 512), BF16),
            pltpu.VMEM((256, KEYS), F32),
            pltpu.VMEM((4, 4, 128, 256), BF16),
            pltpu.VMEM((2048, 4096), BF16),
            pltpu.VMEM((4096, 128), BF16),
            pltpu.VMEM((64, 4096), BF16),
            pltpu.VMEM((80, 4096), BF16),
            pltpu.VMEM((2048, 128), BF16),
            pltpu.VMEM((64, 2048), BF16),
            pltpu.VMEM((64, 2048), BF16),
            pltpu.VMEM((64, 2048), F32),
            pltpu.VMEM((16, 4, 32, 128), BF16),
            pltpu.VMEM((16, 4, 32, 128), BF16),
            pltpu.VMEM((16, 2, 32, 128), BF16),
            pltpu.VMEM((4, 4, 128, 128), BF16),
            pltpu.VMEM((4, 4, 128, 128), BF16),
            pltpu.VMEM((4, 2, 128, 128), BF16),
            pltpu.VMEM((128, 2048), BF16),
            pltpu.VMEM((128, 2048), BF16),
            pltpu.VMEM((2, 3, 128, 1024), BF16),
            pltpu.VMEM((2, 3, 128, 1024), BF16),
            pltpu.VMEM((2, 2, 4, 4, 128, 128), BF16),
            pltpu.VMEM((2, 4, 4, 128, 128), BF16),
            pltpu.VMEM((2, 4, 4, 128, 128), BF16),
            pltpu.VMEM((2, 16, 128, 128), BF16),
            dma((8,)), dma((8,)),
            dma((3,)), dma((3,)), dma((3,)), dma((3,)), dma((3,)), dma((3,)), dma((4,)), dma((4,)),
            dma((15, 4)), dma((15, 4)), dma(()), dma(()),
            dma(()), dma(()), dma((16,)), dma((16,)), dma((16,)), dma((16,)), dma((16,)), dma((16,)), dma((6,)), dma((6,)),
            dma((2,)), dma((2,)), dma((30,)), dma((30,)), dma((3,)),
        ],
        compiler_params=pltpu.CompilerParams(
            collective_id=0, has_side_effects=True, vmem_limit_bytes=60 * 1024 * 1024
        ),
        cost_estimate=pl.CostEstimate(flops=36_000_000_000, bytes_accessed=16_000_000, transcendentals=12_000_000),
        name="step",
    )(
        fine_input.reshape(4, 128, 512),
        jnp.asarray(sel, BF16),
        jnp.asarray(place),
        jnp.asarray(query),
        gain_fine.reshape(1, 512),
        fine_qkv,
        fine_out,
        fine_scale.reshape(1, 8),
        merge_weight,
        gain_coarse.reshape(1, 1024),
        cotangent.reshape(32, 4, 1024),
        coarse_qkv,
        coarse_out,
        coarse_scale.reshape(1, 1),
    )
    return (output.reshape(4, 8, 4, 1024), grad.reshape(4, 8, 4, 1024), qkv_grad, out_grad)


def solution(mesh):
    return jax.shard_map(
        per_device,
        mesh=mesh,
        in_specs=(
            P(None, "row", "col", None),
            P(),
            P(),
            P(),
            P(),
            P(),
            P(),
            P(None, None, "col"),
            P("col", None),
            P("col"),
            P(None, "row", "col", None),
        ),
        out_specs=(
            P(None, "row", "col", None),
            P(None, "row", "col", None),
            P(None, "row", "col"),
            P("col", "row"),
        ),
        check_vma=False,
    )
```

```python
import jax
import jax.numpy as jnp
import numpy as np
from jax import lax
from jax.experimental import pallas as pl
from jax.experimental.pallas import tpu as pltpu
from jax.sharding import PartitionSpec as P

MESH = pl.DeviceIdType.MESH
F32 = jnp.float32
BF16 = jnp.bfloat16
SEG = ((128, 48), (176, 48), (224, 32), (256, 32), (288, 16), (304, 16), (320, 16), (336, 16))
WAY = ((0, 1), (0, -1), (1, 0), (-1, 0), (1, 1), (1, -1), (-1, 1), (-1, -1))
KEYS = 384
RING = (1, 3, 2)
BLOCK = 512
KEY, VALUE, QUERY, ATTN = range(4)
LOG2E = 1.4426950408889634
LN2 = 0.6931471805599453


def dot(a, b):
    return jnp.dot(a, b, preferred_element_type=F32)


def dot_nt(a, b):
    return lax.dot_general(a, b, (((1,), (1,)), ((), ())), preferred_element_type=F32)


def start_copy(source, target, send_sem, recv_sem, device):
    copy = pltpu.make_async_remote_copy(
        src_ref=source, dst_ref=target, send_sem=send_sem, recv_sem=recv_sem, device_id=device, device_id_type=MESH
    )
    copy.start()
    return copy


def swap_peers(x, y, z, core):
    peers = []
    for d in range(1, 16):
        px, py = lax.rem(x + d // 4, 4), lax.rem(y + d % 4, 4)
        peers.append((px, py, (py * 2 + core, px * 4 + z)))
    return peers


def fine_tables():
    sel = np.zeros((KEYS, 128), np.float32)
    place = np.full((8, KEYS), 10000, np.int32)
    query = np.zeros((256, 128), np.int32)
    for p in range(4):
        for u in range(8):
            for w in range(4):
                n = p * 32 + u * 4 + w
                i, j = 2 * u + p // 2, 2 * w + p % 2
                sel[n, i * 8 + j] = 1
                place[0, n], place[1, n] = i, j
                query[n, 0] = query[n + 128, 0] = i
                query[n, 1] = query[n + 128, 1] = j
    for (start, _), (down, right) in zip(SEG, WAY):
        rows = {0: range(16), 1: range(13, 16), -1: range(3)}[down]
        cols = {0: range(8), 1: range(5, 8), -1: range(3)}[right]
        n = start
        for i in rows:
            for j in cols:
                sel[n, i * 8 + j] = 1
                place[0, n], place[1, n] = i - 16 * down, j - 8 * right
                n += 1
    return sel, place, query


def kernel(
    x_ref, sel_ref, place_ref, query_ref, gain_ref, wqkv_hbm, wout_hbm, scale_ref, wmerge_hbm, gain2_ref,
    cot_ref, heads_ref, proj_ref, scale2_ref,
    out_ref, grad_ref, dw_ref, do_ref,
    inner_ref, ng, cg, wg, tr, gr, qg, kv,
    keys_in, send, kn, vv, qn, fr, bias, tk, tq, gs,
    powers, ones_v, kvt, vt, g_aug, g_turn, q_turn, gq_turn, outs_turn, inv, own_v,
    r, rr, gsend, grecv, ps, pr, ws, wt, wsum, wr,
    send_sem, recv_sem, w_s, w_r, f_s, f_r, c_s, c_r, n_s, n_r, a_s, a_r, k_s, k_r,
    x_s, x_r, g_s, g_r, b_s, b_r, p_s, p_r, t_s, t_r, d_s, d_r, l_s,
):
    row, col = lax.axis_index("row"), lax.axis_index("col")
    y, core, x, z = lax.div(row, 2), lax.rem(row, 2), lax.div(col, 4), lax.rem(col, 4)
    barrier = pltpu.get_barrier_semaphore()
    peers = [(lax.rem(row + a + 8, 8), lax.rem(col + b + 16, 16)) for a, b in WAY]
    z_peers = [(row, x * 4 + lax.rem(z + off, 4)) for off in RING]
    x_peers = [(row, lax.rem(x + off, 4) * 4 + z) for off in RING]
    twin = (y * 2 + 1 - core, col)
    swap = swap_peers(x, y, z, core)
    for peer in peers + z_peers + x_peers + [twin] + [p for _, _, p in swap]:
        pl.semaphore_signal(barrier, inc=1, device_id=peer, device_id_type=MESH)

    wqkv_ref = powers.at[0:512, 1024:2560]
    wout_ref = powers.at[512:1024, 1024:1536]
    wmerge_ref = powers.at[:, 0:1024]
    loads = [
        pltpu.make_async_copy(wqkv_hbm, wqkv_ref, l_s.at[0]),
        pltpu.make_async_copy(wout_hbm, wout_ref, l_s.at[1]),
        pltpu.make_async_copy(wmerge_hbm, wmerge_ref, l_s.at[2]),
    ]
    for load in loads:
        load.start()
    own_kv = pl.ds(pl.multiple_of(x * 128, 128), 128)
    own_qo = pl.ds(pl.multiple_of(512 + x * 128, 128), 128)
    wg[:, own_kv] = jnp.concatenate([heads_ref[1], heads_ref[2]], axis=0).astype(F32).T.astype(BF16)
    wg[:, own_qo] = jnp.concatenate([heads_ref[0], proj_ref[...]], axis=0).astype(F32).T.astype(BF16)
    cg[0] = cot_ref[...].reshape(128, 1024)
    back = scale2_ref[...] * (1.0 / 64)
    head_of = lax.shift_right_logical(lax.broadcasted_iota(jnp.int32, (1, 512), 1), 6)
    fine_scale = jnp.zeros((1, 512), F32)
    for h in range(8):
        fine_scale = jnp.where(head_of == h, scale_ref[0:1, h : h + 1] * (1.0 / 64), fine_scale)

    @pl.loop(0, 4)
    def _(img):
        packed = dot(sel_ref[...], x_ref[img]).astype(BF16)
        keys_in[img, 0:128, :] = packed[0:128]
        send[img] = packed[128:352]
        keys_in[img, 352:384, :] = packed[352:384]

    pl.semaphore_wait(barrier, 30)
    copies = []
    for k, ((start, size), peer) in enumerate(zip(SEG, peers)):
        copy = pltpu.make_async_remote_copy(
            src_ref=send.at[:, start - 128 : start - 128 + size, :],
            dst_ref=keys_in.at[:, start : start + size, :],
            send_sem=send_sem.at[k],
            recv_sem=recv_sem.at[k],
            device_id=peer,
            device_id_type=MESH,
        )
        copy.start()
        copies.append(copy)

    seen = (
        (jnp.abs(place_ref[0:1, :] - query_ref[:, 0:1]) <= 3)
        & (jnp.abs(place_ref[1:2, :] - query_ref[:, 1:2]) <= 3)
    )
    gi = place_ref[0:1, :] + row * 16
    gj = place_ref[1:2, :] + col * 8
    inside = (gi >= 0) & (gi < 128) & (gj >= 0) & (gj < 128)
    bias[...] = jnp.where(seen & inside, 0.0, -1e30).astype(F32)

    lane = lax.broadcasted_iota(jnp.int32, (128, 128), 1)
    sub = lax.broadcasted_iota(jnp.int32, (128, 128), 0)
    same = jnp.where((lane < 64) == (sub < 64), 1.0 / 64, 0.0).astype(BF16)

    def token_norm(tokens):
        xf = tokens.astype(F32)
        factor = lax.rsqrt(jnp.mean(xf * xf, axis=-1, keepdims=True) + 1e-06)
        return (xf * factor * gain_ref[...]).astype(BF16)

    def head_norm(values):
        vf = values.astype(BF16).astype(F32)
        sq = (vf * vf).astype(BF16)
        parts = [dot(sq[:, k * 128 : k * 128 + 128], same) for k in range(4)]
        return vf * lax.rsqrt(jnp.concatenate(parts, axis=1) + 1e-06)

    loads[0].wait()

    @pl.loop(0, 4)
    def _(img):
        nx = token_norm(keys_in[img, 0:128, :])
        qn[img] = (head_norm(dot(nx, wqkv_ref[:, 0:512])) * fine_scale).astype(BF16)
        kn[img, 0:128, :] = head_norm(dot(nx, wqkv_ref[:, 512:1024])).astype(BF16)
        vv[img, 0:128, :] = dot(nx, wqkv_ref[:, 1024:1536]).astype(BF16)

    for copy in copies:
        copy.wait()
    half = pl.ds(pl.multiple_of(core * 512, 512), 512)
    quarters = [pl.ds(pl.multiple_of(core * 512 + n * 256, 256), 256) for n in range(2)]

    def head_copies(block, rows, sems, peer, target):
        copies = []
        for n in range(2):
            piece = wg.at[rows, pl.ds(pl.multiple_of(n * 512 + block * 128, 128), 128)]
            copies.append(start_copy(piece, piece, sems[0].at[target, n], sems[1].at[target, n], peer))
        return copies

    w_copies = [head_copies(x, half, (w_s, w_r), x_peers[k], k) for k in range(2)]

    @pl.loop(0, 4)
    def _(img):
        nx = token_norm(keys_in[img, 128:384, :])
        kn[img, 128:384, :] = head_norm(dot(nx, wqkv_ref[:, 512:1024])).astype(BF16)
        vv[img, 128:384, :] = dot(nx, wqkv_ref[:, 1024:1536]).astype(BF16)

    ones = jnp.ones((KEYS, 128), BF16)
    loads[1].wait()
    loads[2].wait()

    @pl.loop(0, 4)
    def _(img):
        mixed = []
        for pair in range(4):
            at = slice(pair * 128, pair * 128 + 128)
            q = qn[img, :, at]
            zero = jnp.zeros_like(q)
            both = jnp.concatenate([jnp.where(lane < 64, q, zero), jnp.where(lane < 64, zero, q)], axis=0)
            powered = jnp.exp(dot_nt(both, kn[img, :, at]) + bias[...]).astype(BF16)
            sums = dot(powered, jnp.concatenate([vv[img, :, at], ones], axis=1))
            ratio = sums[:, 0:128] / sums[:, 128:256]
            mixed.append(jnp.where(lane < 64, ratio[0:128], ratio[128:256]).astype(BF16))
        mix = jnp.concatenate(mixed, axis=1)
        fr[img] = (keys_in[img, 0:128, :].astype(F32) + dot(mix, wout_ref[...])).astype(BF16)

    left, right, across = lax.rem(x + 3, 4), lax.rem(x + 1, 4), lax.rem(x + 2, 4)
    w_far = []
    f_copies = []
    for k, (block, peer) in enumerate(((left, x_peers[0]), (right, x_peers[1]))):
        for copy in w_copies[k]:
            copy.wait()
        w_far += head_copies(block, quarters[k], (w_s, w_r), peer, 2 + k)
        f_copies += head_copies(block, half, (f_s, f_r), twin, k)

    merged = jnp.zeros((128, 1024), F32)
    for p in range(4):
        part = jnp.concatenate([fr[img, p * 32 : p * 32 + 32, :] for img in range(4)], axis=0)
        merged = merged + dot(part, wmerge_ref[p * 512 : p * 512 + 512, :])
    inner = merged.astype(BF16)
    inner_ref[...] = inner
    xf = inner.astype(F32)
    factor = lax.rsqrt(jnp.mean(xf * xf, axis=-1, keepdims=True) + 1e-06)
    ng[0] = (xf * factor * gain2_ref[...]).astype(BF16)
    up, down = z_peers[0], z_peers[1]
    from_below = start_copy(ng.at[0], ng.at[1], n_s.at[0], n_r.at[0], up)
    from_above = start_copy(ng.at[0], ng.at[2], n_s.at[1], n_r.at[1], down)
    for copy in w_far:
        copy.wait()
    f_copies += head_copies(across, half, (f_s, f_r), twin, 2)
    for copy in f_copies:
        copy.wait()

    mine = pl.ds(pl.multiple_of(y * 32, 32), 32)
    here = x * 4 + y
    a_copies = []
    far_copies = []

    def project(j):
        value = dot(ng[j], wg[...]).astype(BF16)
        for h in range(4):
            tk[h, j] = value[:, h * 128 : h * 128 + 128]
            tq[h, j] = value[:, 512 + h * 128 : 640 + h * 128]

    def spread(source, target, pieces, sems):
        copies = []
        for d, (px, py, peer) in enumerate(swap):
            rows = pl.ds(pl.multiple_of(py * 32, 32), 32)
            copies.append(
                start_copy(
                    source.at[px, pieces, rows, :], target.at[here, pieces], sems[0].at[d], sems[1].at[d], peer
                )
            )
        target[here, pieces] = source[x, pieces, mine, :]
        return copies

    def swap_halves(values):
        return pltpu.roll(values, 64, 1)

    project(0)
    a_copies.append(spread(tk, tr, slice(0, 1), (a_s.at[0], a_r.at[0])))
    from_below.wait()
    far_copies.append(
        start_copy(ng.at[1, 0:64, :], ng.at[3, 0:64, :], n_s.at[2], n_r.at[2], up)
    )
    from_above.wait()
    far_copies.append(
        start_copy(ng.at[2, 64:128, :], ng.at[3, 64:128, :], n_s.at[3], n_r.at[3], down)
    )
    c_copies = [
        start_copy(cg.at[0], cg.at[1 + k], c_s.at[k], c_r.at[k], z_peers[k]) for k in range(2)
    ]
    project(1)
    project(2)
    a_copies.append(spread(tk, tr, slice(1, 3), (a_s.at[1], a_r.at[1])))
    for copy in far_copies:
        copy.wait()
    project(3)
    for h in range(4):
        for n in range(2):
            high = swap_halves(tq[h, n + 2].astype(F32))
            tk[h, 4 + n] = jnp.where(lane < 64, tq[h, n].astype(F32), high).astype(BF16)
    a_copies.append(spread(tk, tr, slice(3, 6), (a_s.at[2], a_r.at[2])))
    c_far = []
    for k, peer in enumerate((up, down)):
        c_copies[k].wait()
        rows = slice(k * 64, k * 64 + 64)
        c_far.append(
            start_copy(cg.at[1 + k, rows, :], cg.at[3, rows, :], c_s.at[2 + k], c_r.at[2 + k], peer)
        )

    low = jnp.where(sub < 64, 1.0 / 64, 0.0).astype(BF16)
    lane64 = lane[0:64]
    for d in range(16):
        if d > 0:
            for copies in a_copies:
                copies[d - 1].wait()
        dx, dy = d // 4, d % 4
        slot = lax.rem(x - dx + 4, 4) * 4 + lax.rem(y - dy + 4, 4)
        at = pl.ds(pl.multiple_of(slot * 128, 128), 128)
        k_f = tr[slot, 0:4].reshape(128, 128).astype(F32)
        k_n = k_f * lax.rsqrt(dot((k_f * k_f).astype(BF16), low) + 1e-06)
        kv[at, :] = jnp.where(lane < 64, k_n, k_f).astype(BF16)
        q_f = tr[slot, 4:6].reshape(64, 128).astype(F32)
        q_n = q_f * lax.rsqrt(dot((q_f * q_f).astype(BF16), same) + 1e-06) * (back * LOG2E)
        q_n = jnp.concatenate([q_n, swap_halves(q_n)], axis=0)
        qg[at, :] = jnp.where(lane < 64, q_n, 0.0).astype(BF16)
    k_copy = start_copy(kv.at[0:2048, :], kv.at[2048:4096, :], k_s, k_r, twin)

    for copy in c_far:
        copy.wait()
    for n in range(2):
        first = dot(cg[n], wg[:, 512:1024])
        second = dot(cg[n + 2], wg[:, 512:1024])
        for h in range(4):
            at = slice(h * 128, h * 128 + 128)
            gs[h, n] = jnp.where(lane < 64, swap_halves(first[:, at]), second[:, at]).astype(BF16)
    grad_copies = spread(gs, gr, slice(0, 2), (x_s, x_r))

    def key_side(c):
        at = slice(c * 512, c * 512 + 512)
        tile = kv[at, :]
        ones_v[at, :] = jnp.where(lax.broadcasted_iota(jnp.int32, (512, 128), 1) < 64, jnp.ones_like(tile), tile)
        turned = tile.astype(F32).T.astype(BF16)
        kvt[:, at] = turned[0:64]
        vt[0:64, at] = turned[64:128]

    vt[64:80, :] = jnp.ones((16, 4096), BF16)
    for c in range(4):
        key_side(c)
    k_copy.wait()
    for c in range(4, 8):
        key_side(c)

    def head_back(values, upstream):
        factor = lax.rsqrt(dot((values * values).astype(BF16), same) + 1e-06)
        unit = values * factor
        return factor * (upstream - unit * dot((upstream * unit).astype(BF16), same))

    def pack(turned):
        return jnp.concatenate([turned[:, 0:64], turned[:, 64:128]], axis=0).T

    def block_copy(kind, i, dy):
        px, py = lax.rem(x + i + 1, 4), lax.rem(y + dy, 4)
        n = lax.rem(i + 1, 4) * 4 + dy
        return pltpu.make_async_remote_copy(
            src_ref=r.at[kind, px * 4 + py], dst_ref=rr.at[kind, x, :, mine, :],
            send_sem=b_s.at[kind, n], recv_sem=b_r.at[kind, n],
            device_id=(py * 2 + core, px * 4 + z), device_id_type=MESH,
        )

    def block_start(kind, i):
        for dy in range(1, 4):
            block_copy(kind, i, dy).start()

        @pl.when(i < 3)
        def _():
            block_copy(kind, i, 0).start()

    def block_finish(kind):
        rr[kind, x, :, mine, :] = r[kind, here]
        for i in range(4):
            for dy in range(4):
                if i < 3 or dy > 0:
                    block_copy(kind, i, dy).wait()

    @pl.loop(0, 4)
    def _(i):
        block = lax.rem(x + i + 1, 4)
        rows = pl.ds(pl.multiple_of(block * BLOCK, BLOCK), BLOCK)
        q = qg[rows, :]
        for c in range(8):
            at = slice(c * 512, c * 512 + 512)
            powers[rows, at] = jnp.exp2(dot_nt(q, kv[at, :])).astype(BF16)
        total = dot_nt(vt[...], powers[rows, :])
        inverse = 1.0 / total[64:65]
        outputs = total[0:64] * inverse
        inv[0:1, rows] = inverse
        outs_turn[:, rows] = outputs
        q_turn[:, rows] = q.astype(F32).T[0:64].astype(BF16)
        for py in range(4):
            r[ATTN, block * 4 + py] = pack(outputs[:, py * 128 : py * 128 + 128]).astype(BF16).reshape(2, 32, 128)
        block_start(ATTN, i)

    for copy in grad_copies:
        copy.wait()
    sub64 = lax.broadcasted_iota(jnp.int32, (64, BLOCK), 0)

    @pl.loop(0, 4)
    def _(b):
        rows = pl.ds(pl.multiple_of(b * BLOCK, BLOCK), BLOCK)
        parts = []
        for n in range(4):
            turned = gr[b * 4 + n].reshape(64, 128).astype(F32).T
            parts += [turned[0:64], turned[64:128]]
        g = jnp.concatenate(parts, axis=1)
        inverse = inv[0:1, rows]
        delta = jnp.sum(g * outs_turn[:, rows], axis=0, keepdims=True) * inverse
        high = delta.astype(BF16).astype(F32)
        rest = jnp.where(sub64 == 0, -high, jnp.where(sub64 == 1, high - delta, 0.0))
        scaled = g * inverse
        g_turn[:, rows] = scaled.astype(BF16)
        g_aug[rows, :] = jnp.concatenate([rest, scaled], axis=0).T.astype(BF16)

    for c in range(4):
        at = slice(c * 512, c * 512 + 512)
        gsend[1, :, at] = dot(g_turn[...], powers[:, 2048 + c * 512 : 2560 + c * 512]).astype(BF16)
    twin_v = start_copy(gsend.at[1], grecv.at[1], g_s.at[1], g_r.at[1], twin)
    for c in range(4):
        at = slice(c * 512, c * 512 + 512)
        own_v[:, at] = dot(g_turn[...], powers[:, at])
    gq_turn[...] = jnp.zeros_like(gq_turn)

    def pick(kind, h, j, high):
        packed = rr[kind, h, j % 2].astype(F32)
        return packed if (j >= 2) == high else swap_halves(packed)

    def out_part(j):
        parts = [jnp.where(lane < 64, 0.0, pick(ATTN, h, j, True)).astype(BF16) for h in range(4)]
        return dot_nt(jnp.concatenate(parts, axis=1), wg[:, 512:1024])

    def grad_part(j):
        parts = [jnp.where(lane < 64, pick(KEY, h, j, False), pick(VALUE, h, j, True)) for h in range(4)]
        parts += [jnp.where(lane < 64, pick(QUERY, h, j, False), 0.0) for h in range(4)]
        return dot_nt(jnp.concatenate([part.astype(BF16) for part in parts], axis=1), wg[...])

    p_copies = []

    def send_part(kind, k, value):
        ps[kind, k] = value.astype(BF16)
        n = kind * 3 + k
        p_copies.append(start_copy(ps.at[kind, k], pr.at[kind, k], p_s.at[n], p_r.at[n], z_peers[k]))

    def weight_part(kind):
        tokens = (cg if kind == ATTN else ng)[...].reshape(512, 1024)
        parts = []
        for h in range(4):
            even, odd = rr[kind, h, 0].astype(F32).T, rr[kind, h, 1].astype(F32).T
            parts.append(jnp.concatenate([even[0:64], odd[0:64], even[64:128], odd[64:128]], axis=1).astype(BF16))
        value = dot(jnp.concatenate(parts, axis=0), tokens).astype(BF16)
        for h in range(4):
            for band in range(8):
                ws[kind, band % 2, h, band // 2] = value[h * 64 : h * 64 + 64, band * 128 : band * 128 + 128]
        return start_copy(ws.at[kind, 1 - core], wt.at[kind], t_s.at[kind], t_r.at[kind], twin)

    d_copies = []

    def weight_send(kind, copy):
        copy.wait()
        for h in range(4):
            for py in range(4):
                total = ws[kind, core, h, py].astype(F32) + wt[kind, h, py].astype(F32)
                wsum[kind, h, py] = total.astype(BF16)
        for d, (px, py, peer) in enumerate(swap):
            d_copies.append(
                start_copy(
                    wsum.at[kind, px, py], wr.at[kind, here], d_s.at[kind, d], d_r.at[kind, d], peer
                )
            )
        wr[kind, here] = wsum[kind, x, y]

    block_finish(ATTN)
    for k, j in ((2, 3), (0, 2), (1, 1)):
        send_part(0, k, out_part(j))
    t_attn = weight_part(ATTN)
    twin_v.wait()

    @pl.loop(0, 4)
    def _(i):
        block = lax.rem(x + i + 1, 4)
        for py in range(4):
            slot = block * 4 + py
            at = pl.ds(pl.multiple_of(slot * 128, 128), 128)
            part = own_v[:, at] + grecv[1, :, at].astype(F32)
            r[VALUE, slot] = pack(part).astype(BF16).reshape(2, 32, 128)
        block_start(VALUE, i)

    def key_block(at):
        powers[:, at] = (powers[:, at].astype(F32) * dot_nt(g_aug[...], ones_v[at, :])).astype(BF16)
        grad_s = powers[:, at]
        gq_turn[...] += dot_nt(kvt[:, at], grad_s)
        return dot(q_turn[...], grad_s) * LN2

    @pl.loop(0, 4)
    def _(i):
        at = pl.ds(pl.multiple_of(i * 512, 512), 512)
        gsend[0, :, at] = key_block(pl.ds(pl.multiple_of(2048 + i * 512, 512), 512)).astype(BF16)

    start_copy(gsend.at[0], grecv.at[0], g_s.at[0], g_r.at[0], twin)
    weight_send(ATTN, t_attn)
    block_finish(VALUE)
    t_value = weight_part(VALUE)

    @pl.loop(0, 4)
    def _(i):
        block = lax.rem(x + i + 1, 4)
        at = pl.ds(pl.multiple_of(block * 512, 512), 512)
        own = key_block(at)

        @pl.when(i == 0)
        def _():
            pltpu.make_async_remote_copy(
                src_ref=gsend.at[0], dst_ref=grecv.at[0], send_sem=g_s.at[0], recv_sem=g_r.at[0],
                device_id=twin, device_id_type=MESH,
            ).wait()

        upstream = own + grecv[0, :, at].astype(F32)
        for py in range(4):
            raw = tr[block * 4 + py, 0:4].reshape(128, 128).astype(F32)
            raw = jnp.where(lane64 < 64, raw[0:64], swap_halves(raw[64:128]))
            part = pack(upstream[:, py * 128 : py * 128 + 128])
            r[KEY, block * 4 + py] = head_back(raw, part).astype(BF16).reshape(2, 32, 128)
        block_start(KEY, i)

    @pl.loop(0, 4)
    def _(i):
        block = lax.rem(x + i + 1, 4)
        for py in range(4):
            slot = block * 4 + py
            part = pack(gq_turn[:, pl.ds(pl.multiple_of(slot * 128, 128), 128)] * back)
            raw = tr[slot, 4:6].reshape(64, 128).astype(F32)
            r[QUERY, slot] = head_back(raw, part).astype(BF16).reshape(2, 32, 128)
        block_start(QUERY, i)

    weight_send(VALUE, t_value)
    block_finish(KEY)
    t_key = weight_part(KEY)
    term = out_part(0)
    block_finish(QUERY)
    for k, j in ((2, 3), (0, 2), (1, 1)):
        send_part(1, k, grad_part(j))
    t_query = weight_part(QUERY)
    weight_send(KEY, t_key)
    grad = grad_part(0)
    weight_send(QUERY, t_query)

    for copy in p_copies:
        copy.wait()
    for k in range(3):
        term = term + pr[0, k].astype(F32)
        grad = grad + pr[1, k].astype(F32)
    values = inner_ref[...].astype(F32)
    out_ref[...] = (values + term).astype(BF16).reshape(32, 4, 1024)
    factor = lax.rsqrt(jnp.mean(values * values, axis=-1, keepdims=True) + 1e-06)
    unit = values * factor
    upstream = grad * gain2_ref[...]
    grad = cg[0].astype(F32) + factor * (
        upstream - unit * jnp.mean(upstream * unit, axis=-1, keepdims=True)
    )
    grad_ref[...] = grad.reshape(32, 4, 1024)

    for copy in d_copies:
        copy.wait()
    for kind in range(4):
        total = jnp.zeros((64, 128), F32)
        for n in range(16):
            total = total + wr[kind, n].astype(F32)
        if kind == ATTN:
            do_ref[...] = total
        else:
            dw_ref[(1, 2, 0)[kind]] = total


def store_kernel(a_ref, b_ref, c_ref, d_ref, a_out, b_out, c_out, d_out):
    a_out[...] = a_ref[...]
    b_out[...] = b_ref[...]
    c_out[...] = c_ref[...]
    d_out[...] = d_ref[...]


def per_device(
    fine_input,
    gain_fine,
    fine_qkv,
    fine_out,
    fine_scale,
    merge_weight,
    gain_coarse,
    coarse_qkv,
    coarse_out,
    coarse_scale,
    cotangent,
):
    sel, place, query = fine_tables()
    vmem = pl.BlockSpec(memory_space=pltpu.VMEM)
    hbm = pl.BlockSpec(memory_space=pl.ANY)
    dma = pltpu.SemaphoreType.DMA
    results = pl.pallas_call(
        kernel,
        out_shape=(
            jax.ShapeDtypeStruct((32, 4, 1024), BF16),
            jax.ShapeDtypeStruct((32, 4, 1024), F32),
            jax.ShapeDtypeStruct((3, 64, 128), F32),
            jax.ShapeDtypeStruct((64, 128), F32),
        ),
        in_specs=[vmem] * 5 + [hbm, hbm, vmem, hbm] + [vmem] * 5,
        out_specs=(vmem,) * 4,
        scratch_shapes=[
            pltpu.VMEM((128, 1024), BF16),
            pltpu.VMEM((4, 128, 1024), BF16),
            pltpu.VMEM((4, 128, 1024), BF16),
            pltpu.VMEM((1024, 1024), BF16),
            pltpu.VMEM((16, 6, 32, 128), BF16),
            pltpu.VMEM((16, 2, 32, 128), BF16),
            pltpu.VMEM((2048, 128), BF16),
            pltpu.VMEM((4096, 128), BF16),
            pltpu.VMEM((4, KEYS, 512), BF16),
            pltpu.VMEM((4, 224, 512), BF16),
            pltpu.VMEM((4, KEYS, 512), BF16),
            pltpu.VMEM((4, KEYS, 512), BF16),
            pltpu.VMEM((4, 128, 512), BF16),
            pltpu.VMEM((4, 128, 512), BF16),
            pltpu.VMEM((256, KEYS), F32),
            pltpu.VMEM((4, 6, 128, 128), BF16),
            pltpu.VMEM((4, 4, 128, 128), BF16),
            pltpu.VMEM((4, 2, 128, 128), BF16),
            pltpu.VMEM((2048, 4096), BF16),
            pltpu.VMEM((4096, 128), BF16),
            pltpu.VMEM((64, 4096), BF16),
            pltpu.VMEM((80, 4096), BF16),
            pltpu.VMEM((2048, 128), BF16),
            pltpu.VMEM((64, 2048), BF16),
            pltpu.VMEM((64, 2048), BF16),
            pltpu.VMEM((64, 2048), F32),
            pltpu.VMEM((64, 2048), F32),
            pltpu.VMEM((8, 2048), F32),
            pltpu.VMEM((64, 2048), F32),
            pltpu.VMEM((4, 16, 2, 32, 128), BF16),
            pltpu.VMEM((4, 4, 2, 128, 128), BF16),
            pltpu.VMEM((2, 64, 2048), BF16),
            pltpu.VMEM((2, 64, 2048), BF16),
            pltpu.VMEM((2, 3, 128, 1024), BF16),
            pltpu.VMEM((2, 3, 128, 1024), BF16),
            pltpu.VMEM((4, 2, 4, 4, 64, 128), BF16),
            pltpu.VMEM((4, 4, 4, 64, 128), BF16),
            pltpu.VMEM((4, 4, 4, 64, 128), BF16),
            pltpu.VMEM((4, 16, 64, 128), BF16),
            dma((8,)), dma((8,)),
            dma((4, 2)), dma((4, 2)), dma((3, 2)), dma((3, 2)), dma((4,)), dma((4,)), dma((4,)), dma((4,)),
            dma((3, 15)), dma((3, 15)), dma(()), dma(()),
            dma((15,)), dma((15,)), dma((2,)), dma((2,)), dma((4, 16)), dma((4, 16)), dma((6,)), dma((6,)),
            dma((4,)), dma((4,)), dma((4, 15)), dma((4, 15)), dma((3,)),
        ],
        compiler_params=pltpu.CompilerParams(
            collective_id=0, has_side_effects=True, vmem_limit_bytes=60 * 1024 * 1024
        ),
        cost_estimate=pl.CostEstimate(flops=36_000_000_000, bytes_accessed=16_000_000, transcendentals=12_000_000),
        name="step",
    )(
        fine_input.reshape(4, 128, 512),
        jnp.asarray(sel, BF16),
        jnp.asarray(place),
        jnp.asarray(query),
        gain_fine.reshape(1, 512),
        fine_qkv,
        fine_out,
        fine_scale.reshape(1, 8),
        merge_weight,
        gain_coarse.reshape(1, 1024),
        cotangent.reshape(32, 4, 1024),
        coarse_qkv.transpose(0, 2, 1),
        coarse_out,
        coarse_scale.reshape(1, 1),
    )
    output, grad, qkv_grad, out_grad = pl.pallas_call(
        store_kernel,
        out_shape=tuple(jax.ShapeDtypeStruct(v.shape, v.dtype) for v in results),
        in_specs=[vmem] * 4,
        out_specs=(vmem,) * 4,
        compiler_params=pltpu.CompilerParams(vmem_limit_bytes=60 * 1024 * 1024),
        name="store",
    )(*results)
    return (
        output.reshape(4, 8, 4, 1024),
        grad.reshape(4, 8, 4, 1024),
        qkv_grad.transpose(0, 2, 1),
        out_grad,
    )


def solution(mesh):
    return jax.shard_map(
        per_device,
        mesh=mesh,
        in_specs=(
            P(None, "row", "col", None),
            P(),
            P(),
            P(),
            P(),
            P(),
            P(),
            P(None, None, "col"),
            P("col", None),
            P("col"),
            P(None, "row", "col", None),
        ),
        out_specs=(
            P(None, "row", "col", None),
            P(None, "row", "col", None),
            P(None, "row", "col"),
            P("col", "row"),
        ),
        check_vma=False,
    )
```

```python
import jax
import jax.numpy as jnp
import numpy as np
from jax import lax
from jax.experimental import pallas as pl
from jax.experimental.pallas import tpu as pltpu
from jax.sharding import PartitionSpec as P

MESH = pl.DeviceIdType.MESH
F32 = jnp.float32
BF16 = jnp.bfloat16
SEG = ((128, 48), (176, 48), (224, 32), (256, 32), (288, 16), (304, 16), (320, 16), (336, 16))
WAY = ((0, 1), (0, -1), (1, 0), (-1, 0), (1, 1), (1, -1), (-1, 1), (-1, -1))
KEYS = 384
RING = (1, 3, 2)
BLOCK = 512
ATTN, VALUE, KEY, QUERY = range(4)
LOG2E = 1.4426950408889634
LN2 = 0.6931471805599453


def dot(a, b):
    return jnp.dot(a, b, preferred_element_type=F32)


def dot_nt(a, b):
    return lax.dot_general(a, b, (((1,), (1,)), ((), ())), preferred_element_type=F32)


def start_copy(source, target, send_sem, recv_sem, device):
    copy = pltpu.make_async_remote_copy(
        src_ref=source, dst_ref=target, send_sem=send_sem, recv_sem=recv_sem, device_id=device, device_id_type=MESH
    )
    copy.start()
    return copy


def swap_peers(x, y, z, core):
    peers = []
    for d in range(1, 16):
        px, py = lax.rem(x + d // 4, 4), lax.rem(y + d % 4, 4)
        peers.append((px, py, (py * 2 + core, px * 4 + z)))
    return peers


def fine_tables():
    sel = np.zeros((KEYS, 128), np.float32)
    place = np.full((8, KEYS), 10000, np.int32)
    query = np.zeros((256, 128), np.int32)
    for p in range(4):
        for u in range(8):
            for w in range(4):
                n = p * 32 + u * 4 + w
                i, j = 2 * u + p // 2, 2 * w + p % 2
                sel[n, i * 8 + j] = 1
                place[0, n], place[1, n] = i, j
                query[n, 0] = query[n + 128, 0] = i
                query[n, 1] = query[n + 128, 1] = j
    for (start, _), (down, right) in zip(SEG, WAY):
        rows = {0: range(16), 1: range(13, 16), -1: range(3)}[down]
        cols = {0: range(8), 1: range(5, 8), -1: range(3)}[right]
        n = start
        for i in rows:
            for j in cols:
                sel[n, i * 8 + j] = 1
                place[0, n], place[1, n] = i - 16 * down, j - 8 * right
                n += 1
    return sel, place, query


def kernel(
    x_hbm, sel_hbm, place_hbm, query_hbm, gain_ref, wqkv_hbm, wout_hbm, scale_ref, wmerge_hbm, gain2_ref,
    cot_hbm, heads_hbm, proj_hbm, scale2_ref,
    out_ref, grad_ref, dw_ref, do_ref,
    x_ref, sel_ref, place_ref, query_ref, cot_ref, heads_ref, proj_ref,
    inner_ref, ng, cg, wg, tr, gr, qg, kv,
    keys_in, send, kn, vv, qn, fr, bias, tk, tq, gs,
    powers, ones_v, kvt, vt, g_aug, g_turn, q_turn, gq_turn, outs_turn, inv, own_v,
    r, rr, gsend, grecv, ps, pr, ws, wt, wsum, wr,
    send_sem, recv_sem, w_s, w_r, f_s, f_r, c_s, c_r, n_s, n_r, a_s, a_r, k_s, k_r,
    x_s, x_r, g_s, g_r, b_s, b_r, p_s, p_r, t_s, t_r, d_s, d_r, l_s,
):
    row, col = lax.axis_index("row"), lax.axis_index("col")
    y, core, x, z = lax.div(row, 2), lax.rem(row, 2), lax.div(col, 4), lax.rem(col, 4)
    barrier = pltpu.get_barrier_semaphore()
    peers = [(lax.rem(row + a + 8, 8), lax.rem(col + b + 16, 16)) for a, b in WAY]
    z_peers = [(row, x * 4 + lax.rem(z + off, 4)) for off in RING]
    x_peers = [(row, lax.rem(x + off, 4) * 4 + z) for off in RING]
    twin = (y * 2 + 1 - core, col)
    swap = swap_peers(x, y, z, core)
    for peer in peers + z_peers + x_peers + [twin] + [p for _, _, p in swap]:
        pl.semaphore_signal(barrier, inc=1, device_id=peer, device_id_type=MESH)

    wqkv_ref = powers.at[0:512, 1024:2560]
    wout_ref = powers.at[512:1024, 1024:1536]
    wmerge_ref = powers.at[:, 0:1024]
    pairs = (
        (x_hbm, x_ref), (sel_hbm, sel_ref), (heads_hbm, heads_ref), (proj_hbm, proj_ref), (cot_hbm, cot_ref),
        (place_hbm, place_ref), (query_hbm, query_ref), (wqkv_hbm, wqkv_ref), (wout_hbm, wout_ref),
        (wmerge_hbm, wmerge_ref),
    )
    loads = [pltpu.make_async_copy(pair[0], pair[1], l_s.at[n]) for n, pair in enumerate(pairs)]
    for load in loads:
        load.start()
    back = scale2_ref[...] * (1.0 / 64)
    head_of = lax.shift_right_logical(lax.broadcasted_iota(jnp.int32, (1, 512), 1), 6)
    fine_scale = jnp.zeros((1, 512), F32)
    for h in range(8):
        fine_scale = jnp.where(head_of == h, scale_ref[0:1, h : h + 1] * (1.0 / 64), fine_scale)

    loads[0].wait()
    loads[1].wait()

    @pl.loop(0, 4)
    def _(img):
        packed = dot(sel_ref[...], x_ref[img]).astype(BF16)
        keys_in[img, 0:128, :] = packed[0:128]
        send[img] = packed[128:352]
        keys_in[img, 352:384, :] = packed[352:384]

    pl.semaphore_wait(barrier, 30)
    copies = []
    for k, ((start, size), peer) in enumerate(zip(SEG, peers)):
        copy = pltpu.make_async_remote_copy(
            src_ref=send.at[:, start - 128 : start - 128 + size, :],
            dst_ref=keys_in.at[:, start : start + size, :],
            send_sem=send_sem.at[k],
            recv_sem=recv_sem.at[k],
            device_id=peer,
            device_id_type=MESH,
        )
        copy.start()
        copies.append(copy)

    for load in loads[2:7]:
        load.wait()
    own_kv = pl.ds(pl.multiple_of(x * 128, 128), 128)
    own_qo = pl.ds(pl.multiple_of(512 + x * 128, 128), 128)
    wg[:, own_kv] = jnp.concatenate([heads_ref[1], heads_ref[2]], axis=0).astype(F32).T.astype(BF16)
    wg[:, own_qo] = jnp.concatenate([heads_ref[0], proj_ref[...]], axis=0).astype(F32).T.astype(BF16)
    cg[0] = cot_ref[...].reshape(128, 1024)

    seen = (
        (jnp.abs(place_ref[0:1, :] - query_ref[:, 0:1]) <= 3)
        & (jnp.abs(place_ref[1:2, :] - query_ref[:, 1:2]) <= 3)
    )
    gi = place_ref[0:1, :] + row * 16
    gj = place_ref[1:2, :] + col * 8
    inside = (gi >= 0) & (gi < 128) & (gj >= 0) & (gj < 128)
    bias[...] = jnp.where(seen & inside, 0.0, -1e30).astype(F32)

    lane = lax.broadcasted_iota(jnp.int32, (128, 128), 1)
    sub = lax.broadcasted_iota(jnp.int32, (128, 128), 0)
    same = jnp.where((lane < 64) == (sub < 64), 1.0 / 64, 0.0).astype(BF16)

    def token_norm(tokens):
        xf = tokens.astype(F32)
        factor = lax.rsqrt(jnp.mean(xf * xf, axis=-1, keepdims=True) + 1e-06)
        return (xf * factor * gain_ref[...]).astype(BF16)

    def head_norm(values):
        vf = values.astype(BF16).astype(F32)
        sq = (vf * vf).astype(BF16)
        parts = [dot(sq[:, k * 128 : k * 128 + 128], same) for k in range(4)]
        return vf * lax.rsqrt(jnp.concatenate(parts, axis=1) + 1e-06)

    loads[7].wait()

    @pl.loop(0, 4)
    def _(img):
        nx = token_norm(keys_in[img, 0:128, :])
        qn[img] = (head_norm(dot(nx, wqkv_ref[:, 0:512])) * fine_scale).astype(BF16)
        kn[img, 0:128, :] = head_norm(dot(nx, wqkv_ref[:, 512:1024])).astype(BF16)
        vv[img, 0:128, :] = dot(nx, wqkv_ref[:, 1024:1536]).astype(BF16)

    for copy in copies:
        copy.wait()
    half = pl.ds(pl.multiple_of(core * 512, 512), 512)

    def head_copies(block, rows, sems, peer, target):
        copies = []
        for n in range(2):
            piece = wg.at[rows, pl.ds(pl.multiple_of(n * 512 + block * 128, 128), 128)]
            copies.append(start_copy(piece, piece, sems[0].at[target, n], sems[1].at[target, n], peer))
        return copies

    w_copies = [head_copies(x, half, (w_s, w_r), x_peers[k], k) for k in range(3)]

    ones = jnp.ones((KEYS, 128), BF16)
    loads[8].wait()
    loads[9].wait()

    def tokens_out(img):
        nx = token_norm(keys_in[img, 128:384, :])
        kn[img, 128:384, :] = head_norm(dot(nx, wqkv_ref[:, 512:1024])).astype(BF16)
        vv[img, 128:384, :] = dot(nx, wqkv_ref[:, 1024:1536]).astype(BF16)
        mixed = []
        for pair in range(4):
            at = slice(pair * 128, pair * 128 + 128)
            q = qn[img, :, at]
            zero = jnp.zeros_like(q)
            both = jnp.concatenate([jnp.where(lane < 64, q, zero), jnp.where(lane < 64, zero, q)], axis=0)
            powered = jnp.exp(dot_nt(both, kn[img, :, at]) + bias[...]).astype(BF16)
            sums = dot(powered, jnp.concatenate([vv[img, :, at], ones], axis=1))
            ratio = sums[:, 0:128] / sums[:, 128:256]
            mixed.append(jnp.where(lane < 64, ratio[0:128], ratio[128:256]).astype(BF16))
        mix = jnp.concatenate(mixed, axis=1)
        fr[img] = (keys_in[img, 0:128, :].astype(F32) + dot(mix, wout_ref[...])).astype(BF16)

    n_copies = []
    for part in range(2):
        pl.loop(part * 2, part * 2 + 2)(tokens_out)
        rows = slice(part * 64, part * 64 + 64)
        merged = jnp.zeros((64, 1024), F32)
        for p in range(4):
            group = jnp.concatenate([fr[part * 2 + n, p * 32 : p * 32 + 32, :] for n in range(2)], axis=0)
            merged = merged + dot(group, wmerge_ref[p * 512 : p * 512 + 512, :])
        inner = merged.astype(BF16)
        inner_ref[rows, :] = inner
        xf = inner.astype(F32)
        factor = lax.rsqrt(jnp.mean(xf * xf, axis=-1, keepdims=True) + 1e-06)
        ng[0, rows, :] = (xf * factor * gain2_ref[...]).astype(BF16)
        n_copies.append([
            start_copy(ng.at[0, rows, :], ng.at[1 + k, rows, :], n_s.at[part, k], n_r.at[part, k], z_peers[k])
            for k in range(3)
        ])
    c_copies = [start_copy(cg.at[0], cg.at[1 + k], c_s.at[k], c_r.at[k], z_peers[k]) for k in range(3)]
    f_copies = []
    for k, off in enumerate(RING):
        for copy in w_copies[k]:
            copy.wait()
        f_copies += head_copies(lax.rem(x - off + 4, 4), half, (f_s, f_r), twin, k)
    for copy in f_copies:
        copy.wait()

    mine = pl.ds(pl.multiple_of(y * 32, 32), 32)
    here = x * 4 + y
    a_copies = []

    def project(j):
        value = dot(ng[j], wg[...]).astype(BF16)
        for h in range(4):
            tk[h, j] = value[:, h * 128 : h * 128 + 128]
            tq[h, j] = value[:, 512 + h * 128 : 640 + h * 128]

    def spread(source, target, pieces, sems):
        copies = []
        for d, (px, py, peer) in enumerate(swap):
            rows = pl.ds(pl.multiple_of(py * 32, 32), 32)
            copies.append(
                start_copy(
                    source.at[px, pieces, rows, :], target.at[here, pieces], sems[0].at[d], sems[1].at[d], peer
                )
            )
        target[here, pieces] = source[x, pieces, mine, :]
        return copies

    def swap_halves(values):
        return pltpu.roll(values, 64, 1)

    project(0)
    a_copies.append(spread(tk, tr, slice(0, 1), (a_s.at[0], a_r.at[0])))
    for part in range(2):
        n_copies[part][0].wait()
        n_copies[part][1].wait()
    project(1)
    project(2)
    a_copies.append(spread(tk, tr, slice(1, 3), (a_s.at[1], a_r.at[1])))
    for part in range(2):
        n_copies[part][2].wait()
    project(3)
    for h in range(4):
        for n in range(2):
            high = swap_halves(tq[h, n + 2].astype(F32))
            tk[h, 4 + n] = jnp.where(lane < 64, tq[h, n].astype(F32), high).astype(BF16)
    a_copies.append(spread(tk, tr, slice(3, 6), (a_s.at[2], a_r.at[2])))
    low = jnp.where(sub < 64, 1.0 / 64, 0.0).astype(BF16)
    lane64 = lane[0:64]
    for d in range(16):
        if d > 0:
            for copies in a_copies:
                copies[d - 1].wait()
        dx, dy = d // 4, d % 4
        slot = lax.rem(x - dx + 4, 4) * 4 + lax.rem(y - dy + 4, 4)
        at = pl.ds(pl.multiple_of(slot * 128, 128), 128)
        k_f = tr[slot, 0:4].reshape(128, 128).astype(F32)
        k_n = k_f * lax.rsqrt(dot((k_f * k_f).astype(BF16), low) + 1e-06)
        kv[at, :] = jnp.where(lane < 64, k_n, k_f).astype(BF16)
        q_f = tr[slot, 4:6].reshape(64, 128).astype(F32)
        q_n = q_f * lax.rsqrt(dot((q_f * q_f).astype(BF16), same) + 1e-06) * (back * LOG2E)
        q_n = jnp.concatenate([q_n, swap_halves(q_n)], axis=0)
        qg[at, :] = jnp.where(lane < 64, q_n, 0.0).astype(BF16)
    k_copy = start_copy(kv.at[0:2048, :], kv.at[2048:4096, :], k_s, k_r, twin)

    for copy in c_copies:
        copy.wait()
    for n in range(2):
        first = dot(cg[n], wg[:, 512:1024])
        second = dot(cg[n + 2], wg[:, 512:1024])
        for h in range(4):
            at = slice(h * 128, h * 128 + 128)
            gs[h, n] = jnp.where(lane < 64, swap_halves(first[:, at]), second[:, at]).astype(BF16)
    grad_copies = spread(gs, gr, slice(0, 2), (x_s, x_r))

    def key_side(c):
        at = slice(c * 512, c * 512 + 512)
        tile = kv[at, :]
        ones_v[at, :] = jnp.where(lax.broadcasted_iota(jnp.int32, (512, 128), 1) < 64, jnp.ones_like(tile), tile)
        turned = tile.astype(F32).T.astype(BF16)
        kvt[:, at] = turned[0:64]
        vt[0:64, at] = turned[64:128]

    vt[64:80, :] = jnp.ones((16, 4096), BF16)
    for c in range(4):
        key_side(c)
    k_copy.wait()
    for c in range(4, 8):
        key_side(c)

    def head_back(values, upstream):
        factor = lax.rsqrt(dot((values * values).astype(BF16), same) + 1e-06)
        unit = values * factor
        return factor * (upstream - unit * dot((upstream * unit).astype(BF16), same))

    def pack(turned):
        return jnp.concatenate([turned[:, 0:64], turned[:, 64:128]], axis=0).T

    def block_copy(kind, i, dy):
        px, py = lax.rem(x + i + 1, 4), lax.rem(y + dy, 4)
        n = lax.rem(i + 1, 4) * 4 + dy
        return pltpu.make_async_remote_copy(
            src_ref=r.at[kind, px * 4 + py], dst_ref=rr.at[kind, x, :, mine, :],
            send_sem=b_s.at[kind, n], recv_sem=b_r.at[kind, n],
            device_id=(py * 2 + core, px * 4 + z), device_id_type=MESH,
        )

    def block_start(kind, i):
        for dy in range(1, 4):
            block_copy(kind, i, dy).start()

        @pl.when(i < 3)
        def _():
            block_copy(kind, i, 0).start()

    def block_finish(kind):
        rr[kind, x, :, mine, :] = r[kind, here]
        for i in range(4):
            for dy in range(4):
                if i < 3 or dy > 0:
                    block_copy(kind, i, dy).wait()

    @pl.loop(0, 4)
    def _(i):
        block = lax.rem(x + i + 1, 4)
        rows = pl.ds(pl.multiple_of(block * BLOCK, BLOCK), BLOCK)
        q = qg[rows, :]
        for c in range(8):
            at = slice(c * 512, c * 512 + 512)
            powers[rows, at] = jnp.exp2(dot_nt(q, kv[at, :])).astype(BF16)
        total = dot_nt(vt[...], powers[rows, :])
        inverse = 1.0 / total[64:65]
        outputs = total[0:64] * inverse
        inv[0:1, rows] = inverse
        outs_turn[:, rows] = outputs
        q_turn[:, rows] = q.astype(F32).T[0:64].astype(BF16)
        for py in range(4):
            r[ATTN, block * 4 + py] = pack(outputs[:, py * 128 : py * 128 + 128]).astype(BF16).reshape(2, 32, 128)
        block_start(ATTN, i)

    for copy in grad_copies:
        copy.wait()
    sub64 = lax.broadcasted_iota(jnp.int32, (64, BLOCK), 0)

    @pl.loop(0, 4)
    def _(b):
        rows = pl.ds(pl.multiple_of(b * BLOCK, BLOCK), BLOCK)
        parts = []
        for n in range(4):
            turned = gr[b * 4 + n].reshape(64, 128).astype(F32).T
            parts += [turned[0:64], turned[64:128]]
        g = jnp.concatenate(parts, axis=1)
        inverse = inv[0:1, rows]
        delta = jnp.sum(g * outs_turn[:, rows], axis=0, keepdims=True) * inverse
        high = delta.astype(BF16).astype(F32)
        rest = jnp.where(sub64 == 0, -high, jnp.where(sub64 == 1, high - delta, 0.0))
        scaled = g * inverse
        g_turn[:, rows] = scaled.astype(BF16)
        g_aug[rows, :] = jnp.concatenate([rest, scaled], axis=0).T.astype(BF16)

    for c in range(4):
        at = slice(c * 512, c * 512 + 512)
        gsend[1, :, at] = dot(g_turn[...], powers[:, 2048 + c * 512 : 2560 + c * 512]).astype(BF16)
    twin_v = start_copy(gsend.at[1], grecv.at[1], g_s.at[1], g_r.at[1], twin)
    for c in range(4):
        at = slice(c * 512, c * 512 + 512)
        own_v[:, at] = dot(g_turn[...], powers[:, at])
    gq_turn[...] = jnp.zeros_like(gq_turn)

    def pick(kind, h, j, high):
        packed = rr[kind, h, j % 2].astype(F32)
        return packed if (j >= 2) == high else swap_halves(packed)

    def out_part(j):
        parts = [jnp.where(lane < 64, 0.0, pick(ATTN, h, j, True)).astype(BF16) for h in range(4)]
        return dot_nt(jnp.concatenate(parts, axis=1), wg[:, 512:1024])

    def grad_part(j):
        parts = [jnp.where(lane < 64, pick(KEY, h, j, False), pick(VALUE, h, j, True)) for h in range(4)]
        parts += [jnp.where(lane < 64, pick(QUERY, h, j, False), 0.0) for h in range(4)]
        return dot_nt(jnp.concatenate([part.astype(BF16) for part in parts], axis=1), wg[...])

    p_copies = []

    def send_part(kind, k, value):
        ps[kind, k] = value.astype(BF16)
        n = kind * 3 + k
        p_copies.append(start_copy(ps.at[kind, k], pr.at[kind, k], p_s.at[n], p_r.at[n], z_peers[k]))

    def weight_part(kind):
        tokens = (cg if kind == ATTN else ng)[...].reshape(512, 1024)
        parts = []
        for h in range(4):
            even, odd = rr[kind, h, 0].astype(F32).T, rr[kind, h, 1].astype(F32).T
            parts.append(jnp.concatenate([even[0:64], odd[0:64], even[64:128], odd[64:128]], axis=1).astype(BF16))
        value = dot(jnp.concatenate(parts, axis=0), tokens).astype(BF16)
        for h in range(4):
            for band in range(8):
                piece = value[h * 64 : h * 64 + 64, band * 128 : band * 128 + 128]
                ws[band % 2, kind, h, band // 2] = piece

    def weight_twin(kinds, n):
        return start_copy(ws.at[1 - core, kinds], wt.at[kinds], t_s.at[n], t_r.at[n], twin)

    d_copies = []

    def weight_send(kinds, n):
        for kind in range(kinds.start, kinds.stop):
            for h in range(4):
                for py in range(4):
                    total = ws[core, kind, h, py].astype(F32) + wt[kind, h, py].astype(F32)
                    wsum[h, py, kind] = total.astype(BF16)
        for d, (px, py, peer) in enumerate(swap):
            d_copies.append(
                start_copy(wsum.at[px, py, kinds], wr.at[here, kinds], d_s.at[n, d], d_r.at[n, d], peer)
            )
        wr[here, kinds] = wsum[x, y, kinds]

    block_finish(ATTN)
    for k, j in ((2, 3), (0, 2), (1, 1)):
        send_part(0, k, out_part(j))
    twin_v.wait()

    @pl.loop(0, 4)
    def _(i):
        block = lax.rem(x + i + 1, 4)
        for py in range(4):
            slot = block * 4 + py
            at = pl.ds(pl.multiple_of(slot * 128, 128), 128)
            part = own_v[:, at] + grecv[1, :, at].astype(F32)
            r[VALUE, slot] = pack(part).astype(BF16).reshape(2, 32, 128)
        block_start(VALUE, i)

    def key_block(at):
        powers[:, at] = (powers[:, at].astype(F32) * dot_nt(g_aug[...], ones_v[at, :])).astype(BF16)
        grad_s = powers[:, at]
        gq_turn[...] += dot_nt(kvt[:, at], grad_s)
        return dot(q_turn[...], grad_s) * LN2

    @pl.loop(0, 4)
    def _(i):
        at = pl.ds(pl.multiple_of(i * 512, 512), 512)
        gsend[0, :, at] = key_block(pl.ds(pl.multiple_of(2048 + i * 512, 512), 512)).astype(BF16)

    start_copy(gsend.at[0], grecv.at[0], g_s.at[0], g_r.at[0], twin)

    @pl.loop(0, 4)
    def _(i):
        block = lax.rem(x + i + 1, 4)
        at = pl.ds(pl.multiple_of(block * 512, 512), 512)
        own = key_block(at)

        @pl.when(i == 0)
        def _():
            pltpu.make_async_remote_copy(
                src_ref=gsend.at[0], dst_ref=grecv.at[0], send_sem=g_s.at[0], recv_sem=g_r.at[0],
                device_id=twin, device_id_type=MESH,
            ).wait()

        upstream = own + grecv[0, :, at].astype(F32)
        for py in range(4):
            raw = tr[block * 4 + py, 0:4].reshape(128, 128).astype(F32)
            raw = jnp.where(lane64 < 64, raw[0:64], swap_halves(raw[64:128]))
            part = pack(upstream[:, py * 128 : py * 128 + 128])
            r[KEY, block * 4 + py] = head_back(raw, part).astype(BF16).reshape(2, 32, 128)
        block_start(KEY, i)

    @pl.loop(0, 4)
    def _(i):
        block = lax.rem(x + i + 1, 4)
        for py in range(4):
            slot = block * 4 + py
            part = pack(gq_turn[:, pl.ds(pl.multiple_of(slot * 128, 128), 128)] * back)
            raw = tr[slot, 4:6].reshape(64, 128).astype(F32)
            r[QUERY, slot] = head_back(raw, part).astype(BF16).reshape(2, 32, 128)
        block_start(QUERY, i)

    block_finish(VALUE)
    weight_part(ATTN)
    weight_part(VALUE)
    first = weight_twin(slice(0, 2), 0)
    block_finish(KEY)
    weight_part(KEY)
    first.wait()
    weight_send(slice(0, 2), 0)
    term = out_part(0)
    block_finish(QUERY)
    for k, j in ((2, 3), (0, 2), (1, 1)):
        send_part(1, k, grad_part(j))
    weight_part(QUERY)
    last = weight_twin(slice(2, 4), 1)
    grad = grad_part(0)
    last.wait()
    weight_send(slice(2, 4), 1)

    for copy in p_copies:
        copy.wait()
    for k in range(3):
        term = term + pr[0, k].astype(F32)
        grad = grad + pr[1, k].astype(F32)
    values = inner_ref[...].astype(F32)
    out_ref[...] = (values + term).astype(BF16).reshape(32, 4, 1024)
    factor = lax.rsqrt(jnp.mean(values * values, axis=-1, keepdims=True) + 1e-06)
    unit = values * factor
    upstream = grad * gain2_ref[...]
    grad = cg[0].astype(F32) + factor * (
        upstream - unit * jnp.mean(upstream * unit, axis=-1, keepdims=True)
    )
    grad_ref[...] = grad.reshape(32, 4, 1024)

    for copy in d_copies:
        copy.wait()
    for kind in range(4):
        total = jnp.zeros((64, 128), F32)
        for n in range(16):
            total = total + wr[n, kind].astype(F32)
        if kind == ATTN:
            do_ref[...] = total
        else:
            dw_ref[(3, 2, 1, 0)[kind]] = total


def store_kernel(a_ref, b_ref, c_ref, d_ref, a_out, b_out, c_out, d_out):
    a_out[...] = a_ref[...]
    b_out[...] = b_ref[...]
    c_out[...] = c_ref[...]
    d_out[...] = d_ref[...]


def per_device(
    fine_input,
    gain_fine,
    fine_qkv,
    fine_out,
    fine_scale,
    merge_weight,
    gain_coarse,
    coarse_qkv,
    coarse_out,
    coarse_scale,
    cotangent,
):
    sel, place, query = fine_tables()
    vmem = pl.BlockSpec(memory_space=pltpu.VMEM)
    hbm = pl.BlockSpec(memory_space=pl.ANY)
    dma = pltpu.SemaphoreType.DMA
    results = pl.pallas_call(
        kernel,
        out_shape=(
            jax.ShapeDtypeStruct((32, 4, 1024), BF16),
            jax.ShapeDtypeStruct((32, 4, 1024), F32),
            jax.ShapeDtypeStruct((3, 64, 128), F32),
            jax.ShapeDtypeStruct((64, 128), F32),
        ),
        in_specs=[hbm] * 4 + [vmem, hbm, hbm, vmem, hbm, vmem] + [hbm] * 3 + [vmem],
        out_specs=(vmem,) * 4,
        scratch_shapes=[
            pltpu.VMEM((4, 128, 512), BF16),
            pltpu.VMEM((KEYS, 128), BF16),
            pltpu.VMEM((8, KEYS), jnp.int32),
            pltpu.VMEM((256, 128), jnp.int32),
            pltpu.VMEM((32, 4, 1024), BF16),
            pltpu.VMEM((3, 64, 1024), BF16),
            pltpu.VMEM((64, 1024), BF16),
            pltpu.VMEM((128, 1024), BF16),
            pltpu.VMEM((4, 128, 1024), BF16),
            pltpu.VMEM((4, 128, 1024), BF16),
            pltpu.VMEM((1024, 1024), BF16),
            pltpu.VMEM((16, 6, 32, 128), BF16),
            pltpu.VMEM((16, 2, 32, 128), BF16),
            pltpu.VMEM((2048, 128), BF16),
            pltpu.VMEM((4096, 128), BF16),
            pltpu.VMEM((4, KEYS, 512), BF16),
            pltpu.VMEM((4, 224, 512), BF16),
            pltpu.VMEM((4, KEYS, 512), BF16),
            pltpu.VMEM((4, KEYS, 512), BF16),
            pltpu.VMEM((4, 128, 512), BF16),
            pltpu.VMEM((4, 128, 512), BF16),
            pltpu.VMEM((256, KEYS), F32),
            pltpu.VMEM((4, 6, 128, 128), BF16),
            pltpu.VMEM((4, 4, 128, 128), BF16),
            pltpu.VMEM((4, 2, 128, 128), BF16),
            pltpu.VMEM((2048, 4096), BF16),
            pltpu.VMEM((4096, 128), BF16),
            pltpu.VMEM((64, 4096), BF16),
            pltpu.VMEM((80, 4096), BF16),
            pltpu.VMEM((2048, 128), BF16),
            pltpu.VMEM((64, 2048), BF16),
            pltpu.VMEM((64, 2048), BF16),
            pltpu.VMEM((64, 2048), F32),
            pltpu.VMEM((64, 2048), F32),
            pltpu.VMEM((8, 2048), F32),
            pltpu.VMEM((64, 2048), F32),
            pltpu.VMEM((4, 16, 2, 32, 128), BF16),
            pltpu.VMEM((4, 4, 2, 128, 128), BF16),
            pltpu.VMEM((2, 64, 2048), BF16),
            pltpu.VMEM((2, 64, 2048), BF16),
            pltpu.VMEM((2, 3, 128, 1024), BF16),
            pltpu.VMEM((2, 3, 128, 1024), BF16),
            pltpu.VMEM((2, 4, 4, 4, 64, 128), BF16),
            pltpu.VMEM((4, 4, 4, 64, 128), BF16),
            pltpu.VMEM((4, 4, 4, 64, 128), BF16),
            pltpu.VMEM((16, 4, 64, 128), BF16),
            dma((8,)), dma((8,)),
            dma((3, 2)), dma((3, 2)), dma((3, 2)), dma((3, 2)), dma((3,)), dma((3,)), dma((2, 3)), dma((2, 3)),
            dma((3, 15)), dma((3, 15)), dma(()), dma(()),
            dma((15,)), dma((15,)), dma((2,)), dma((2,)), dma((4, 16)), dma((4, 16)), dma((6,)), dma((6,)),
            dma((2,)), dma((2,)), dma((2, 15)), dma((2, 15)), dma((10,)),
        ],
        compiler_params=pltpu.CompilerParams(
            collective_id=0, has_side_effects=True, vmem_limit_bytes=60 * 1024 * 1024
        ),
        cost_estimate=pl.CostEstimate(flops=36_000_000_000, bytes_accessed=16_000_000, transcendentals=12_000_000),
        name="step",
    )(
        fine_input.reshape(4, 128, 512),
        jnp.asarray(sel, BF16),
        jnp.asarray(place),
        jnp.asarray(query),
        gain_fine.reshape(1, 512),
        fine_qkv,
        fine_out,
        fine_scale.reshape(1, 8),
        merge_weight,
        gain_coarse.reshape(1, 1024),
        cotangent.reshape(32, 4, 1024),
        coarse_qkv.transpose(0, 2, 1),
        coarse_out,
        coarse_scale.reshape(1, 1),
    )
    output, grad, qkv_grad, out_grad = pl.pallas_call(
        store_kernel,
        out_shape=tuple(jax.ShapeDtypeStruct(v.shape, v.dtype) for v in results),
        in_specs=[vmem] * 4,
        out_specs=(vmem,) * 4,
        compiler_params=pltpu.CompilerParams(vmem_limit_bytes=60 * 1024 * 1024),
        name="store",
    )(*results)
    return (
        output.reshape(4, 8, 4, 1024),
        grad.reshape(4, 8, 4, 1024),
        qkv_grad.transpose(0, 2, 1),
        out_grad,
    )


def solution(mesh):
    return jax.shard_map(
        per_device,
        mesh=mesh,
        in_specs=(
            P(None, "row", "col", None),
            P(),
            P(),
            P(),
            P(),
            P(),
            P(),
            P(None, None, "col"),
            P("col", None),
            P("col"),
            P(None, "row", "col", None),
        ),
        out_specs=(
            P(None, "row", "col", None),
            P(None, "row", "col", None),
            P(None, "row", "col"),
            P("col", "row"),
        ),
        check_vma=False,
    )
```

```python
import jax
import jax.numpy as jnp
import numpy as np
from jax import lax
from jax.experimental import pallas as pl
from jax.experimental.pallas import tpu as pltpu
from jax.sharding import PartitionSpec as P

MESH = pl.DeviceIdType.MESH
F32 = jnp.float32
BF16 = jnp.bfloat16
SEG = ((128, 48), (176, 48), (224, 32), (256, 32), (288, 16), (304, 16), (320, 16), (336, 16))
WAY = ((0, 1), (0, -1), (1, 0), (-1, 0), (1, 1), (1, -1), (-1, 1), (-1, -1))
KEYS = 384
RING = (1, 3, 2)
BLOCK = 512
ATTN, VALUE, KEY, QUERY = range(4)
LOG2E = 1.4426950408889634
LN2 = 0.6931471805599453


def dot(a, b):
    return jnp.dot(a, b, preferred_element_type=F32)


def dot_nt(a, b):
    return lax.dot_general(a, b, (((1,), (1,)), ((), ())), preferred_element_type=F32)


def start_copy(source, target, send_sem, recv_sem, device):
    copy = pltpu.make_async_remote_copy(
        src_ref=source, dst_ref=target, send_sem=send_sem, recv_sem=recv_sem, device_id=device, device_id_type=MESH
    )
    copy.start()
    return copy


def swap_peers(x, y, z, core):
    peers = []
    for d in range(1, 16):
        px, py = lax.rem(x + d // 4, 4), lax.rem(y + d % 4, 4)
        peers.append((px, py, (py * 2 + core, px * 4 + z)))
    return peers


def fine_tables():
    sel = np.zeros((KEYS, 128), np.float32)
    place = np.full((8, KEYS), 10000, np.int32)
    query = np.zeros((256, 128), np.int32)
    for p in range(4):
        for u in range(8):
            for w in range(4):
                n = p * 32 + u * 4 + w
                i, j = 2 * u + p // 2, 2 * w + p % 2
                sel[n, i * 8 + j] = 1
                place[0, n], place[1, n] = i, j
                query[n, 0] = query[n + 128, 0] = i
                query[n, 1] = query[n + 128, 1] = j
    for (start, _), (down, right) in zip(SEG, WAY):
        rows = {0: range(16), 1: range(13, 16), -1: range(3)}[down]
        cols = {0: range(8), 1: range(5, 8), -1: range(3)}[right]
        n = start
        for i in rows:
            for j in cols:
                sel[n, i * 8 + j] = 1
                place[0, n], place[1, n] = i - 16 * down, j - 8 * right
                n += 1
    return sel, place, query


def kernel(
    x_hbm, sel_hbm, place_hbm, query_hbm, gain_ref, wqkv_hbm, wout_hbm, scale_ref, wmerge_hbm, gain2_ref,
    cot_hbm, heads_hbm, proj_hbm, scale2_ref,
    out_ref, grad_ref, dw_ref, do_ref,
    x_ref, sel_ref, place_ref, query_ref, cot_ref, heads_ref, proj_ref,
    inner_ref, ng, cg, wg, tr, gr, qg, kv,
    keys_in, send, kn, vv, qn, fr, bias, tk, tq, gs,
    powers, ones_v, kvt, vt, g_aug, g_turn, q_turn, gq_turn, outs_turn, inv, own_v,
    r, rr, gsend, grecv, ps, pr, ws, wt, wsum, wr,
    send_sem, recv_sem, w_s, w_r, f_s, f_r, c_s, c_r, n_s, n_r, a_s, a_r, k_s, k_r,
    x_s, x_r, g_s, g_r, b_s, b_r, p_s, p_r, t_s, t_r, d_s, d_r, l_s,
):
    row, col = lax.axis_index("row"), lax.axis_index("col")
    y, core, x, z = lax.div(row, 2), lax.rem(row, 2), lax.div(col, 4), lax.rem(col, 4)
    barrier = pltpu.get_barrier_semaphore()
    peers = [(lax.rem(row + a + 8, 8), lax.rem(col + b + 16, 16)) for a, b in WAY]
    z_peers = [(row, x * 4 + lax.rem(z + off, 4)) for off in RING]
    x_peers = [(row, lax.rem(x + off, 4) * 4 + z) for off in RING]
    twin = (y * 2 + 1 - core, col)
    swap = swap_peers(x, y, z, core)
    for peer in peers + z_peers + x_peers + [twin] + [p for _, _, p in swap]:
        pl.semaphore_signal(barrier, inc=1, device_id=peer, device_id_type=MESH)

    wqkv_ref = powers.at[0:512, 1024:2560]
    wout_ref = powers.at[512:1024, 1024:1536]
    wmerge_ref = powers.at[:, 0:1024]
    pairs = (
        (x_hbm, x_ref), (sel_hbm, sel_ref), (heads_hbm, heads_ref), (proj_hbm, proj_ref), (cot_hbm, cot_ref),
        (place_hbm, place_ref), (query_hbm, query_ref), (wqkv_hbm, wqkv_ref), (wout_hbm, wout_ref),
        (wmerge_hbm, wmerge_ref),
    )
    loads = [pltpu.make_async_copy(pair[0], pair[1], l_s.at[n]) for n, pair in enumerate(pairs)]
    for load in loads:
        load.start()
    back = scale2_ref[...] * (1.0 / 64)
    head_of = lax.shift_right_logical(lax.broadcasted_iota(jnp.int32, (1, 512), 1), 6)
    fine_scale = jnp.zeros((1, 512), F32)
    for h in range(8):
        fine_scale = jnp.where(head_of == h, scale_ref[0:1, h : h + 1] * (1.0 / 64), fine_scale)

    loads[0].wait()
    loads[1].wait()

    @pl.loop(0, 4)
    def _(img):
        packed = dot(sel_ref[...], x_ref[img]).astype(BF16)
        keys_in[img, 0:128, :] = packed[0:128]
        send[img] = packed[128:352]
        keys_in[img, 352:384, :] = packed[352:384]

    pl.semaphore_wait(barrier, 30)
    copies = []
    for k, ((start, size), peer) in enumerate(zip(SEG, peers)):
        copy = pltpu.make_async_remote_copy(
            src_ref=send.at[:, start - 128 : start - 128 + size, :],
            dst_ref=keys_in.at[:, start : start + size, :],
            send_sem=send_sem.at[k],
            recv_sem=recv_sem.at[k],
            device_id=peer,
            device_id_type=MESH,
        )
        copy.start()
        copies.append(copy)

    for load in loads[2:7]:
        load.wait()
    own_kv = pl.ds(pl.multiple_of(x * 128, 128), 128)
    own_qo = pl.ds(pl.multiple_of(512 + x * 128, 128), 128)
    wg[:, own_kv] = jnp.concatenate([heads_ref[1], heads_ref[2]], axis=0).astype(F32).T.astype(BF16)
    wg[:, own_qo] = jnp.concatenate([heads_ref[0], proj_ref[...]], axis=0).astype(F32).T.astype(BF16)
    cg[0] = cot_ref[...].reshape(128, 1024)

    seen = (
        (jnp.abs(place_ref[0:1, :] - query_ref[:, 0:1]) <= 3)
        & (jnp.abs(place_ref[1:2, :] - query_ref[:, 1:2]) <= 3)
    )
    gi = place_ref[0:1, :] + row * 16
    gj = place_ref[1:2, :] + col * 8
    inside = (gi >= 0) & (gi < 128) & (gj >= 0) & (gj < 128)
    bias[...] = jnp.where(seen & inside, 0.0, -1e30).astype(F32)

    lane = lax.broadcasted_iota(jnp.int32, (128, 128), 1)
    sub = lax.broadcasted_iota(jnp.int32, (128, 128), 0)
    same = jnp.where((lane < 64) == (sub < 64), 1.0 / 64, 0.0).astype(BF16)

    def token_norm(tokens):
        xf = tokens.astype(F32)
        factor = lax.rsqrt(jnp.mean(xf * xf, axis=-1, keepdims=True) + 1e-06)
        return (xf * factor * gain_ref[...]).astype(BF16)

    def head_norm(values):
        vf = values.astype(BF16).astype(F32)
        sq = (vf * vf).astype(BF16)
        parts = [dot(sq[:, k * 128 : k * 128 + 128], same) for k in range(4)]
        return vf * lax.rsqrt(jnp.concatenate(parts, axis=1) + 1e-06)

    loads[7].wait()

    @pl.loop(0, 4)
    def _(img):
        nx = token_norm(keys_in[img, 0:128, :])
        qn[img] = (head_norm(dot(nx, wqkv_ref[:, 0:512])) * fine_scale).astype(BF16)
        kn[img, 0:128, :] = head_norm(dot(nx, wqkv_ref[:, 512:1024])).astype(BF16)
        vv[img, 0:128, :] = dot(nx, wqkv_ref[:, 1024:1536]).astype(BF16)

    for copy in copies:
        copy.wait()
    half = pl.ds(pl.multiple_of(core * 512, 512), 512)

    def head_copies(block, rows, sems, peer, target):
        copies = []
        for n in range(2):
            piece = wg.at[rows, pl.ds(pl.multiple_of(n * 512 + block * 128, 128), 128)]
            copies.append(start_copy(piece, piece, sems[0].at[target, n], sems[1].at[target, n], peer))
        return copies

    w_copies = [head_copies(x, half, (w_s, w_r), x_peers[k], k) for k in range(3)]

    ones = jnp.ones((KEYS, 128), BF16)
    loads[8].wait()
    loads[9].wait()

    def tokens_out(img):
        nx = token_norm(keys_in[img, 128:384, :])
        kn[img, 128:384, :] = head_norm(dot(nx, wqkv_ref[:, 512:1024])).astype(BF16)
        vv[img, 128:384, :] = dot(nx, wqkv_ref[:, 1024:1536]).astype(BF16)
        mixed = []
        for pair in range(4):
            at = slice(pair * 128, pair * 128 + 128)
            q = qn[img, :, at]
            zero = jnp.zeros_like(q)
            both = jnp.concatenate([jnp.where(lane < 64, q, zero), jnp.where(lane < 64, zero, q)], axis=0)
            powered = jnp.exp(dot_nt(both, kn[img, :, at]) + bias[...]).astype(BF16)
            sums = dot(powered, jnp.concatenate([vv[img, :, at], ones], axis=1))
            ratio = sums[:, 0:128] / sums[:, 128:256]
            mixed.append(jnp.where(lane < 64, ratio[0:128], ratio[128:256]).astype(BF16))
        mix = jnp.concatenate(mixed, axis=1)
        fr[img] = (keys_in[img, 0:128, :].astype(F32) + dot(mix, wout_ref[...])).astype(BF16)

    n_copies = []
    for part in range(2):
        pl.loop(part * 2, part * 2 + 2)(tokens_out)
        rows = slice(part * 64, part * 64 + 64)
        merged = jnp.zeros((64, 1024), F32)
        for p in range(4):
            group = jnp.concatenate([fr[part * 2 + n, p * 32 : p * 32 + 32, :] for n in range(2)], axis=0)
            merged = merged + dot(group, wmerge_ref[p * 512 : p * 512 + 512, :])
        inner = merged.astype(BF16)
        inner_ref[rows, :] = inner
        xf = inner.astype(F32)
        factor = lax.rsqrt(jnp.mean(xf * xf, axis=-1, keepdims=True) + 1e-06)
        ng[0, rows, :] = (xf * factor * gain2_ref[...]).astype(BF16)
        n_copies.append([
            start_copy(ng.at[0, rows, :], ng.at[1 + k, rows, :], n_s.at[part, k], n_r.at[part, k], z_peers[k])
            for k in range(3)
        ])
    c_copies = [start_copy(cg.at[0], cg.at[1 + k], c_s.at[k], c_r.at[k], z_peers[k]) for k in range(3)]
    f_copies = []
    for k, off in enumerate(RING):
        for copy in w_copies[k]:
            copy.wait()
        f_copies += head_copies(lax.rem(x - off + 4, 4), half, (f_s, f_r), twin, k)
    for copy in f_copies:
        copy.wait()

    mine = pl.ds(pl.multiple_of(y * 32, 32), 32)
    here = x * 4 + y
    a_copies = []

    def project(first, last):
        value = dot(ng[first:last].reshape((last - first) * 128, 1024), wg[...]).astype(BF16)
        for j in range(first, last):
            rows = slice((j - first) * 128, (j - first) * 128 + 128)
            for h in range(4):
                tk[h, j] = value[rows, h * 128 : h * 128 + 128]
                tq[h, j] = value[rows, 512 + h * 128 : 640 + h * 128]

    def spread(source, target, pieces, sems):
        copies = []
        for d, (px, py, peer) in enumerate(swap):
            rows = pl.ds(pl.multiple_of(py * 32, 32), 32)
            copies.append(
                start_copy(
                    source.at[px, pieces, rows, :], target.at[here, pieces], sems[0].at[d], sems[1].at[d], peer
                )
            )
        target[here, pieces] = source[x, pieces, mine, :]
        return copies

    def swap_halves(values):
        return pltpu.roll(values, 64, 1)

    project(0, 1)
    a_copies.append(spread(tk, tr, slice(0, 1), (a_s.at[0], a_r.at[0])))
    for part in range(2):
        for copy in n_copies[part]:
            copy.wait()
    project(1, 4)
    for h in range(4):
        for n in range(2):
            high = swap_halves(tq[h, n + 2].astype(F32))
            tk[h, 4 + n] = jnp.where(lane < 64, tq[h, n].astype(F32), high).astype(BF16)
    a_copies.append(spread(tk, tr, slice(1, 6), (a_s.at[1], a_r.at[1])))
    low = jnp.where(sub < 64, 1.0 / 64, 0.0).astype(BF16)
    lane64 = lane[0:64]
    for d in range(16):
        if d > 0:
            for copies in a_copies:
                copies[d - 1].wait()
        dx, dy = d // 4, d % 4
        slot = lax.rem(x - dx + 4, 4) * 4 + lax.rem(y - dy + 4, 4)
        at = pl.ds(pl.multiple_of(slot * 128, 128), 128)
        k_f = tr[slot, 0:4].reshape(128, 128).astype(F32)
        k_n = k_f * lax.rsqrt(dot((k_f * k_f).astype(BF16), low) + 1e-06)
        kv[at, :] = jnp.where(lane < 64, k_n, k_f).astype(BF16)
        q_f = tr[slot, 4:6].reshape(64, 128).astype(F32)
        q_n = q_f * lax.rsqrt(dot((q_f * q_f).astype(BF16), same) + 1e-06) * (back * LOG2E)
        q_n = jnp.concatenate([q_n, swap_halves(q_n)], axis=0)
        qg[at, :] = jnp.where(lane < 64, q_n, 0.0).astype(BF16)
    k_copy = start_copy(kv.at[0:2048, :], kv.at[2048:4096, :], k_s, k_r, twin)

    for copy in c_copies:
        copy.wait()
    for n in range(2):
        first = dot(cg[n], wg[:, 512:1024])
        second = dot(cg[n + 2], wg[:, 512:1024])
        for h in range(4):
            at = slice(h * 128, h * 128 + 128)
            gs[h, n] = jnp.where(lane < 64, swap_halves(first[:, at]), second[:, at]).astype(BF16)
    grad_copies = spread(gs, gr, slice(0, 2), (x_s, x_r))

    def key_side(c):
        at = slice(c * 512, c * 512 + 512)
        tile = kv[at, :]
        ones_v[at, :] = jnp.where(lax.broadcasted_iota(jnp.int32, (512, 128), 1) < 64, jnp.ones_like(tile), tile)
        turned = tile.astype(F32).T.astype(BF16)
        kvt[:, at] = turned[0:64]
        vt[0:64, at] = turned[64:128]

    vt[64:80, :] = jnp.ones((16, 4096), BF16)
    for c in range(4):
        key_side(c)
    k_copy.wait()
    for c in range(4, 8):
        key_side(c)

    def head_back(values, upstream):
        factor = lax.rsqrt(dot((values * values).astype(BF16), same) + 1e-06)
        unit = values * factor
        return factor * (upstream - unit * dot((upstream * unit).astype(BF16), same))

    def pack(turned):
        return jnp.concatenate([turned[:, 0:64], turned[:, 64:128]], axis=0).T

    def block_copy(kind, i, dy):
        px, py = lax.rem(x + i + 1, 4), lax.rem(y + dy, 4)
        n = lax.rem(i + 1, 4) * 4 + dy
        return pltpu.make_async_remote_copy(
            src_ref=r.at[kind, px * 4 + py], dst_ref=rr.at[kind, x, :, mine, :],
            send_sem=b_s.at[kind, n], recv_sem=b_r.at[kind, n],
            device_id=(py * 2 + core, px * 4 + z), device_id_type=MESH,
        )

    def block_start(kind, i):
        for dy in range(1, 4):
            block_copy(kind, i, dy).start()

        @pl.when(i < 3)
        def _():
            block_copy(kind, i, 0).start()

    def block_finish(kind):
        rr[kind, x, :, mine, :] = r[kind, here]
        for i in range(4):
            for dy in range(4):
                if i < 3 or dy > 0:
                    block_copy(kind, i, dy).wait()

    @pl.loop(0, 4)
    def _(i):
        block = lax.rem(x + i + 1, 4)
        rows = pl.ds(pl.multiple_of(block * BLOCK, BLOCK), BLOCK)
        q = qg[rows, :]
        for c in range(8):
            at = slice(c * 512, c * 512 + 512)
            powers[rows, at] = jnp.exp2(dot_nt(q, kv[at, :])).astype(BF16)
        total = dot_nt(vt[...], powers[rows, :])
        inverse = 1.0 / total[64:65]
        outputs = total[0:64] * inverse
        inv[0:1, rows] = inverse
        outs_turn[:, rows] = outputs
        q_turn[:, rows] = q.astype(F32).T[0:64].astype(BF16)
        for py in range(4):
            r[ATTN, block * 4 + py] = pack(outputs[:, py * 128 : py * 128 + 128]).astype(BF16).reshape(2, 32, 128)
        block_start(ATTN, i)

    for copy in grad_copies:
        copy.wait()
    sub64 = lax.broadcasted_iota(jnp.int32, (64, BLOCK), 0)

    @pl.loop(0, 4)
    def _(b):
        rows = pl.ds(pl.multiple_of(b * BLOCK, BLOCK), BLOCK)
        parts = []
        for n in range(4):
            turned = gr[b * 4 + n].reshape(64, 128).astype(F32).T
            parts += [turned[0:64], turned[64:128]]
        g = jnp.concatenate(parts, axis=1)
        inverse = inv[0:1, rows]
        delta = jnp.sum(g * outs_turn[:, rows], axis=0, keepdims=True) * inverse
        high = delta.astype(BF16).astype(F32)
        rest = jnp.where(sub64 == 0, -high, jnp.where(sub64 == 1, high - delta, 0.0))
        scaled = g * inverse
        g_turn[:, rows] = scaled.astype(BF16)
        g_aug[rows, :] = jnp.concatenate([rest, scaled], axis=0).T.astype(BF16)

    for c in range(4):
        at = slice(c * 512, c * 512 + 512)
        gsend[1, :, at] = dot(g_turn[...], powers[:, 2048 + c * 512 : 2560 + c * 512]).astype(BF16)
    twin_v = start_copy(gsend.at[1], grecv.at[1], g_s.at[1], g_r.at[1], twin)
    for c in range(4):
        at = slice(c * 512, c * 512 + 512)
        own_v[:, at] = dot(g_turn[...], powers[:, at])
    gq_turn[...] = jnp.zeros_like(gq_turn)

    def pick(kind, h, j, high):
        packed = rr[kind, h, j % 2].astype(F32)
        return packed if (j >= 2) == high else swap_halves(packed)

    def out_part(j):
        parts = [jnp.where(lane < 64, 0.0, pick(ATTN, h, j, True)).astype(BF16) for h in range(4)]
        return dot_nt(jnp.concatenate(parts, axis=1), wg[:, 512:1024])

    def grad_part(j):
        parts = [jnp.where(lane < 64, pick(KEY, h, j, False), pick(VALUE, h, j, True)) for h in range(4)]
        parts += [jnp.where(lane < 64, pick(QUERY, h, j, False), 0.0) for h in range(4)]
        return dot_nt(jnp.concatenate([part.astype(BF16) for part in parts], axis=1), wg[...])

    p_copies = []

    def send_part(kind, k, value):
        ps[kind, k] = value.astype(BF16)
        n = kind * 3 + k
        p_copies.append(start_copy(ps.at[kind, k], pr.at[kind, k], p_s.at[n], p_r.at[n], z_peers[k]))

    def weight_part(kind):
        tokens = (cg if kind == ATTN else ng)[...].reshape(512, 1024)
        parts = []
        for h in range(4):
            even, odd = rr[kind, h, 0].astype(F32).T, rr[kind, h, 1].astype(F32).T
            parts.append(jnp.concatenate([even[0:64], odd[0:64], even[64:128], odd[64:128]], axis=1).astype(BF16))
        value = dot(jnp.concatenate(parts, axis=0), tokens).astype(BF16)
        for h in range(4):
            for band in range(8):
                piece = value[h * 64 : h * 64 + 64, band * 128 : band * 128 + 128]
                ws[band % 2, kind, h, band // 2] = piece

    def weight_twin(kinds, n):
        return start_copy(ws.at[1 - core, kinds], wt.at[kinds], t_s.at[n], t_r.at[n], twin)

    d_copies = []

    def weight_send(kinds, n):
        for kind in range(kinds.start, kinds.stop):
            for h in range(4):
                for py in range(4):
                    total = ws[core, kind, h, py].astype(F32) + wt[kind, h, py].astype(F32)
                    wsum[h, py, kind] = total.astype(BF16)
        for d, (px, py, peer) in enumerate(swap):
            d_copies.append(
                start_copy(wsum.at[px, py, kinds], wr.at[here, kinds], d_s.at[n, d], d_r.at[n, d], peer)
            )
        wr[here, kinds] = wsum[x, y, kinds]

    block_finish(ATTN)
    for k, j in ((2, 3), (0, 2), (1, 1)):
        send_part(0, k, out_part(j))
    twin_v.wait()

    @pl.loop(0, 4)
    def _(i):
        block = lax.rem(x + i + 1, 4)
        for py in range(4):
            slot = block * 4 + py
            at = pl.ds(pl.multiple_of(slot * 128, 128), 128)
            part = own_v[:, at] + grecv[1, :, at].astype(F32)
            r[VALUE, slot] = pack(part).astype(BF16).reshape(2, 32, 128)
        block_start(VALUE, i)

    def key_block(at):
        powers[:, at] = (powers[:, at].astype(F32) * dot_nt(g_aug[...], ones_v[at, :])).astype(BF16)
        grad_s = powers[:, at]
        gq_turn[...] += dot_nt(kvt[:, at], grad_s)
        return dot(q_turn[...], grad_s) * LN2

    @pl.loop(0, 4)
    def _(i):
        at = pl.ds(pl.multiple_of(i * 512, 512), 512)
        gsend[0, :, at] = key_block(pl.ds(pl.multiple_of(2048 + i * 512, 512), 512)).astype(BF16)

    start_copy(gsend.at[0], grecv.at[0], g_s.at[0], g_r.at[0], twin)

    @pl.loop(0, 4)
    def _(i):
        block = lax.rem(x + i + 1, 4)
        at = pl.ds(pl.multiple_of(block * 512, 512), 512)
        own = key_block(at)

        @pl.when(i == 0)
        def _():
            pltpu.make_async_remote_copy(
                src_ref=gsend.at[0], dst_ref=grecv.at[0], send_sem=g_s.at[0], recv_sem=g_r.at[0],
                device_id=twin, device_id_type=MESH,
            ).wait()

        upstream = own + grecv[0, :, at].astype(F32)
        for py in range(4):
            raw = tr[block * 4 + py, 0:4].reshape(128, 128).astype(F32)
            raw = jnp.where(lane64 < 64, raw[0:64], swap_halves(raw[64:128]))
            part = pack(upstream[:, py * 128 : py * 128 + 128])
            r[KEY, block * 4 + py] = head_back(raw, part).astype(BF16).reshape(2, 32, 128)
        block_start(KEY, i)

    @pl.loop(0, 4)
    def _(i):
        block = lax.rem(x + i + 1, 4)
        for py in range(4):
            slot = block * 4 + py
            part = pack(gq_turn[:, pl.ds(pl.multiple_of(slot * 128, 128), 128)] * back)
            raw = tr[slot, 4:6].reshape(64, 128).astype(F32)
            r[QUERY, slot] = head_back(raw, part).astype(BF16).reshape(2, 32, 128)
        block_start(QUERY, i)

    block_finish(VALUE)
    weight_part(ATTN)
    weight_part(VALUE)
    first = weight_twin(slice(0, 2), 0)
    block_finish(KEY)
    weight_part(KEY)
    first.wait()
    weight_send(slice(0, 2), 0)
    term = out_part(0)
    block_finish(QUERY)
    for k, j in ((2, 3), (0, 2), (1, 1)):
        send_part(1, k, grad_part(j))
    weight_part(QUERY)
    last = weight_twin(slice(2, 4), 1)
    grad = grad_part(0)
    last.wait()
    weight_send(slice(2, 4), 1)

    for copy in p_copies:
        copy.wait()
    for k in range(3):
        term = term + pr[0, k].astype(F32)
        grad = grad + pr[1, k].astype(F32)
    values = inner_ref[...].astype(F32)
    out_ref[...] = (values + term).astype(BF16).reshape(32, 4, 1024)
    factor = lax.rsqrt(jnp.mean(values * values, axis=-1, keepdims=True) + 1e-06)
    unit = values * factor
    upstream = grad * gain2_ref[...]
    grad = cg[0].astype(F32) + factor * (
        upstream - unit * jnp.mean(upstream * unit, axis=-1, keepdims=True)
    )
    grad_ref[...] = grad.reshape(32, 4, 1024)

    for copy in d_copies:
        copy.wait()
    for kind in range(4):
        total = jnp.zeros((64, 128), F32)
        for n in range(16):
            total = total + wr[n, kind].astype(F32)
        if kind == ATTN:
            do_ref[...] = total
        else:
            dw_ref[(3, 2, 1, 0)[kind]] = total


def store_kernel(a_ref, b_ref, c_ref, d_ref, a_out, b_out, c_out, d_out):
    a_out[...] = a_ref[...]
    b_out[...] = b_ref[...]
    c_out[...] = c_ref[...]
    d_out[...] = d_ref[...]


def per_device(
    fine_input,
    gain_fine,
    fine_qkv,
    fine_out,
    fine_scale,
    merge_weight,
    gain_coarse,
    coarse_qkv,
    coarse_out,
    coarse_scale,
    cotangent,
):
    sel, place, query = fine_tables()
    vmem = pl.BlockSpec(memory_space=pltpu.VMEM)
    hbm = pl.BlockSpec(memory_space=pl.ANY)
    dma = pltpu.SemaphoreType.DMA
    results = pl.pallas_call(
        kernel,
        out_shape=(
            jax.ShapeDtypeStruct((32, 4, 1024), BF16),
            jax.ShapeDtypeStruct((32, 4, 1024), F32),
            jax.ShapeDtypeStruct((3, 64, 128), F32),
            jax.ShapeDtypeStruct((64, 128), F32),
        ),
        in_specs=[hbm] * 4 + [vmem, hbm, hbm, vmem, hbm, vmem] + [hbm] * 3 + [vmem],
        out_specs=(vmem,) * 4,
        scratch_shapes=[
            pltpu.VMEM((4, 128, 512), BF16),
            pltpu.VMEM((KEYS, 128), BF16),
            pltpu.VMEM((8, KEYS), jnp.int32),
            pltpu.VMEM((256, 128), jnp.int32),
            pltpu.VMEM((32, 4, 1024), BF16),
            pltpu.VMEM((3, 64, 1024), BF16),
            pltpu.VMEM((64, 1024), BF16),
            pltpu.VMEM((128, 1024), BF16),
            pltpu.VMEM((4, 128, 1024), BF16),
            pltpu.VMEM((4, 128, 1024), BF16),
            pltpu.VMEM((1024, 1024), BF16),
            pltpu.VMEM((16, 6, 32, 128), BF16),
            pltpu.VMEM((16, 2, 32, 128), BF16),
            pltpu.VMEM((2048, 128), BF16),
            pltpu.VMEM((4096, 128), BF16),
            pltpu.VMEM((4, KEYS, 512), BF16),
            pltpu.VMEM((4, 224, 512), BF16),
            pltpu.VMEM((4, KEYS, 512), BF16),
            pltpu.VMEM((4, KEYS, 512), BF16),
            pltpu.VMEM((4, 128, 512), BF16),
            pltpu.VMEM((4, 128, 512), BF16),
            pltpu.VMEM((256, KEYS), F32),
            pltpu.VMEM((4, 6, 128, 128), BF16),
            pltpu.VMEM((4, 4, 128, 128), BF16),
            pltpu.VMEM((4, 2, 128, 128), BF16),
            pltpu.VMEM((2048, 4096), BF16),
            pltpu.VMEM((4096, 128), BF16),
            pltpu.VMEM((64, 4096), BF16),
            pltpu.VMEM((80, 4096), BF16),
            pltpu.VMEM((2048, 128), BF16),
            pltpu.VMEM((64, 2048), BF16),
            pltpu.VMEM((64, 2048), BF16),
            pltpu.VMEM((64, 2048), F32),
            pltpu.VMEM((64, 2048), F32),
            pltpu.VMEM((8, 2048), F32),
            pltpu.VMEM((64, 2048), F32),
            pltpu.VMEM((4, 16, 2, 32, 128), BF16),
            pltpu.VMEM((4, 4, 2, 128, 128), BF16),
            pltpu.VMEM((2, 64, 2048), BF16),
            pltpu.VMEM((2, 64, 2048), BF16),
            pltpu.VMEM((2, 3, 128, 1024), BF16),
            pltpu.VMEM((2, 3, 128, 1024), BF16),
            pltpu.VMEM((2, 4, 4, 4, 64, 128), BF16),
            pltpu.VMEM((4, 4, 4, 64, 128), BF16),
            pltpu.VMEM((4, 4, 4, 64, 128), BF16),
            pltpu.VMEM((16, 4, 64, 128), BF16),
            dma((8,)), dma((8,)),
            dma((3, 2)), dma((3, 2)), dma((3, 2)), dma((3, 2)), dma((3,)), dma((3,)), dma((2, 3)), dma((2, 3)),
            dma((2, 15)), dma((2, 15)), dma(()), dma(()),
            dma((15,)), dma((15,)), dma((2,)), dma((2,)), dma((4, 16)), dma((4, 16)), dma((6,)), dma((6,)),
            dma((2,)), dma((2,)), dma((2, 15)), dma((2, 15)), dma((10,)),
        ],
        compiler_params=pltpu.CompilerParams(
            collective_id=0, has_side_effects=True, vmem_limit_bytes=60 * 1024 * 1024
        ),
        cost_estimate=pl.CostEstimate(flops=36_000_000_000, bytes_accessed=16_000_000, transcendentals=12_000_000),
        name="step",
    )(
        fine_input.reshape(4, 128, 512),
        jnp.asarray(sel, BF16),
        jnp.asarray(place),
        jnp.asarray(query),
        gain_fine.reshape(1, 512),
        fine_qkv,
        fine_out,
        fine_scale.reshape(1, 8),
        merge_weight,
        gain_coarse.reshape(1, 1024),
        cotangent.reshape(32, 4, 1024),
        coarse_qkv.transpose(0, 2, 1),
        coarse_out,
        coarse_scale.reshape(1, 1),
    )
    output, grad, qkv_grad, out_grad = pl.pallas_call(
        store_kernel,
        out_shape=tuple(jax.ShapeDtypeStruct(v.shape, v.dtype) for v in results),
        in_specs=[vmem] * 4,
        out_specs=(vmem,) * 4,
        compiler_params=pltpu.CompilerParams(vmem_limit_bytes=60 * 1024 * 1024),
        name="store",
    )(*results)
    return (
        output.reshape(4, 8, 4, 1024),
        grad.reshape(4, 8, 4, 1024),
        qkv_grad.transpose(0, 2, 1),
        out_grad,
    )


def solution(mesh):
    return jax.shard_map(
        per_device,
        mesh=mesh,
        in_specs=(
            P(None, "row", "col", None),
            P(),
            P(),
            P(),
            P(),
            P(),
            P(),
            P(None, None, "col"),
            P("col", None),
            P("col"),
            P(None, "row", "col", None),
        ),
        out_specs=(
            P(None, "row", "col", None),
            P(None, "row", "col", None),
            P(None, "row", "col"),
            P("col", "row"),
        ),
        check_vma=False,
    )
```

```python
import jax
import jax.numpy as jnp
import numpy as np
from jax import lax
from jax.experimental import pallas as pl
from jax.experimental.pallas import tpu as pltpu
from jax.sharding import PartitionSpec as P

MESH = pl.DeviceIdType.MESH
F32 = jnp.float32
BF16 = jnp.bfloat16
SEG = ((128, 48), (176, 48), (224, 32), (256, 32), (288, 16), (304, 16), (320, 16), (336, 16))
WAY = ((0, 1), (0, -1), (1, 0), (-1, 0), (1, 1), (1, -1), (-1, 1), (-1, -1))
KEYS = 384
RING = (1, 3, 2)
BLOCK = 512
ATTN, VALUE, KEY, QUERY = range(4)
FAR_FIRST = sorted(range(15), key=lambda d: -((0, 1, 2, 1)[(d + 1) // 4] + (0, 1, 2, 1)[(d + 1) % 4]))
LOG2E = 1.4426950408889634
LN2 = 0.6931471805599453


def dot(a, b):
    return jnp.dot(a, b, preferred_element_type=F32)


def dot_nt(a, b):
    return lax.dot_general(a, b, (((1,), (1,)), ((), ())), preferred_element_type=F32)


def start_copy(source, target, send_sem, recv_sem, device):
    copy = pltpu.make_async_remote_copy(
        src_ref=source, dst_ref=target, send_sem=send_sem, recv_sem=recv_sem, device_id=device, device_id_type=MESH
    )
    copy.start()
    return copy


def swap_peers(x, y, z, core):
    peers = []
    for d in range(1, 16):
        px, py = lax.rem(x + d // 4, 4), lax.rem(y + d % 4, 4)
        peers.append((px, py, (py * 2 + core, px * 4 + z)))
    return peers


def fine_tables():
    sel = np.zeros((KEYS, 128), np.float32)
    place = np.full((8, KEYS), 10000, np.int32)
    query = np.zeros((256, 128), np.int32)
    for p in range(4):
        for u in range(8):
            for w in range(4):
                n = p * 32 + u * 4 + w
                i, j = 2 * u + p // 2, 2 * w + p % 2
                sel[n, i * 8 + j] = 1
                place[0, n], place[1, n] = i, j
                query[n, 0] = query[n + 128, 0] = i
                query[n, 1] = query[n + 128, 1] = j
    for (start, _), (down, right) in zip(SEG, WAY):
        rows = {0: range(16), 1: range(13, 16), -1: range(3)}[down]
        cols = {0: range(8), 1: range(5, 8), -1: range(3)}[right]
        n = start
        for i in rows:
            for j in cols:
                sel[n, i * 8 + j] = 1
                place[0, n], place[1, n] = i - 16 * down, j - 8 * right
                n += 1
    return sel, place, query


def kernel(
    x_hbm, sel_hbm, place_hbm, query_hbm, gain_ref, wqkv_hbm, wout_hbm, scale_ref, wmerge_hbm, gain2_ref,
    cot_hbm, heads_hbm, proj_hbm, scale2_ref,
    out_ref, grad_ref, dw_ref, do_ref,
    x_ref, sel_ref, place_ref, query_ref, cot_ref, heads_ref, proj_ref,
    inner_ref, ng, cg, wg, tr, gr, qg, kv,
    keys_in, send, kn, vv, qn, fr, bias, tk, tq, gs,
    powers, ones_v, kvt, vt, g_aug, g_turn, q_turn, gq_turn, outs_turn, inv, own_v,
    r, rr, gsend, grecv, ps, pr, ws, wt, wsum, wr,
    send_sem, recv_sem, w_s, w_r, f_s, f_r, c_s, c_r, n_s, n_r, a_s, a_r, k_s, k_r,
    x_s, x_r, g_s, g_r, b_s, b_r, p_s, p_r, t_s, t_r, d_s, d_r, l_s,
):
    row, col = lax.axis_index("row"), lax.axis_index("col")
    y, core, x, z = lax.div(row, 2), lax.rem(row, 2), lax.div(col, 4), lax.rem(col, 4)
    barrier = pltpu.get_barrier_semaphore()
    peers = [(lax.rem(row + a + 8, 8), lax.rem(col + b + 16, 16)) for a, b in WAY]
    z_peers = [(row, x * 4 + lax.rem(z + off, 4)) for off in RING]
    x_peers = [(row, lax.rem(x + off, 4) * 4 + z) for off in RING]
    twin = (y * 2 + 1 - core, col)
    swap = swap_peers(x, y, z, core)
    for peer in peers + z_peers + x_peers + [twin] + [p for _, _, p in swap]:
        pl.semaphore_signal(barrier, inc=1, device_id=peer, device_id_type=MESH)

    wqkv_ref = powers.at[0:512, 1024:2560]
    wout_ref = powers.at[512:1024, 1024:1536]
    wmerge_ref = powers.at[:, 0:1024]
    pairs = (
        (x_hbm, x_ref), (sel_hbm, sel_ref), (heads_hbm, heads_ref), (proj_hbm, proj_ref), (cot_hbm, cot_ref),
        (place_hbm, place_ref), (query_hbm, query_ref), (wqkv_hbm, wqkv_ref), (wout_hbm, wout_ref),
        (wmerge_hbm, wmerge_ref),
    )
    loads = [pltpu.make_async_copy(pair[0], pair[1], l_s.at[n]) for n, pair in enumerate(pairs)]
    for load in loads:
        load.start()
    back = scale2_ref[...] * (1.0 / 64)
    head_of = lax.shift_right_logical(lax.broadcasted_iota(jnp.int32, (1, 512), 1), 6)
    fine_scale = jnp.zeros((1, 512), F32)
    for h in range(8):
        fine_scale = jnp.where(head_of == h, scale_ref[0:1, h : h + 1] * (1.0 / 64), fine_scale)

    loads[0].wait()
    loads[1].wait()

    @pl.loop(0, 4)
    def _(img):
        packed = dot(sel_ref[...], x_ref[img]).astype(BF16)
        keys_in[img, 0:128, :] = packed[0:128]
        send[img] = packed[128:352]
        keys_in[img, 352:384, :] = packed[352:384]

    pl.semaphore_wait(barrier, 30)
    copies = []
    for k, ((start, size), peer) in enumerate(zip(SEG, peers)):
        copy = pltpu.make_async_remote_copy(
            src_ref=send.at[:, start - 128 : start - 128 + size, :],
            dst_ref=keys_in.at[:, start : start + size, :],
            send_sem=send_sem.at[k],
            recv_sem=recv_sem.at[k],
            device_id=peer,
            device_id_type=MESH,
        )
        copy.start()
        copies.append(copy)

    for load in loads[2:7]:
        load.wait()
    own_kv = pl.ds(pl.multiple_of(x * 128, 128), 128)
    own_qo = pl.ds(pl.multiple_of(512 + x * 128, 128), 128)
    wg[:, own_kv] = jnp.concatenate([heads_ref[1], heads_ref[2]], axis=0).astype(F32).T.astype(BF16)
    wg[:, own_qo] = jnp.concatenate([heads_ref[0], proj_ref[...]], axis=0).astype(F32).T.astype(BF16)
    cg[0] = cot_ref[...].reshape(128, 1024)

    seen = (
        (jnp.abs(place_ref[0:1, :] - query_ref[:, 0:1]) <= 3)
        & (jnp.abs(place_ref[1:2, :] - query_ref[:, 1:2]) <= 3)
    )
    gi = place_ref[0:1, :] + row * 16
    gj = place_ref[1:2, :] + col * 8
    inside = (gi >= 0) & (gi < 128) & (gj >= 0) & (gj < 128)
    bias[...] = jnp.where(seen & inside, 0.0, -1e30).astype(F32)

    lane = lax.broadcasted_iota(jnp.int32, (128, 128), 1)
    sub = lax.broadcasted_iota(jnp.int32, (128, 128), 0)
    same = jnp.where((lane < 64) == (sub < 64), 1.0 / 64, 0.0).astype(BF16)

    def token_norm(tokens):
        xf = tokens.astype(F32)
        factor = lax.rsqrt(jnp.mean(xf * xf, axis=-1, keepdims=True) + 1e-06)
        return (xf * factor * gain_ref[...]).astype(BF16)

    def head_norm(values):
        vf = values.astype(BF16).astype(F32)
        sq = (vf * vf).astype(BF16)
        parts = [dot(sq[:, k * 128 : k * 128 + 128], same) for k in range(4)]
        return vf * lax.rsqrt(jnp.concatenate(parts, axis=1) + 1e-06)

    loads[7].wait()

    @pl.loop(0, 4)
    def _(img):
        nx = token_norm(keys_in[img, 0:128, :])
        qn[img] = (head_norm(dot(nx, wqkv_ref[:, 0:512])) * fine_scale).astype(BF16)
        kn[img, 0:128, :] = head_norm(dot(nx, wqkv_ref[:, 512:1024])).astype(BF16)
        vv[img, 0:128, :] = dot(nx, wqkv_ref[:, 1024:1536]).astype(BF16)

    for copy in copies:
        copy.wait()
    half = pl.ds(pl.multiple_of(core * 512, 512), 512)

    def head_copies(block, rows, sems, peer, target):
        copies = []
        for n in range(2):
            piece = wg.at[rows, pl.ds(pl.multiple_of(n * 512 + block * 128, 128), 128)]
            copies.append(start_copy(piece, piece, sems[0].at[target, n], sems[1].at[target, n], peer))
        return copies

    w_copies = [head_copies(x, half, (w_s, w_r), x_peers[k], k) for k in range(3)]

    ones = jnp.ones((KEYS, 128), BF16)
    loads[8].wait()
    loads[9].wait()

    def tokens_out(img):
        nx = token_norm(keys_in[img, 128:384, :])
        kn[img, 128:384, :] = head_norm(dot(nx, wqkv_ref[:, 512:1024])).astype(BF16)
        vv[img, 128:384, :] = dot(nx, wqkv_ref[:, 1024:1536]).astype(BF16)
        mixed = []
        for pair in range(4):
            at = slice(pair * 128, pair * 128 + 128)
            q = qn[img, :, at]
            zero = jnp.zeros_like(q)
            both = jnp.concatenate([jnp.where(lane < 64, q, zero), jnp.where(lane < 64, zero, q)], axis=0)
            powered = jnp.exp(dot_nt(both, kn[img, :, at]) + bias[...]).astype(BF16)
            sums = dot(powered, jnp.concatenate([vv[img, :, at], ones], axis=1))
            ratio = sums[:, 0:128] / sums[:, 128:256]
            mixed.append(jnp.where(lane < 64, ratio[0:128], ratio[128:256]).astype(BF16))
        mix = jnp.concatenate(mixed, axis=1)
        fr[img] = (keys_in[img, 0:128, :].astype(F32) + dot(mix, wout_ref[...])).astype(BF16)

    n_copies = []
    for part in range(2):
        pl.loop(part * 2, part * 2 + 2)(tokens_out)
        rows = slice(part * 64, part * 64 + 64)
        merged = jnp.zeros((64, 1024), F32)
        for p in range(4):
            group = jnp.concatenate([fr[part * 2 + n, p * 32 : p * 32 + 32, :] for n in range(2)], axis=0)
            merged = merged + dot(group, wmerge_ref[p * 512 : p * 512 + 512, :])
        inner = merged.astype(BF16)
        inner_ref[rows, :] = inner
        xf = inner.astype(F32)
        factor = lax.rsqrt(jnp.mean(xf * xf, axis=-1, keepdims=True) + 1e-06)
        ng[0, rows, :] = (xf * factor * gain2_ref[...]).astype(BF16)
        n_copies.append([
            start_copy(ng.at[0, rows, :], ng.at[1 + k, rows, :], n_s.at[part, k], n_r.at[part, k], z_peers[k])
            for k in range(3)
        ])
    c_copies = [start_copy(cg.at[0], cg.at[1 + k], c_s.at[k], c_r.at[k], z_peers[k]) for k in range(3)]
    f_copies = []
    for k, off in enumerate(RING):
        for copy in w_copies[k]:
            copy.wait()
        f_copies += head_copies(lax.rem(x - off + 4, 4), half, (f_s, f_r), twin, k)
    for copy in f_copies:
        copy.wait()

    mine = pl.ds(pl.multiple_of(y * 32, 32), 32)
    here = x * 4 + y
    a_copies = []

    def project(j):
        value = dot(ng[j], wg[...]).astype(BF16)
        for h in range(4):
            tk[h, j] = value[:, h * 128 : h * 128 + 128]
            tq[h, j] = value[:, 512 + h * 128 : 640 + h * 128]

    def spread(source, target, pieces, sems):
        copies = [None] * 15
        for d in FAR_FIRST:
            px, py, peer = swap[d]
            rows = pl.ds(pl.multiple_of(py * 32, 32), 32)
            copies[d] = start_copy(
                source.at[px, pieces, rows, :], target.at[here, pieces], sems[0].at[d], sems[1].at[d], peer
            )
        target[here, pieces] = source[x, pieces, mine, :]
        return copies

    def swap_halves(values):
        return pltpu.roll(values, 64, 1)

    project(0)
    a_copies.append(spread(tk, tr, slice(0, 1), (a_s.at[0], a_r.at[0])))
    for part in range(2):
        n_copies[part][0].wait()
        n_copies[part][1].wait()
    project(1)
    project(2)
    a_copies.append(spread(tk, tr, slice(1, 3), (a_s.at[1], a_r.at[1])))
    for part in range(2):
        n_copies[part][2].wait()
    project(3)
    for h in range(4):
        for n in range(2):
            high = swap_halves(tq[h, n + 2].astype(F32))
            tk[h, 4 + n] = jnp.where(lane < 64, tq[h, n].astype(F32), high).astype(BF16)
    a_copies.append(spread(tk, tr, slice(3, 6), (a_s.at[2], a_r.at[2])))
    low = jnp.where(sub < 64, 1.0 / 64, 0.0).astype(BF16)
    lane64 = lane[0:64]
    for d in range(16):
        if d > 0:
            for copies in a_copies:
                copies[d - 1].wait()
        dx, dy = d // 4, d % 4
        slot = lax.rem(x - dx + 4, 4) * 4 + lax.rem(y - dy + 4, 4)
        at = pl.ds(pl.multiple_of(slot * 128, 128), 128)
        k_f = tr[slot, 0:4].reshape(128, 128).astype(F32)
        k_n = k_f * lax.rsqrt(dot((k_f * k_f).astype(BF16), low) + 1e-06)
        kv[at, :] = jnp.where(lane < 64, k_n, k_f).astype(BF16)
        q_f = tr[slot, 4:6].reshape(64, 128).astype(F32)
        q_n = q_f * lax.rsqrt(dot((q_f * q_f).astype(BF16), same) + 1e-06) * (back * LOG2E)
        q_n = jnp.concatenate([q_n, swap_halves(q_n)], axis=0)
        qg[at, :] = jnp.where(lane < 64, q_n, 0.0).astype(BF16)
    k_copy = start_copy(kv.at[0:2048, :], kv.at[2048:4096, :], k_s, k_r, twin)

    for copy in c_copies:
        copy.wait()
    for n in range(2):
        first = dot(cg[n], wg[:, 512:1024])
        second = dot(cg[n + 2], wg[:, 512:1024])
        for h in range(4):
            at = slice(h * 128, h * 128 + 128)
            gs[h, n] = jnp.where(lane < 64, swap_halves(first[:, at]), second[:, at]).astype(BF16)
    grad_copies = spread(gs, gr, slice(0, 2), (x_s, x_r))

    def key_side(c):
        at = slice(c * 512, c * 512 + 512)
        tile = kv[at, :]
        ones_v[at, :] = jnp.where(lax.broadcasted_iota(jnp.int32, (512, 128), 1) < 64, jnp.ones_like(tile), tile)
        turned = tile.astype(F32).T.astype(BF16)
        kvt[:, at] = turned[0:64]
        vt[0:64, at] = turned[64:128]

    vt[64:80, :] = jnp.ones((16, 4096), BF16)
    for c in range(4):
        key_side(c)
    k_copy.wait()
    for c in range(4, 8):
        key_side(c)

    def head_back(values, upstream):
        factor = lax.rsqrt(dot((values * values).astype(BF16), same) + 1e-06)
        unit = values * factor
        return factor * (upstream - unit * dot((upstream * unit).astype(BF16), same))

    def pack(turned):
        return jnp.concatenate([turned[:, 0:64], turned[:, 64:128]], axis=0).T

    def block_copy(kind, i, dy):
        px, py = lax.rem(x + i + 1, 4), lax.rem(y + dy, 4)
        n = lax.rem(i + 1, 4) * 4 + dy
        return pltpu.make_async_remote_copy(
            src_ref=r.at[kind, px * 4 + py], dst_ref=rr.at[kind, x, :, mine, :],
            send_sem=b_s.at[kind, n], recv_sem=b_r.at[kind, n],
            device_id=(py * 2 + core, px * 4 + z), device_id_type=MESH,
        )

    def block_start(kind, i):
        for dy in range(1, 4):
            block_copy(kind, i, dy).start()

        @pl.when(i < 3)
        def _():
            block_copy(kind, i, 0).start()

    def block_finish(kind):
        rr[kind, x, :, mine, :] = r[kind, here]
        for i in range(4):
            for dy in range(4):
                if i < 3 or dy > 0:
                    block_copy(kind, i, dy).wait()

    @pl.loop(0, 4)
    def _(i):
        block = lax.rem(x + i + 1, 4)
        rows = pl.ds(pl.multiple_of(block * BLOCK, BLOCK), BLOCK)
        q = qg[rows, :]
        for c in range(8):
            at = slice(c * 512, c * 512 + 512)
            powers[rows, at] = jnp.exp2(dot_nt(q, kv[at, :])).astype(BF16)
        total = dot_nt(vt[...], powers[rows, :])
        inverse = 1.0 / total[64:65]
        outputs = total[0:64] * inverse
        inv[0:1, rows] = inverse
        outs_turn[:, rows] = outputs
        q_turn[:, rows] = q.astype(F32).T[0:64].astype(BF16)
        for py in range(4):
            r[ATTN, block * 4 + py] = pack(outputs[:, py * 128 : py * 128 + 128]).astype(BF16).reshape(2, 32, 128)
        block_start(ATTN, i)

    for copy in grad_copies:
        copy.wait()
    sub64 = lax.broadcasted_iota(jnp.int32, (64, BLOCK), 0)

    @pl.loop(0, 4)
    def _(b):
        rows = pl.ds(pl.multiple_of(b * BLOCK, BLOCK), BLOCK)
        parts = []
        for n in range(4):
            turned = gr[b * 4 + n].reshape(64, 128).astype(F32).T
            parts += [turned[0:64], turned[64:128]]
        g = jnp.concatenate(parts, axis=1)
        inverse = inv[0:1, rows]
        delta = jnp.sum(g * outs_turn[:, rows], axis=0, keepdims=True) * inverse
        high = delta.astype(BF16).astype(F32)
        rest = jnp.where(sub64 == 0, -high, jnp.where(sub64 == 1, high - delta, 0.0))
        scaled = g * inverse
        g_turn[:, rows] = scaled.astype(BF16)
        g_aug[rows, :] = jnp.concatenate([rest, scaled], axis=0).T.astype(BF16)

    for c in range(4):
        at = slice(c * 512, c * 512 + 512)
        gsend[1, :, at] = dot(g_turn[...], powers[:, 2048 + c * 512 : 2560 + c * 512]).astype(BF16)
    twin_v = start_copy(gsend.at[1], grecv.at[1], g_s.at[1], g_r.at[1], twin)
    for c in range(4):
        at = slice(c * 512, c * 512 + 512)
        own_v[:, at] = dot(g_turn[...], powers[:, at])
    gq_turn[...] = jnp.zeros_like(gq_turn)

    def pick(kind, h, j, high):
        packed = rr[kind, h, j % 2].astype(F32)
        return packed if (j >= 2) == high else swap_halves(packed)

    def out_part(j):
        parts = [jnp.where(lane < 64, 0.0, pick(ATTN, h, j, True)).astype(BF16) for h in range(4)]
        return dot_nt(jnp.concatenate(parts, axis=1), wg[:, 512:1024])

    def grad_part(j):
        parts = [jnp.where(lane < 64, pick(KEY, h, j, False), pick(VALUE, h, j, True)) for h in range(4)]
        parts += [jnp.where(lane < 64, pick(QUERY, h, j, False), 0.0) for h in range(4)]
        return dot_nt(jnp.concatenate([part.astype(BF16) for part in parts], axis=1), wg[...])

    p_copies = []

    def send_part(kind, k, value):
        ps[kind, k] = value.astype(BF16)
        n = kind * 3 + k
        p_copies.append(start_copy(ps.at[kind, k], pr.at[kind, k], p_s.at[n], p_r.at[n], z_peers[k]))

    def weight_part(kind):
        tokens = (cg if kind == ATTN else ng)[...].reshape(512, 1024)
        parts = []
        for h in range(4):
            even, odd = rr[kind, h, 0].astype(F32).T, rr[kind, h, 1].astype(F32).T
            parts.append(jnp.concatenate([even[0:64], odd[0:64], even[64:128], odd[64:128]], axis=1).astype(BF16))
        value = dot(jnp.concatenate(parts, axis=0), tokens).astype(BF16)
        for h in range(4):
            for band in range(8):
                piece = value[h * 64 : h * 64 + 64, band * 128 : band * 128 + 128]
                ws[band % 2, kind, h, band // 2] = piece

    def weight_twin(kinds, n):
        return start_copy(ws.at[1 - core, kinds], wt.at[kinds], t_s.at[n], t_r.at[n], twin)

    d_copies = []

    def weight_send(kinds, n):
        for kind in range(kinds.start, kinds.stop):
            for h in range(4):
                for py in range(4):
                    total = ws[core, kind, h, py].astype(F32) + wt[kind, h, py].astype(F32)
                    wsum[h, py, kind] = total.astype(BF16)
        for d in FAR_FIRST:
            px, py, peer = swap[d]
            d_copies.append(
                start_copy(wsum.at[px, py, kinds], wr.at[here, kinds], d_s.at[n, d], d_r.at[n, d], peer)
            )
        wr[here, kinds] = wsum[x, y, kinds]

    block_finish(ATTN)
    for k, j in ((2, 3), (0, 2), (1, 1)):
        send_part(0, k, out_part(j))
    twin_v.wait()

    @pl.loop(0, 4)
    def _(i):
        block = lax.rem(x + i + 1, 4)
        for py in range(4):
            slot = block * 4 + py
            at = pl.ds(pl.multiple_of(slot * 128, 128), 128)
            part = own_v[:, at] + grecv[1, :, at].astype(F32)
            r[VALUE, slot] = pack(part).astype(BF16).reshape(2, 32, 128)
        block_start(VALUE, i)

    def key_block(at):
        powers[:, at] = (powers[:, at].astype(F32) * dot_nt(g_aug[...], ones_v[at, :])).astype(BF16)
        grad_s = powers[:, at]
        gq_turn[...] += dot_nt(kvt[:, at], grad_s)
        return dot(q_turn[...], grad_s) * LN2

    @pl.loop(0, 4)
    def _(i):
        at = pl.ds(pl.multiple_of(i * 512, 512), 512)
        gsend[0, :, at] = key_block(pl.ds(pl.multiple_of(2048 + i * 512, 512), 512)).astype(BF16)

    start_copy(gsend.at[0], grecv.at[0], g_s.at[0], g_r.at[0], twin)

    @pl.loop(0, 4)
    def _(i):
        block = lax.rem(x + i + 1, 4)
        at = pl.ds(pl.multiple_of(block * 512, 512), 512)
        own = key_block(at)

        @pl.when(i == 0)
        def _():
            pltpu.make_async_remote_copy(
                src_ref=gsend.at[0], dst_ref=grecv.at[0], send_sem=g_s.at[0], recv_sem=g_r.at[0],
                device_id=twin, device_id_type=MESH,
            ).wait()

        upstream = own + grecv[0, :, at].astype(F32)
        for py in range(4):
            raw = tr[block * 4 + py, 0:4].reshape(128, 128).astype(F32)
            raw = jnp.where(lane64 < 64, raw[0:64], swap_halves(raw[64:128]))
            part = pack(upstream[:, py * 128 : py * 128 + 128])
            r[KEY, block * 4 + py] = head_back(raw, part).astype(BF16).reshape(2, 32, 128)
        block_start(KEY, i)

    @pl.loop(0, 4)
    def _(i):
        block = lax.rem(x + i + 1, 4)
        for py in range(4):
            slot = block * 4 + py
            part = pack(gq_turn[:, pl.ds(pl.multiple_of(slot * 128, 128), 128)] * back)
            raw = tr[slot, 4:6].reshape(64, 128).astype(F32)
            r[QUERY, slot] = head_back(raw, part).astype(BF16).reshape(2, 32, 128)
        block_start(QUERY, i)

    block_finish(VALUE)
    weight_part(ATTN)
    weight_part(VALUE)
    first = weight_twin(slice(0, 2), 0)
    block_finish(KEY)
    weight_part(KEY)
    first.wait()
    weight_send(slice(0, 2), 0)
    term = out_part(0)
    block_finish(QUERY)
    for k, j in ((2, 3), (0, 2), (1, 1)):
        send_part(1, k, grad_part(j))
    weight_part(QUERY)
    last = weight_twin(slice(2, 4), 1)
    grad = grad_part(0)
    last.wait()
    weight_send(slice(2, 4), 1)

    for copy in p_copies:
        copy.wait()
    for k in range(3):
        term = term + pr[0, k].astype(F32)
        grad = grad + pr[1, k].astype(F32)
    values = inner_ref[...].astype(F32)
    out_ref[...] = (values + term).astype(BF16).reshape(32, 4, 1024)
    factor = lax.rsqrt(jnp.mean(values * values, axis=-1, keepdims=True) + 1e-06)
    unit = values * factor
    upstream = grad * gain2_ref[...]
    grad = cg[0].astype(F32) + factor * (
        upstream - unit * jnp.mean(upstream * unit, axis=-1, keepdims=True)
    )
    grad_ref[...] = grad.reshape(32, 4, 1024)

    for copy in d_copies:
        copy.wait()
    for kind in range(4):
        total = jnp.zeros((64, 128), F32)
        for n in range(16):
            total = total + wr[n, kind].astype(F32)
        if kind == ATTN:
            do_ref[...] = total
        else:
            dw_ref[(3, 2, 1, 0)[kind]] = total


def store_kernel(a_ref, b_ref, c_ref, d_ref, a_out, b_out, c_out, d_out):
    a_out[...] = a_ref[...]
    b_out[...] = b_ref[...]
    c_out[...] = c_ref[...]
    d_out[...] = d_ref[...]


def per_device(
    fine_input,
    gain_fine,
    fine_qkv,
    fine_out,
    fine_scale,
    merge_weight,
    gain_coarse,
    coarse_qkv,
    coarse_out,
    coarse_scale,
    cotangent,
):
    sel, place, query = fine_tables()
    vmem = pl.BlockSpec(memory_space=pltpu.VMEM)
    hbm = pl.BlockSpec(memory_space=pl.ANY)
    dma = pltpu.SemaphoreType.DMA
    results = pl.pallas_call(
        kernel,
        out_shape=(
            jax.ShapeDtypeStruct((32, 4, 1024), BF16),
            jax.ShapeDtypeStruct((32, 4, 1024), F32),
            jax.ShapeDtypeStruct((3, 64, 128), F32),
            jax.ShapeDtypeStruct((64, 128), F32),
        ),
        in_specs=[hbm] * 4 + [vmem, hbm, hbm, vmem, hbm, vmem] + [hbm] * 3 + [vmem],
        out_specs=(vmem,) * 4,
        scratch_shapes=[
            pltpu.VMEM((4, 128, 512), BF16),
            pltpu.VMEM((KEYS, 128), BF16),
            pltpu.VMEM((8, KEYS), jnp.int32),
            pltpu.VMEM((256, 128), jnp.int32),
            pltpu.VMEM((32, 4, 1024), BF16),
            pltpu.VMEM((3, 64, 1024), BF16),
            pltpu.VMEM((64, 1024), BF16),
            pltpu.VMEM((128, 1024), BF16),
            pltpu.VMEM((4, 128, 1024), BF16),
            pltpu.VMEM((4, 128, 1024), BF16),
            pltpu.VMEM((1024, 1024), BF16),
            pltpu.VMEM((16, 6, 32, 128), BF16),
            pltpu.VMEM((16, 2, 32, 128), BF16),
            pltpu.VMEM((2048, 128), BF16),
            pltpu.VMEM((4096, 128), BF16),
            pltpu.VMEM((4, KEYS, 512), BF16),
            pltpu.VMEM((4, 224, 512), BF16),
            pltpu.VMEM((4, KEYS, 512), BF16),
            pltpu.VMEM((4, KEYS, 512), BF16),
            pltpu.VMEM((4, 128, 512), BF16),
            pltpu.VMEM((4, 128, 512), BF16),
            pltpu.VMEM((256, KEYS), F32),
            pltpu.VMEM((4, 6, 128, 128), BF16),
            pltpu.VMEM((4, 4, 128, 128), BF16),
            pltpu.VMEM((4, 2, 128, 128), BF16),
            pltpu.VMEM((2048, 4096), BF16),
            pltpu.VMEM((4096, 128), BF16),
            pltpu.VMEM((64, 4096), BF16),
            pltpu.VMEM((80, 4096), BF16),
            pltpu.VMEM((2048, 128), BF16),
            pltpu.VMEM((64, 2048), BF16),
            pltpu.VMEM((64, 2048), BF16),
            pltpu.VMEM((64, 2048), F32),
            pltpu.VMEM((64, 2048), F32),
            pltpu.VMEM((8, 2048), F32),
            pltpu.VMEM((64, 2048), F32),
            pltpu.VMEM((4, 16, 2, 32, 128), BF16),
            pltpu.VMEM((4, 4, 2, 128, 128), BF16),
            pltpu.VMEM((2, 64, 2048), BF16),
            pltpu.VMEM((2, 64, 2048), BF16),
            pltpu.VMEM((2, 3, 128, 1024), BF16),
            pltpu.VMEM((2, 3, 128, 1024), BF16),
            pltpu.VMEM((2, 4, 4, 4, 64, 128), BF16),
            pltpu.VMEM((4, 4, 4, 64, 128), BF16),
            pltpu.VMEM((4, 4, 4, 64, 128), BF16),
            pltpu.VMEM((16, 4, 64, 128), BF16),
            dma((8,)), dma((8,)),
            dma((3, 2)), dma((3, 2)), dma((3, 2)), dma((3, 2)), dma((3,)), dma((3,)), dma((2, 3)), dma((2, 3)),
            dma((3, 15)), dma((3, 15)), dma(()), dma(()),
            dma((15,)), dma((15,)), dma((2,)), dma((2,)), dma((4, 16)), dma((4, 16)), dma((6,)), dma((6,)),
            dma((2,)), dma((2,)), dma((2, 15)), dma((2, 15)), dma((10,)),
        ],
        compiler_params=pltpu.CompilerParams(
            collective_id=0, has_side_effects=True, vmem_limit_bytes=60 * 1024 * 1024
        ),
        cost_estimate=pl.CostEstimate(flops=36_000_000_000, bytes_accessed=16_000_000, transcendentals=12_000_000),
        name="step",
    )(
        fine_input.reshape(4, 128, 512),
        jnp.asarray(sel, BF16),
        jnp.asarray(place),
        jnp.asarray(query),
        gain_fine.reshape(1, 512),
        fine_qkv,
        fine_out,
        fine_scale.reshape(1, 8),
        merge_weight,
        gain_coarse.reshape(1, 1024),
        cotangent.reshape(32, 4, 1024),
        coarse_qkv.transpose(0, 2, 1),
        coarse_out,
        coarse_scale.reshape(1, 1),
    )
    output, grad, qkv_grad, out_grad = pl.pallas_call(
        store_kernel,
        out_shape=tuple(jax.ShapeDtypeStruct(v.shape, v.dtype) for v in results),
        in_specs=[vmem] * 4,
        out_specs=(vmem,) * 4,
        compiler_params=pltpu.CompilerParams(vmem_limit_bytes=60 * 1024 * 1024),
        name="store",
    )(*results)
    return (
        output.reshape(4, 8, 4, 1024),
        grad.reshape(4, 8, 4, 1024),
        qkv_grad.transpose(0, 2, 1),
        out_grad,
    )


def solution(mesh):
    return jax.shard_map(
        per_device,
        mesh=mesh,
        in_specs=(
            P(None, "row", "col", None),
            P(),
            P(),
            P(),
            P(),
            P(),
            P(),
            P(None, None, "col"),
            P("col", None),
            P("col"),
            P(None, "row", "col", None),
        ),
        out_specs=(
            P(None, "row", "col", None),
            P(None, "row", "col", None),
            P(None, "row", "col"),
            P("col", "row"),
        ),
        check_vma=False,
    )
```
